32 devices in a mesh: dp: 16 (over z, y, core), seq: 2 (over x).
Axes of the slice: x: 2, y: 2, z: 4, core: 2. Of those that a mesh axis runs over, the one named last changes fastest.
Arguments:
- tokens_short: bfloat16 [16, 128, 768], P('dp', 'seq'), may hold values from -6 to 6
- tokens_middle: bfloat16 [16, 256, 768], P('dp', 'seq'), may hold values from -6 to 6
- tokens_long: bfloat16 [64, 512, 768], P('dp', 'seq'), may hold values from -6 to 6
- length_short: int32 [16], P('dp'), may hold values from 16 to 128, as said below
- length_middle: int32 [16], P('dp'), may hold values from 32 to 256, as said below
- length_long: int32 [64], P('dp'), may hold values from 64 to 512, as said below
- query_weight: bfloat16 [768, 768], replicated, may hold values from -0.21875 to 0.21875
- query_bias: float32 [768], replicated, may hold values from -3 to 3
- key_weight: bfloat16 [768, 768], replicated, may hold values from -0.21875 to 0.21875
- value_weight: bfloat16 [768, 768], replicated, may hold values from -0.21875 to 0.21875
- value_bias: float32 [768], replicated, may hold values from -3 to 3
- output_weight: bfloat16 [768, 768], replicated, may hold values from -0.875 to 0.875
- output_bias: float32 [768], replicated, may hold values from -3 to 3
- attention_gain: float32 [768], replicated, may hold values from 0.1 to 1.9
- attention_shift: float32 [768], replicated, may hold values from -3 to 3
- up_weight: bfloat16 [768, 3072], replicated, may hold values from -0.21875 to 0.21875
- up_bias: float32 [3072], replicated, may hold values from -3 to 3
- down_weight: bfloat16 [3072, 768], replicated, may hold values from -0.109375 to 0.109375
- down_bias: float32 [768], replicated, may hold values from -3 to 3
- output_gain: float32 [768], replicated, may hold values from 0.1 to 1.9
- output_shift: float32 [768], replicated, may hold values from -3 to 3
- upstream_short: bfloat16 [16, 128, 768], P('dp', 'seq'), may hold values from -6 to 6
- upstream_middle: bfloat16 [16, 256, 768], P('dp', 'seq'), may hold values from -6 to 6
- upstream_long: bfloat16 [64, 512, 768], P('dp', 'seq'), may hold values from -6 to 6
Outputs:
- result_short: bfloat16 [16, 128, 768], P('dp', 'seq')
- result_middle: bfloat16 [16, 256, 768], P('dp', 'seq')
- result_long: bfloat16 [64, 512, 768], P('dp', 'seq')
- input_grad_short: bfloat16 [16, 128, 768], P('dp', 'seq')
- input_grad_middle: bfloat16 [16, 256, 768], P('dp', 'seq')
- input_grad_long: bfloat16 [64, 512, 768], P('dp', 'seq')
- query_weight_grad: float32 [768, 768], P(('dp', 'seq'))
- query_bias_grad: float32 [768], P(('dp', 'seq'))
- key_weight_grad: float32 [768, 768], P(('dp', 'seq'))
- value_weight_grad: float32 [768, 768], P(('dp', 'seq'))
- value_bias_grad: float32 [768], P(('dp', 'seq'))
- output_weight_grad: float32 [768, 768], P(('dp', 'seq'))
- output_bias_grad: float32 [768], P(('dp', 'seq'))
- attention_gain_grad: float32 [768], P(('dp', 'seq'))
- attention_shift_grad: float32 [768], P(('dp', 'seq'))
- up_weight_grad: float32 [768, 3072], P(('dp', 'seq'))
- up_bias_grad: float32 [3072], P(('dp', 'seq'))
- down_weight_grad: float32 [3072, 768], P(('dp', 'seq'))
- down_bias_grad: float32 [768], P(('dp', 'seq'))
- output_gain_grad: float32 [768], P(('dp', 'seq'))
- output_shift_grad: float32 [768], P(('dp', 'seq'))
The draws below stay inside these ranges and needn't reach their ends.
Inputs may be any that keep to these rules, and one draw needn't show every extreme that they name: `length_short`: in each aligned block of 8 rows, one row drawn from the seed has length 128; the others are at least one eighth of it. `length_middle`: in each aligned block of 8 rows, one row drawn from the seed has length 256; the others are at least one eighth of it. `length_long`: in each aligned block of 32 rows, one row drawn from the seed has length 512; the others are at least one eighth of it.
All inputs are finite; a program needn't handle non-finite values.
Results may differ from the reference program's by a relative error of at most 0.014.
Values may be sent and summed in bfloat16 or wider, within the bound.
No kernel may reach another device: no remote copies, remote signals or barrier semaphores. Data moves between devices by JAX's collectives and lax.ppermute only.
A program may use at most 256 MiB of HBM per device.

```python
import jax
import jax.numpy as jnp
from jax import lax

D = 768
HEADS = 12
HEAD_DIM = 64
FF = 3072
LEN_SHORT = 128
LEN_MIDDLE = 256
LEN_LONG = 512
ROWS_SHORT = 1
ROWS_MIDDLE = 1
ROWS_LONG = 4
BATCH_SHORT = 16
BATCH_MIDDLE = 16
BATCH_LONG = 64


def bucket_lengths(key, total_rows, rows_device, length):
    per_group = 8 * rows_device
    groups = total_rows // per_group
    key_len, key_pick = jax.random.split(key)
    drawn = jax.random.randint(key_len, (groups, per_group), length // 8, length + 1, dtype=jnp.int32)
    pick = jax.random.randint(key_pick, (groups, 1), 0, per_group, dtype=jnp.int32)
    column = jnp.arange(per_group, dtype=jnp.int32)[None, :]
    filled = jnp.where(column == pick, jnp.int32(length), drawn)
    return filled.reshape(groups * per_group).astype(jnp.int32)


def draw_length_short(key, part):
    key = jax.random.fold_in(key, 11)
    return bucket_lengths(key, BATCH_SHORT, ROWS_SHORT, LEN_SHORT)


def draw_length_middle(key, part):
    key = jax.random.fold_in(key, 12)
    return bucket_lengths(key, BATCH_MIDDLE, ROWS_MIDDLE, LEN_MIDDLE)


def draw_length_long(key, part):
    key = jax.random.fold_in(key, 13)
    return bucket_lengths(key, BATCH_LONG, ROWS_LONG, LEN_LONG)


def level_of(own_key, shape, cuts, least, largest):
    level, own = 1.0, jax.random.fold_in(own_key, 6)
    for dim, parts in cuts:
        steps = jnp.exp(jax.random.uniform(jax.random.fold_in(own, dim), (parts,), jnp.float32, least / len(cuts), largest / len(cuts)))
        level = level * jnp.repeat(steps, shape[dim] // parts).reshape([-1 if axis == dim else 1 for axis in range(len(shape))])
    return level


def scatter_about(key, dims, width, bound, cuts=(), held_as=jnp.bfloat16):
    level = level_of(key, dims, cuts, -0.22, 0.18) if cuts else 1.0
    array = jax.random.normal(key, dims, jnp.float32) * width * level
    return jnp.minimum(jnp.maximum(array, -bound), bound).astype(held_as)


def setup_inputs(seed: int = 0) -> dict:
    key_of = jax.random.split(jax.random.key(seed), 25)
    tokens_short = scatter_about(key_of[0], (BATCH_SHORT, LEN_SHORT, D), 1.0, 6.0, ((0, 16), (1, 2)))
    tokens_middle = scatter_about(key_of[1], (BATCH_MIDDLE, LEN_MIDDLE, D), 1.0, 6.0, ((0, 16), (1, 2)))
    tokens_long = scatter_about(key_of[2], (BATCH_LONG, LEN_LONG, D), 1.0, 6.0, ((0, 16), (1, 2)))
    length_short = draw_length_short(jax.random.fold_in(key_of[24], 71), 0)
    length_middle = draw_length_middle(jax.random.fold_in(key_of[24], 71), 0)
    length_long = draw_length_long(jax.random.fold_in(key_of[24], 71), 0)
    query_weight = scatter_about(key_of[6], (D, D), D ** -0.5, 0.21875)
    query_bias = scatter_about(key_of[7], (D,), 0.5, 3.0, (), jnp.float32)
    key_weight = scatter_about(key_of[8], (D, D), D ** -0.5, 0.21875)
    value_weight = scatter_about(key_of[9], (D, D), D ** -0.5, 0.21875)
    value_bias = scatter_about(key_of[10], (D,), 0.5, 3.0, (), jnp.float32)
    output_weight = scatter_about(key_of[11], (D, D), (D // 16) ** -0.5, 0.875)
    output_bias = scatter_about(key_of[12], (D,), 0.5, 3.0, (), jnp.float32)
    attention_gain = jnp.clip(1.0 + 0.18 * jax.random.normal(key_of[13], (D,), jnp.float32), 0.1, 1.9)
    attention_shift = scatter_about(key_of[14], (D,), 0.5, 3.0, (), jnp.float32)
    up_weight = scatter_about(key_of[15], (D, FF), D ** -0.5, 0.21875)
    up_bias = scatter_about(key_of[16], (FF,), 0.5, 3.0, (), jnp.float32)
    down_weight = scatter_about(key_of[17], (FF, D), FF ** -0.5, 0.109375)
    down_bias = scatter_about(key_of[18], (D,), 0.5, 3.0, (), jnp.float32)
    output_gain = jnp.clip(1.0 + 0.18 * jax.random.normal(key_of[19], (D,), jnp.float32), 0.1, 1.9)
    output_shift = scatter_about(key_of[20], (D,), 0.5, 3.0, (), jnp.float32)
    upstream_short = scatter_about(key_of[21], (BATCH_SHORT, LEN_SHORT, D), 1.0, 6.0, ((0, 16), (1, 2)))
    upstream_middle = scatter_about(key_of[22], (BATCH_MIDDLE, LEN_MIDDLE, D), 1.0, 6.0, ((0, 16), (1, 2)))
    upstream_long = scatter_about(key_of[23], (BATCH_LONG, LEN_LONG, D), 1.0, 6.0, ((0, 16), (1, 2)))
    return dict(tokens_short=tokens_short, tokens_middle=tokens_middle, tokens_long=tokens_long, length_short=length_short, length_middle=length_middle, length_long=length_long, query_weight=query_weight, query_bias=query_bias, key_weight=key_weight, value_weight=value_weight, value_bias=value_bias, output_weight=output_weight, output_bias=output_bias, attention_gain=attention_gain, attention_shift=attention_shift, up_weight=up_weight, up_bias=up_bias, down_weight=down_weight, down_bias=down_bias, output_gain=output_gain, output_shift=output_shift, upstream_short=upstream_short, upstream_middle=upstream_middle, upstream_long=upstream_long)


@jax.custom_vjp
def low(v):
    return lax.optimization_barrier(v.astype(jnp.bfloat16)).astype(jnp.float32)

@jax.custom_vjp
def low_back(v):
    return v

def low_keep(v):
    return (low(v), None)

def low_pass(kept, grad):
    return (grad,)

def back_keep(v):
    return (v, None)

def back_low(kept, grad):
    return (low(grad),)
low.defvjp(low_keep, low_pass)
low_back.defvjp(back_keep, back_low)
EPS = 1e-12
NEG = -1e+30
HIGH = lax.Precision.HIGHEST

def project(left, weight):
    return jnp.einsum('rtd,de->rte', left, weight, precision=HIGH)

def norm_rows(values, gain, shift):
    mean = lax.optimization_barrier(jnp.mean(values, axis=-1, keepdims=True))
    centred = values - mean
    spread = lax.optimization_barrier(jnp.mean(centred * centred, axis=-1, keepdims=True))
    return centred * lax.rsqrt(spread + EPS) * gain + shift

def attend_row(pieces):
    query, keys, values, length = pieces
    count = query.shape[0]
    q_heads = query.reshape(count, HEADS, HEAD_DIM)
    k_heads = keys.reshape(count, HEADS, HEAD_DIM)
    v_heads = values.reshape(count, HEADS, HEAD_DIM)
    scores = low_back(jnp.einsum('qhd,khd->hqk', q_heads, k_heads, precision=HIGH) * HEAD_DIM ** (-0.5))
    live = jnp.arange(count, dtype=jnp.int32) < length
    scores = jnp.where(live[None, None, :], scores, NEG)
    probs = jax.nn.softmax(scores, axis=-1)
    context = jnp.einsum('hqk,khd->qhd', low(probs), v_heads, precision=HIGH)
    return context.reshape(count, HEADS * HEAD_DIM)

def encoder(tokens, lengths, params):
    w_query, b_query, w_key, w_value, b_value, w_out, b_out, gain_one, shift_one, w_up, b_up, w_down, b_down, gain_two, shift_two = params
    query = low(low_back(project(tokens, w_query) + b_query))
    keys = low(low_back(project(tokens, w_key)))
    values = low(low_back(project(tokens, w_value) + b_value))
    context = lax.map(jax.checkpoint(attend_row), (query, keys, values, lengths))
    context = low(low_back(context))
    branch = low_back(project(context, w_out) + b_out)
    normed = norm_rows(tokens + branch, gain_one, shift_one)
    inner = low_back(project(low(normed), w_up) + b_up)
    act = low(jax.nn.gelu(inner, approximate=False))
    second = low_back(project(act, w_down) + b_down)
    return norm_rows(normed + second, gain_two, shift_two)

def reference(tokens_short, tokens_middle, tokens_long, length_short, length_middle, length_long, query_weight, query_bias, key_weight, value_weight, value_bias, output_weight, output_bias, attention_gain, attention_shift, up_weight, up_bias, down_weight, down_bias, output_gain, output_shift, upstream_short, upstream_middle, upstream_long):
    params = tuple((p.astype(jnp.float32) for p in (query_weight, query_bias, key_weight, value_weight, value_bias, output_weight, output_bias, attention_gain, attention_shift, up_weight, up_bias, down_weight, down_bias, output_gain, output_shift)))
    inputs = (tokens_short.astype(jnp.float32), tokens_middle.astype(jnp.float32), tokens_long.astype(jnp.float32))

    def forward(first, second, third, weights):
        return (encoder(first, length_short, weights), encoder(second, length_middle, weights), encoder(third, length_long, weights))
    outputs, backward = jax.vjp(forward, inputs[0], inputs[1], inputs[2], params)
    grads = backward((upstream_short.astype(jnp.float32), upstream_middle.astype(jnp.float32), upstream_long.astype(jnp.float32)))
    wg = grads[3]
    return (outputs[0].astype(jnp.bfloat16), outputs[1].astype(jnp.bfloat16), outputs[2].astype(jnp.bfloat16), grads[0].astype(jnp.bfloat16), grads[1].astype(jnp.bfloat16), grads[2].astype(jnp.bfloat16), wg[0], wg[1], wg[2], wg[3], wg[4], wg[5], wg[6], wg[7], wg[8], wg[9], wg[10], wg[11], wg[12], wg[13], wg[14])
```

```python
import functools

import jax
import jax.numpy as jnp
from jax import lax
from jax.experimental import pallas as pl
from jax.experimental.pallas import tpu as pltpu
from jax.sharding import PartitionSpec as P

D = 768
FF = 3072
HEADS = 12
PAIRS = HEADS // 2
EPS = 1e-12
NEG = -1e30
BLOCKS = 32
VMEM_LIMIT = 60 * 2**20

bf16 = jnp.bfloat16
f32 = jnp.float32
SDS = jax.ShapeDtypeStruct


def dot(a, b):
    return lax.dot_general(a, b, (((1,), (0,)), ((), ())), preferred_element_type=f32)


def dot_nt(a, b):
    return lax.dot_general(a, b, (((1,), (1,)), ((), ())), preferred_element_type=f32)


def dot_tn(a, b):
    return lax.dot_general(a, b, (((0,), (0,)), ((), ())), preferred_element_type=f32)


def mean(v):
    return jnp.mean(v, axis=-1, keepdims=True)


def column_sum(v):
    return jnp.sum(v.astype(f32), axis=0, keepdims=True)


A1, A2, A3, A4, A5 = 0.254829592, -0.284496736, 1.421413741, -1.453152027, 1.061405429
P_SCALED = 0.3275911 * 0.7071067811865476
INV_SQRT_2PI = 0.3989422804014327


def gelu_and_slope(v):
    t = 1.0 / (1.0 + P_SCALED * jnp.abs(v))
    e = jnp.exp(v * v * -0.5)
    tail = t * (A1 + t * (A2 + t * (A3 + t * (A4 + t * A5)))) * (0.5 * e)
    cdf = jnp.where(v < 0, tail, 1.0 - tail)
    return v * cdf, cdf + v * (e * INV_SQRT_2PI)


def mask_column(info, row, length):
    half = length // 2
    i = lax.broadcasted_iota(jnp.int32, (length, 1), 0)
    inner = jnp.where(i < half, i, i - half)
    place = inner + jnp.where(i < half, info[row, 1], info[row, 2])
    live = (place < info[row, 0]) & (inner < info[row, 3])
    return jnp.where(live, 0.0, NEG).astype(f32)


def low_lanes():
    return lax.broadcasted_iota(jnp.int32, (1, 128), 1) < 64


def stack_heads(pair, low):
    zero = jnp.zeros_like(pair)
    return jnp.concatenate([jnp.where(low, pair, zero), jnp.where(low, zero, pair)], axis=0)


def split_rows(pair_t):
    row = lax.broadcasted_iota(jnp.int32, (128, 1), 0) < 64
    zero = jnp.zeros_like(pair_t)
    return jnp.where(row, pair_t, zero), jnp.where(row, zero, pair_t)


def scaled(q):
    return (q.astype(f32) * 0.125).astype(bf16)


def emit_24(scr, lane, d, out, r, base):
    for g in range(3):
        rows = pl.ds(pl.multiple_of(24 * d + 8 * g, 8), 8)
        both = jnp.concatenate(
            [scr[rows, lane : lane + 384], scr[rows, lane + 384 : lane + 768]], axis=0
        )
        out[r, :, base + 384 * g : base + 384 * (g + 1)] = both.astype(bf16)


def block_number(half, r):
    return ((r >> 1) << 2) | (half << 1) | (r & 1)


def forward_kernel(info, xl, xr, wq, wk, wv, bq, bv, *rest, length, row, chained):
    x_o, q_o, k_o, v_o, c_o, lse_o = rest[6:] if chained else rest
    x = jnp.concatenate([xl[...], xr[...]], axis=0)
    x_o[...] = x
    q_o[...] = (dot(x, wq[...]) + bq[...]).astype(bf16)
    k_o[...] = dot(x, wk[...]).astype(bf16)
    v_o[...] = (dot(x, wv[...]) + bv[...]).astype(bf16)
    bias = mask_column(info, row, length)
    low = low_lanes()
    row_low = lax.broadcasted_iota(jnp.int32, (128, 1), 0) < 64
    for p in range(PAIRS):
        sl = slice(128 * p, 128 * p + 128)
        scores = dot_nt(stack_heads(k_o[:, sl], low), scaled(q_o[:, sl]))
        parts = []
        inverse = []
        for h in range(2):
            s = scores[h * length : (h + 1) * length, :] + bias
            top = jnp.max(s, axis=0, keepdims=True)
            raised = jnp.exp(s - top)
            total = jnp.sum(raised, axis=0, keepdims=True)
            lse_o[2 * p + h : 2 * p + h + 1, 0:length] = top + jnp.log(total)
            parts.append(raised.astype(bf16))
            inverse.append(1.0 / total)
        upper, lower = split_rows(v_o[:, sl].T)
        context = dot(upper, parts[0]) + dot(lower, parts[1])
        context = context * jnp.where(row_low, inverse[0], inverse[1])
        c_o[:, sl] = context.T.astype(bf16)


def attention_forward(info, own, other, weights, row, length, block, chain, rows):
    half = pl.BlockSpec((length // 2, D), lambda i: (0, 0))
    full = lambda a: pl.BlockSpec(a.shape, lambda i: (0, 0))
    tok = pl.BlockSpec((length, D), lambda i: (block, 0))
    lse = pl.BlockSpec((16, 512), lambda i: (row, 0))
    chained = chain is not None
    extra = list(chain) if chained else []
    flops = 2 * length * D * D * 3 + 4 * length * length * 256 * HEADS
    return pl.pallas_call(
        functools.partial(forward_kernel, length=length, row=row, chained=chained),
        grid=(1,),
        in_specs=[pl.BlockSpec(memory_space=pltpu.SMEM), half, half]
        + [full(w) for w in weights]
        + [pl.BlockSpec(memory_space=pl.ANY)] * len(extra),
        out_specs=[tok] * 5 + [lse],
        out_shape=[SDS((rows, D), bf16)] * 5 + [SDS((48, 512), f32)],
        input_output_aliases={8 + i: i for i in range(6)} if chained else {},
        compiler_params=pltpu.CompilerParams(vmem_limit_bytes=VMEM_LIMIT),
        cost_estimate=pl.CostEstimate(
            flops=flops, bytes_accessed=12 * length * D + 6 * D * D, transcendentals=0
        ),
        name=f"attend_{row}",
    )(info, own, other, *weights, *extra)


def dense_kernel(
    ctx, x, up, wo, wup, wdn, bo, g1, s1, bup, bdn, g2, s2,
    res, act, dinn, nlow_o, dbr, datt, dr1_o, dctx, vec, slope_s, bupg, *, chunks
):
    step = pl.program_id(0)

    @pl.when(step == 0)
    def _():
        vec[...] = jnp.zeros_like(vec)
        bupg[...] = jnp.zeros_like(bupg)

    r1 = x[...].astype(f32) + dot(ctx[...], wo[...]) + bo[...]
    c1 = r1 - mean(r1)
    rs1 = lax.rsqrt(mean(c1 * c1) + EPS)
    n1 = c1 * rs1
    normed = n1 * g1[...] + s1[...]
    nlow = normed.astype(bf16)
    nlow_o[...] = nlow
    acc = normed + bdn[...]
    width = FF // chunks
    for j in range(chunks):
        sl = slice(j * width, (j + 1) * width)
        value, slope = gelu_and_slope(dot(nlow, wup[:, sl]) + bup[:, sl])
        value = value.astype(bf16)
        act[:, sl] = value
        slope_s[:, sl] = slope
        acc = acc + dot(value, wdn[sl, :])
    c2 = acc - mean(acc)
    rs2 = lax.rsqrt(mean(c2 * c2) + EPS)
    n2 = c2 * rs2
    res[...] = (n2 * g2[...] + s2[...]).astype(bf16)
    upstream = up[...].astype(f32)
    u = upstream * g2[...]
    dr2 = (u - mean(u) - n2 * mean(u * n2)) * rs2
    branch = dr2.astype(bf16)
    dbr[...] = branch
    vec[0:1, :] += column_sum(upstream * n2)
    vec[1:2, :] += column_sum(upstream)
    vec[2:3, :] += column_sum(branch)
    acc = dr2
    for j in range(chunks):
        sl = slice(j * width, (j + 1) * width)
        d_inner = (dot_nt(branch, wdn[sl, :]) * slope_s[:, sl]).astype(bf16)
        dinn[:, sl] = d_inner
        bupg[:, sl] += column_sum(d_inner)
        acc = acc + dot_nt(d_inner, wup[:, sl])
    vec[3:4, :] += column_sum(acc * n1)
    vec[4:5, :] += column_sum(acc)
    u1 = acc * g1[...]
    d1 = (u1 - mean(u1) - n1 * mean(u1 * n1)) * rs1
    d_attn = d1.astype(bf16)
    datt[...] = d_attn
    dr1_o[...] = d1
    vec[5:6, :] += column_sum(d_attn)
    dctx[...] = dot_nt(d_attn, wo[...]).astype(bf16)

    @pl.when(step == pl.num_programs(0) - 1)
    def _():
        for k in range(4):
            vec[8 + k : 9 + k, :] = bupg[:, k * D : (k + 1) * D]


def dense_steps(ctx, x, up, mats, vecs, tokens, rows):
    tile = 256
    tok = pl.BlockSpec((tile, D), lambda i: (i, 0))
    ffs = pl.BlockSpec((tile, FF), lambda i: (i, 0))
    full = lambda a: pl.BlockSpec(a.shape, lambda i: (0, 0), pipeline_mode=pl.Buffered(1))
    return pl.pallas_call(
        functools.partial(dense_kernel, chunks=4),
        grid=(tokens // tile,),
        in_specs=[tok] * 3 + [full(a) for a in mats + vecs],
        out_specs=[tok, ffs, ffs] + [tok] * 5 + [pl.BlockSpec((16, D), lambda i: (0, 0))],
        out_shape=[
            SDS((tokens, D), bf16),
            SDS((tokens, FF), bf16),
            SDS((tokens, FF), bf16),
            SDS((tokens, D), bf16),
            SDS((tokens, D), bf16),
            SDS((tokens, D), bf16),
            SDS((rows, D), f32),
            SDS((rows, D), bf16),
            SDS((16, D), f32),
        ],
        scratch_shapes=[pltpu.VMEM((tile, FF), f32), pltpu.VMEM((1, FF), f32)],
        compiler_params=pltpu.CompilerParams(vmem_limit_bytes=VMEM_LIMIT),
        cost_estimate=pl.CostEstimate(
            flops=2 * tokens * D * D * 18, bytes_accessed=24 * tokens * D, transcendentals=0
        ),
        name="dense",
    )(ctx, x, up, *mats, *vecs)


def up_grad_kernel(me, nlow, left, right, send, keep, turned, scr):
    @pl.when(pl.program_id(0) == 0)
    def _():
        turned[...] = nlow[...].T

    scr[:, 0:384] = dot(turned[...], left[...])
    scr[:, 384:768] = dot(turned[...], right[...])
    for half, out in ((0, keep), (1, send)):
        for r in range(16):
            emit_24(scr, 0, block_number(half, r) ^ me[0], out, r, 0)


def up_grad(me, nlow, dinn, tokens):
    out = pl.BlockSpec((16, 16, 1152), lambda j, m: (0, 0, j))
    return pl.pallas_call(
        up_grad_kernel,
        grid_spec=pltpu.PrefetchScalarGridSpec(
            num_scalar_prefetch=1,
            grid=(4,),
            in_specs=[
                pl.BlockSpec((tokens, D), lambda j, m: (0, 0)),
                pl.BlockSpec((tokens, 384), lambda j, m: (0, j)),
                pl.BlockSpec((tokens, 384), lambda j, m: (0, j + 4)),
            ],
            out_specs=[out, out],
            scratch_shapes=[pltpu.VMEM((D, tokens), bf16), pltpu.VMEM((D, D), f32)],
        ),
        out_shape=[SDS((16, 16, 4608), bf16)] * 2,
        compiler_params=pltpu.CompilerParams(vmem_limit_bytes=VMEM_LIMIT),
        cost_estimate=pl.CostEstimate(
            flops=2 * tokens * D * FF, bytes_accessed=8 * tokens * D + 4 * D * FF, transcendentals=0
        ),
        name="up_grad",
    )(me, nlow, dinn, dinn)


DOWN_WIDTH = 4608 + 1152 + 128


def down_grad_kernel(me, act, dbr, ctx, datt, vec, send, keep, scr, wo_s):
    j = pl.program_id(0)

    @pl.when(j == 0)
    def _():
        wo_s[...] = dot_tn(ctx[...], datt[...])

    scr[...] = dot_tn(act[...], dbr[...])
    z = j ^ (me[0] >> 3)
    for half, out in ((0, keep), (1, send)):
        for r in range(4):
            near = block_number(half, r) ^ (me[0] & 7)
            d = z * 8 + near
            for g in range(6):
                rows = pl.ds(pl.multiple_of(96 * near + 16 * g, 16), 16)
                out[r, :, D * g : D * (g + 1)] = scr[rows, :].astype(bf16)
            emit_24(wo_s, 0, d, out, r, 4608)
            small = pltpu.roll(vec[0:8, :], lax.rem(D - 24 * d, D), 1)[:, 0:128]
            wide = pltpu.roll(vec[8:16, :], lax.rem(D - 96 * near, D), 1)[:, 0:128]
            out[r, :, 5760:5888] = jnp.concatenate([small, wide], axis=0).astype(bf16)


def down_grad(me, act, dbr, ctx, datt, vec, tokens):
    out = pl.BlockSpec((4, 16, DOWN_WIDTH), lambda j, m: (j, 0, 0))
    tok = pl.BlockSpec((tokens, D), lambda j, m: (0, 0))
    return pl.pallas_call(
        down_grad_kernel,
        grid_spec=pltpu.PrefetchScalarGridSpec(
            num_scalar_prefetch=1,
            grid=(4,),
            in_specs=[
                pl.BlockSpec((tokens, D), lambda j, m: (0, j ^ (m[0] >> 3))),
                tok,
                tok,
                tok,
                pl.BlockSpec((16, D), lambda j, m: (0, 0)),
            ],
            out_specs=[out, out],
            scratch_shapes=[pltpu.VMEM((D, D), f32), pltpu.VMEM((D, D), f32)],
        ),
        out_shape=[SDS((16, 16, DOWN_WIDTH), bf16)] * 2,
        compiler_params=pltpu.CompilerParams(vmem_limit_bytes=VMEM_LIMIT),
        cost_estimate=pl.CostEstimate(
            flops=2 * tokens * D * (FF + D),
            bytes_accessed=12 * tokens * D + 4 * D * FF,
            transcendentals=0,
        ),
        name="down_grad",
    )(me, act, dbr, ctx, datt, vec)


QKV_WIDTH = 3 * 1152 + 128


def backward_row(info, row, length, q_r, k_r, v_r, g_r, lse, dr1, x, wq, wk, wv, ig, dw, bg, dq_s, dk_s, dv_s):
    n = slice(0, length)
    bias = mask_column(info, row, length)
    low = low_lanes()
    for p in range(PAIRS):
        sl = slice(128 * p, 128 * p + 128)
        q2 = scaled(q_r[n, sl])
        k2 = k_r[n, sl]
        g2 = g_r[n, sl]
        scores = dot_nt(stack_heads(k2, low), q2)
        d_probs = dot_nt(stack_heads(v_r[n, sl], low), g2)
        probs_low = []
        d_scores = []
        for h in range(2):
            part = slice(h * length, (h + 1) * length)
            probs = jnp.exp(scores[part, :] + bias - lse[2 * p + h : 2 * p + h + 1, n])
            d_part = d_probs[part, :]
            centre = jnp.sum(probs * d_part, axis=0, keepdims=True)
            probs_low.append(probs.astype(bf16))
            d_scores.append((probs * (d_part - centre)).astype(bf16))
        dv_s[n, sl] = jnp.where(low, dot(probs_low[0], g2), dot(probs_low[1], g2)).astype(bf16)
        dk_s[n, sl] = jnp.where(low, dot(d_scores[0], q2), dot(d_scores[1], q2)).astype(bf16)
        upper, lower = split_rows(k2.T)
        turned = dot(upper, d_scores[0]) + dot(lower, d_scores[1])
        dq_s[n, sl] = (turned * 0.125).T.astype(bf16)
    dq, dk, dv = dq_s[n, :], dk_s[n, :], dv_s[n, :]
    ig[n, :] = (
        dr1[n, :] + dot_nt(dq, wq[...]) + dot_nt(dk, wk[...]) + dot_nt(dv, wv[...])
    ).astype(bf16)
    bg[0:1, :] += column_sum(dq)
    bg[1:2, :] += column_sum(dv)
    tokens = x[n, :]
    dw[:, 0:768] += dot_tn(tokens, dq)
    dw[:, 768:1536] += dot_tn(tokens, dk)
    dw[:, 1536:2304] += dot_tn(tokens, dv)


def backward_kernel(
    me, info, q_r, k_r, v_r, g_r, lse, dr1, x, wq, wk, wv, ig, send, keep, bg, dw, dq_s, dk_s, dv_s,
    *, lengths
):
    step = pl.program_id(0)

    @pl.when(step == 0)
    def _():
        dw[...] = jnp.zeros_like(dw)
        bg[...] = jnp.zeros_like(bg)

    args = (q_r, k_r, v_r, g_r, lse, dr1, x, wq, wk, wv, ig, dw, bg, dq_s, dk_s, dv_s)

    @pl.when(step < 2)
    def _():
        backward_row(info, step, lengths[0], *args)

    @pl.when(step == 2)
    def _():
        backward_row(info, step, lengths[2], *args)
        for half, out in ((0, keep), (1, send)):
            for r in range(16):
                d = block_number(half, r) ^ me[0]
                for a in range(3):
                    emit_24(dw, D * a, d, out, r, 1152 * a)
                small = pltpu.roll(bg[...], lax.rem(D - 24 * d, D), 1)[:, 0:128]
                out[r, :, 3456:3584] = jnp.concatenate([small, small], axis=0).astype(bf16)


def attention_backward(me, info, q, k, v, dctx, lse, dr1, x, wq, wk, wv, lengths, rows):
    tok = pl.BlockSpec((512, D), lambda i, m, n: (i, 0))
    full = pl.BlockSpec((D, D), lambda i, m, n: (0, 0), pipeline_mode=pl.Buffered(1))
    out = pl.BlockSpec((16, 16, QKV_WIDTH), lambda i, m, n: (0, 0, 0))
    return pl.pallas_call(
        functools.partial(backward_kernel, lengths=lengths),
        grid_spec=pltpu.PrefetchScalarGridSpec(
            num_scalar_prefetch=2,
            grid=(3,),
            in_specs=[tok] * 4 + [pl.BlockSpec((16, 512), lambda i, m, n: (i, 0)), tok, tok] + [full] * 3,
            out_specs=[tok, out, out, pl.BlockSpec((8, D), lambda i, m, n: (0, 0))],
            scratch_shapes=[pltpu.VMEM((D, 2304), f32)] + [pltpu.VMEM((512, D), bf16)] * 3,
        ),
        out_shape=[
            SDS((rows, D), bf16),
            SDS((16, 16, QKV_WIDTH), bf16),
            SDS((16, 16, QKV_WIDTH), bf16),
            SDS((8, D), f32),
        ],
        compiler_params=pltpu.CompilerParams(vmem_limit_bytes=VMEM_LIMIT),
        cost_estimate=pl.CostEstimate(
            flops=2 * sum(lengths) * D * D * 6 + sum(10 * n * n * 256 * HEADS for n in lengths),
            bytes_accessed=20 * rows * D,
            transcendentals=0,
        ),
        name="attend_back",
    )(me, info, q, k, v, dctx, lse, dr1, x, wq, wk, wv)


def swap_seq(v):
    return lax.ppermute(v, "seq", [(0, 1), (1, 0)])


def swap_dp(v, bit):
    n = lax.axis_size("dp")
    return lax.ppermute(v, "dp", [(i, i ^ bit) for i in range(n)])


STEPS = {"x": (3, swap_seq), "y": (2, lambda v: swap_dp(v, 2)), "z": (1, lambda v: swap_dp(v, 4)), "w": (0, lambda v: swap_dp(v, 8))}


def halve(send, keep, order):
    width = send.shape[-1]
    received = swap_dp(send, 1).reshape(2, 2, 2, 2, 16, width)
    kept = keep.reshape(2, 2, 2, 2, 16, width)
    for name in order:
        axis, swap = STEPS[name]
        part = lambda v, i: lax.index_in_dim(v, i, axis, keepdims=True)
        outgoing = (part(received, 1).astype(f32) + part(kept, 1).astype(f32)).astype(bf16)
        staying = (part(received, 0).astype(f32) + part(kept, 0).astype(f32)).astype(bf16)
        received, kept = swap(outgoing), staying
    return (received.astype(f32) + kept.astype(f32)).reshape(16, width)


def rows_24(block):
    return block.reshape(2, 8, 3, 384).transpose(2, 1, 0, 3).reshape(24, D)


def unpack_up(block):
    return block.reshape(2, 8, 4, 3, 384).transpose(3, 1, 0, 2, 4).reshape(24, FF)


def unpack_down(block):
    return block[:, :4608].reshape(16, 6, D).transpose(1, 0, 2).reshape(96, D), rows_24(block[:, 4608:5760])


def unpack_qkv(block):
    return [rows_24(block[:, 1152 * a : 1152 * (a + 1)]) for a in range(3)]


def reduce_payloads(up_pair, down_pair, qkv_pair, me):
    up = halve(*up_pair, "yzxw")
    down = halve(*down_pair, "zxyw")
    qkv = halve(*qkv_pair, "xyzw")
    w_up = unpack_up(up)
    w_down, w_out = unpack_down(down)
    w_query, w_key, w_value = unpack_qkv(qkv)
    vec = down[:8, 5760:5784]
    b_up = lax.dynamic_slice(down, (8 + (me >> 3), 5760), (1, 96))[0]
    bq, bv = qkv[0, 3456:3480], qkv[1, 3456:3480]
    return w_query, bq, w_key, w_value, bv, w_out, vec, w_up, b_up, w_down


def reduce_plain(up_pair, down_pair, qkv_pair, vec, bg):
    def ordered(pair):
        send, keep = pair
        both = jnp.stack([keep.reshape(8, 2, 16, -1), send.reshape(8, 2, 16, -1)], axis=1)
        return both.reshape(BLOCKS, 16, -1).astype(f32)

    scatter = lambda v: lax.psum_scatter(v, ("dp", "seq"), scatter_dimension=0, tiled=True)
    w_up = jax.vmap(unpack_up)(ordered(up_pair)).reshape(D, FF)
    w_down, w_out = (a.reshape(-1, D) for a in jax.vmap(unpack_down)(ordered(down_pair)))
    qkv = [a.reshape(D, D) for a in jax.vmap(unpack_qkv)(ordered(qkv_pair))]
    small = [scatter(vec[i]) for i in range(6)]
    return (
        scatter(qkv[0]), scatter(bg[0]), scatter(qkv[1]), scatter(qkv[2]), scatter(bg[1]), scatter(w_out),
        small, scatter(w_up), scatter(vec[8:12].reshape(FF)), scatter(w_down),
    )


def per_device(
    tokens_short, tokens_middle, tokens_long, length_short, length_middle, length_long,
    query_weight, query_bias, key_weight, value_weight, value_bias, output_weight, output_bias,
    attention_gain, attention_shift, up_weight, up_bias, down_weight, down_bias, output_gain, output_shift,
    upstream_short, upstream_middle, upstream_long,
):
    seq = lax.axis_index("seq")
    first = seq == 0
    device = (lax.axis_index("dp") * 2 + seq).astype(jnp.int32)
    fast = lax.axis_size("dp") * lax.axis_size("seq") == BLOCKS
    me = device if fast else jnp.int32(0)
    me_ref = me.reshape(1)
    count, half, _ = tokens_long.shape
    mine = count // 2
    mid = tokens_middle.shape[1]
    short = tokens_short.shape[1]
    lengths = (2 * half,) * mine + (2 * mid,)
    tokens = sum(lengths)
    rows = 2 * half * (mine + 1)

    def own_rows(v):
        return lax.dynamic_slice_in_dim(v, mine * seq, mine, 0)

    def other_rows(v):
        return lax.dynamic_slice_in_dim(v, mine * (1 - seq), mine, 0)

    def middle_rows(middle, low):
        low = jnp.pad(low[0], ((0, mid - short), (0, 0)))
        return jnp.where(first, middle[0], low), jnp.where(first, low, middle[0])

    x_mid, x_mid_out = middle_rows(tokens_middle, tokens_short)
    x_own, x_out = own_rows(tokens_long), other_rows(tokens_long)
    x_mid_in = swap_seq(x_mid_out)
    x_in = [swap_seq(x_out[i]) for i in range(mine)]
    u_mid, u_mid_out = middle_rows(upstream_middle, upstream_short)
    u_own = own_rows(upstream_long)
    u_in = swap_seq(jnp.concatenate([other_rows(upstream_long).reshape(mine * half, D), u_mid_out], axis=0))

    own_lengths = lax.dynamic_slice_in_dim(length_long, mine * seq, mine, 0)
    long_info = jnp.stack(
        [own_lengths, jnp.full((mine,), seq * half), jnp.full((mine,), (1 - seq) * half), jnp.full((mine,), half)], axis=1
    ).astype(jnp.int32)
    mid_info = jnp.where(
        first,
        jnp.stack([length_middle[0], 0, mid, mid]),
        jnp.stack([length_short[0], short, 0, short]),
    ).astype(jnp.int32)
    info = jnp.concatenate([long_info, mid_info[None]], axis=0)

    row = lambda v: v.reshape(1, -1)
    qkv = [query_weight, key_weight, value_weight, row(query_bias), row(value_bias)]
    chain = attention_forward(info, x_mid, x_mid_in, qkv, mine, 2 * mid, mine * half // mid, None, rows)
    for i in range(mine):
        chain = attention_forward(info, x_own[i], x_in[i], qkv, i, 2 * half, i, chain, rows)
    x, q, k, v, ctx, lse = chain

    pieces = []
    for i in range(mine):
        pieces += [u_own[i], u_in[i * half : (i + 1) * half]]
    up = jnp.concatenate(pieces + [u_mid, u_in[mine * half :]], axis=0)
    mats = [output_weight, up_weight, down_weight]
    vecs = [row(a) for a in (output_bias, attention_gain, attention_shift, up_bias, down_bias, output_gain, output_shift)]
    res, act, dinn, nlow, dbr, datt, dr1, dctx, vec = dense_steps(ctx, x, up, mats, vecs, tokens, rows)

    def give_back(v):
        body = v[: mine * 2 * half].reshape(mine, 2, half, D)
        tail = v[mine * 2 * half : tokens].reshape(2, mid, D)
        got = swap_seq(jnp.concatenate([body[:, 1].reshape(mine * half, D), tail[1]], axis=0))
        here, there = body[:, 0], got[: mine * half].reshape(mine, half, D)
        long = jnp.concatenate([jnp.where(first, here, there), jnp.where(first, there, here)], axis=0)
        low, middle = jnp.where(first, got[mine * half :], tail[0]), jnp.where(first, tail[0], got[mine * half :])
        return low[None, :short], middle[None], long

    results = give_back(res)
    up_pair = up_grad(me_ref, nlow, dinn, tokens)
    down_pair = down_grad(me_ref, act, dbr, ctx, datt, vec, tokens)
    ig, send, keep, bg = attention_backward(
        me_ref, info, q, k, v, dctx, lse, dr1, x, query_weight, key_weight, value_weight, lengths, rows
    )
    qkv_pair = (send, keep)
    input_grads = give_back(ig)
    if fast:
        done = reduce_payloads(up_pair, down_pair, qkv_pair, me)
    else:
        done = reduce_plain(up_pair, down_pair, qkv_pair, vec, bg)
    w_query, bq, w_key, w_value, bv, w_out, small, w_up, b_up, w_down = done
    return (
        *results, *input_grads,
        w_query, bq, w_key, w_value, bv, w_out, small[5], small[3], small[4],
        w_up, b_up, w_down, small[2], small[0], small[1],
    )


def solution(mesh):
    tokens = P("dp", "seq", None)
    wide = P(("dp", "seq"), None)
    flat = P(("dp", "seq"))
    in_specs = (tokens,) * 3 + (P("dp"),) * 3 + (P(),) * 15 + (tokens,) * 3
    out_specs = (tokens,) * 6 + (
        wide, flat, wide, wide, flat, wide, flat, flat, flat, wide, flat, wide, flat, flat, flat,
    )
    return jax.shard_map(per_device, mesh=mesh, in_specs=in_specs, out_specs=out_specs, check_vma=False)
```

```python
import functools

import jax
import jax.numpy as jnp
from jax import lax
from jax.experimental import pallas as pl
from jax.experimental.pallas import tpu as pltpu
from jax.sharding import PartitionSpec as P

D = 768
FF = 3072
HEADS = 12
PAIRS = HEADS // 2
EPS = 1e-12
NEG = -1e30
SHORT_HALF = 64
BLOCKS = 32
VMEM_LIMIT = 60 * 2**20

bf16 = jnp.bfloat16
f32 = jnp.float32
SDS = jax.ShapeDtypeStruct
ANY = pl.BlockSpec(memory_space=pl.ANY)
HINT = pl.CostEstimate(flops=1024, bytes_accessed=1024, transcendentals=0)


def dot(a, b):
    return lax.dot_general(a, b, (((1,), (0,)), ((), ())), preferred_element_type=f32)


def dot_nt(a, b):
    return lax.dot_general(a, b, (((1,), (1,)), ((), ())), preferred_element_type=f32)


def dot_tn(a, b):
    return lax.dot_general(a, b, (((0,), (0,)), ((), ())), preferred_element_type=f32)


def wide(vector):
    return vector[...].reshape(1, -1)


def mean(v):
    return jnp.mean(v, axis=-1, keepdims=True)


def column_sum(v):
    return jnp.sum(v.astype(f32), axis=0, keepdims=True)


A1, A2, A3, A4, A5 = 0.254829592, -0.284496736, 1.421413741, -1.453152027, 1.061405429
P_SCALED = 0.3275911 * 0.7071067811865476
INV_SQRT_2PI = 0.3989422804014327


def gelu_and_slope(v):
    t = 1.0 / (1.0 + P_SCALED * jnp.abs(v))
    e = jnp.exp(v * v * -0.5)
    tail = t * (A1 + t * (A2 + t * (A3 + t * (A4 + t * A5)))) * (0.5 * e)
    cdf = jnp.where(v < 0, tail, 1.0 - tail)
    return v * cdf, cdf + v * (e * INV_SQRT_2PI)


def mask_column(place, row, length):
    seq, short, middle, long = place
    half = length // 2
    mine = long.shape[0] // 2
    s = seq[0]
    if row < mine:
        count, valid, own, other = long[mine * s + row], half, half * s, half * (1 - s)
    else:
        is_first = s == 0
        count = jnp.where(is_first, middle[0], short[0])
        valid = jnp.where(is_first, half, SHORT_HALF)
        own, other = jnp.where(is_first, 0, SHORT_HALF), jnp.where(is_first, half, 0)
    i = lax.broadcasted_iota(jnp.int32, (length, 1), 0)
    inner = jnp.where(i < half, i, i - half)
    live = (inner + jnp.where(i < half, own, other) < count) & (inner < valid)
    return jnp.where(live, 0.0, NEG).astype(f32)


def low_lanes():
    return lax.broadcasted_iota(jnp.int32, (1, 128), 1) < 64


def stack_heads(pair, low):
    zero = jnp.zeros_like(pair)
    return jnp.concatenate([jnp.where(low, pair, zero), jnp.where(low, zero, pair)], axis=0)


def split_rows(pair_t):
    row = lax.broadcasted_iota(jnp.int32, (128, 1), 0) < 64
    zero = jnp.zeros_like(pair_t)
    return jnp.where(row, pair_t, zero), jnp.where(row, zero, pair_t)


def scaled(q):
    return (q.astype(f32) * 0.125).astype(bf16)


def emit_24(scr, lane, d, out, r, base):
    for g in range(3):
        rows = pl.ds(pl.multiple_of(24 * d + 8 * g, 8), 8)
        both = jnp.concatenate(
            [scr[rows, lane : lane + 384], scr[rows, lane + 384 : lane + 768]], axis=0
        )
        out[r, :, base + 384 * g : base + 384 * (g + 1)] = both.astype(bf16)


def block_number(half, r):
    return ((r >> 1) << 2) | (half << 1) | (r & 1)


def forward_kernel(s0, s1, s2, s3, xl, xr, wq, wk, wv, bq, bv, *rest, length, row, chained):
    x_o, q_o, k_o, v_o, c_o, lse_o, xt_o = rest[7:] if chained else rest
    x = jnp.concatenate([xl[...], xr[...]], axis=0)
    x_o[...] = x
    xt_o[...] = x.T
    q_o[...] = (dot(x, wq[...]) + wide(bq)).astype(bf16)
    k_o[...] = dot(x, wk[...]).astype(bf16)
    v_o[...] = (dot(x, wv[...]) + wide(bv)).astype(bf16)
    bias = mask_column((s0, s1, s2, s3), row, length)
    low = low_lanes()
    row_low = lax.broadcasted_iota(jnp.int32, (128, 1), 0) < 64
    for p in range(PAIRS):
        sl = slice(128 * p, 128 * p + 128)
        scores = dot_nt(stack_heads(k_o[:, sl], low), scaled(q_o[:, sl]))
        parts = []
        inverse = []
        for h in range(2):
            s = scores[h * length : (h + 1) * length, :] + bias
            top = jnp.max(s, axis=0, keepdims=True)
            raised = jnp.exp(s - top)
            total = jnp.sum(raised, axis=0, keepdims=True)
            lse_o[2 * p + h : 2 * p + h + 1, 0:length] = top + jnp.log(total)
            parts.append(raised.astype(bf16))
            inverse.append(1.0 / total)
        upper, lower = split_rows(v_o[:, sl].T)
        context = dot(upper, parts[0]) + dot(lower, parts[1])
        context = context * jnp.where(row_low, inverse[0], inverse[1])
        c_o[:, sl] = context.T.astype(bf16)


def attention_forward(place, own, other, weights, row, length, block, chain, rows):
    half = pl.BlockSpec((length // 2, D), lambda i: (0, 0))
    full = lambda a: pl.BlockSpec(a.shape, lambda i: (0,) * a.ndim)
    tok = pl.BlockSpec((length, D), lambda i: (block, 0))
    lse = pl.BlockSpec((16, 512), lambda i: (row, 0))
    turned = pl.BlockSpec((D, length), lambda i: (0, block))
    chained = chain is not None
    extra = list(chain) if chained else []
    return pl.pallas_call(
        functools.partial(forward_kernel, length=length, row=row, chained=chained),
        grid=(1,),
        in_specs=[pl.BlockSpec(memory_space=pltpu.SMEM)] * 4
        + [half, half]
        + [full(w) for w in weights]
        + [ANY] * len(extra),
        out_specs=[tok] * 5 + [lse, turned],
        out_shape=[SDS((rows, D), bf16)] * 5 + [SDS((48, 512), f32), SDS((D, rows), bf16)],
        input_output_aliases={11 + i: i for i in range(7)} if chained else {},
        compiler_params=pltpu.CompilerParams(vmem_limit_bytes=VMEM_LIMIT),
        cost_estimate=HINT,
        name=f"attend_{row}",
    )(*place, own, other, *weights, *extra)


def drop_first(kernel):
    return lambda _, *refs, **options: kernel(*refs, **options)


def dense_kernel(*refs, chunks, own):
    ctx, x = refs[0], refs[1]
    step = pl.program_id(0)
    last = step == pl.num_programs(0) - 1
    if own:
        up_refs, refs = refs[2:3], refs[3:]
        up = up_refs[0][0]
    else:
        up_refs, refs = refs[2:5], refs[5:]
        up = jnp.concatenate([jnp.where(last, up_refs[2][...], up_refs[0][...]), up_refs[1][...]], axis=0)
    wo, wup, wdn, bup, bo, g1, s1, bdn, g2, s2 = refs[:10]
    bup, bo, g1, s1, bdn, g2, s2 = (wide(v) for v in (bup, bo, g1, s1, bdn, g2, s2))
    if own:
        res_own, act, dinn, nlow_o, dbr, datt, dr1_o, dctx, vec, slope_s = refs[10:]
    else:
        vec_in = refs[10]
        res_other, res_mid, act, dinn, nlow_o, dbr, datt, dr1_o, dctx, vec, slope_s = refs[18:]

    @pl.when(step == 0)
    def _():
        vec[...] = jnp.zeros_like(vec) if own else vec_in[...]

    r1 = x[...].astype(f32) + dot(ctx[...], wo[...]) + bo
    c1 = r1 - mean(r1)
    rs1 = lax.rsqrt(mean(c1 * c1) + EPS)
    n1 = c1 * rs1
    normed = n1 * g1 + s1
    nlow = normed.astype(bf16)
    nlow_o[...] = nlow
    acc = normed + bdn
    width = FF // chunks
    for j in range(chunks):
        sl = slice(j * width, (j + 1) * width)
        value, slope = gelu_and_slope(dot(nlow, wup[:, sl]) + bup[:, sl])
        value = value.astype(bf16)
        act[:, sl] = value
        slope_s[:, sl] = slope
        acc = acc + dot(value, wdn[sl, :])
    c2 = acc - mean(acc)
    rs2 = lax.rsqrt(mean(c2 * c2) + EPS)
    n2 = c2 * rs2
    result = (n2 * g2 + s2).astype(bf16)
    if own:
        res_own[...] = result
    else:
        size = result.shape[0]

        @pl.when(jnp.logical_not(last))
        def _():
            res_other[pl.ds(pl.multiple_of(step * size, size), size), :] = result

        @pl.when(last)
        def _():
            res_mid[...] = result[: size // 2]
            res_other[res_other.shape[0] - size // 2 :, :] = result[size // 2 :]

    upstream = up.astype(f32)
    u = upstream * g2
    dr2 = (u - mean(u) - n2 * mean(u * n2)) * rs2
    branch = dr2.astype(bf16)
    dbr[...] = branch
    vec[0:1, :] += column_sum(upstream * n2)
    vec[1:2, :] += column_sum(upstream)
    vec[2:3, :] += column_sum(branch)
    acc = dr2
    for j in range(chunks):
        sl = slice(j * width, (j + 1) * width)
        d_inner = (dot_nt(branch, wdn[sl, :]) * slope_s[:, sl]).astype(bf16)
        dinn[:, sl] = d_inner
        vec[8 + j : 9 + j, :] += column_sum(d_inner)
        acc = acc + dot_nt(d_inner, wup[:, sl])
    vec[3:4, :] += column_sum(acc * n1)
    vec[4:5, :] += column_sum(acc)
    u1 = acc * g1
    d1 = (u1 - mean(u1) - n1 * mean(u1 * n1)) * rs1
    d_attn = d1.astype(bf16)
    datt[...] = d_attn
    dr1_o[...] = d1
    vec[5:6, :] += column_sum(d_attn)
    dctx[...] = dot_nt(d_attn, wo[...]).astype(bf16)


def dense_steps(seq, ctx, x, ups, mats, vecs, tokens, rows, before):
    tile = 256
    half = tile // 2
    mine = tokens // tile // 2
    own = before is None
    full = lambda a: pl.BlockSpec(a.shape, lambda i, s: (0,) * a.ndim, pipeline_mode=pl.Buffered(1))
    whole = lambda n: pl.BlockSpec((n, D), lambda i, s: (0, 0))
    if own:
        place = lambda i: 2 * i
        steps = mine
        up_specs = [pl.BlockSpec((1, tile, D), lambda i, s: (s[0] * mine + i, 0, 0))]
        res_specs = [pl.BlockSpec((tile, D), lambda i, s: (i, 0))]
        res_shapes = [SDS((mine * tile, D), bf16)]
        extra, extra_specs, aliases = [], [], {}
    else:
        place = lambda i: jnp.minimum(2 * i + 1, 2 * mine)
        steps = mine + 1
        up_specs = [
            pl.BlockSpec((half, D), lambda i, s: (jnp.minimum(2 * i, 2 * mine - 2), 0)),
            pl.BlockSpec((half, D), lambda i, s: (jnp.minimum(2 * i + 1, 2 * mine), 0)),
            whole(half),
        ]
        res_specs = [whole(tokens // 2), whole(half)]
        res_shapes = [SDS((tokens // 2, D), bf16), SDS((half, D), bf16)]
        *arrays, vec = before
        extra = [vec] + arrays
        extra_specs = [whole(16)] + [ANY] * len(arrays)
        first = 1 + 2 + len(ups) + len(mats) + len(vecs) + 1
        aliases = {first + i: 2 + i for i in range(len(arrays))}
    tok = pl.BlockSpec((tile, D), lambda i, s: (place(i), 0))
    ffs = pl.BlockSpec((tile, FF), lambda i, s: (place(i), 0))
    return pl.pallas_call(
        functools.partial(drop_first(dense_kernel), chunks=4, own=own),
        grid_spec=pltpu.PrefetchScalarGridSpec(
            num_scalar_prefetch=1,
            grid=(steps,),
            in_specs=[tok, tok] + up_specs + [full(a) for a in mats + vecs] + extra_specs,
            out_specs=res_specs + [ffs, ffs] + [tok] * 5 + [whole(16)],
            scratch_shapes=[pltpu.VMEM((tile, FF), f32)],
        ),
        out_shape=res_shapes
        + [SDS((tokens, FF), bf16)] * 2
        + [SDS((tokens, D), bf16)] * 3
        + [SDS((rows, D), f32), SDS((rows, D), bf16), SDS((16, D), f32)],
        input_output_aliases=aliases,
        compiler_params=pltpu.CompilerParams(vmem_limit_bytes=VMEM_LIMIT),
        cost_estimate=HINT,
        name="dense_own" if own else "dense_rest",
    )(seq, ctx, x, *ups, *mats, *vecs, *extra)


def up_grad_kernel(me, nlow, left, right, send, keep, turned, scr):

    @pl.when(pl.program_id(0) == 0)
    def _():
        turned[...] = nlow[...].T

    scr[:, 0:384] = dot(turned[...], left[...])
    scr[:, 384:768] = dot(turned[...], right[...])
    for half, out in ((0, keep), (1, send)):
        for r in range(16):
            emit_24(scr, 0, block_number(half, r) ^ me[0], out, r, 0)


def up_grad(me, nlow, dinn, tokens):
    out = pl.BlockSpec((16, 16, 1152), lambda j, m: (0, 0, j))
    return pl.pallas_call(
        up_grad_kernel,
        grid_spec=pltpu.PrefetchScalarGridSpec(
            num_scalar_prefetch=1,
            grid=(4,),
            in_specs=[
                pl.BlockSpec((tokens, D), lambda j, m: (0, 0)),
                pl.BlockSpec((tokens, 384), lambda j, m: (0, j)),
                pl.BlockSpec((tokens, 384), lambda j, m: (0, j + 4)),
            ],
            out_specs=[out, out],
            scratch_shapes=[pltpu.VMEM((D, tokens), bf16), pltpu.VMEM((D, D), f32)],
        ),
        out_shape=[SDS((16, 16, 4608), bf16)] * 2,
        compiler_params=pltpu.CompilerParams(vmem_limit_bytes=VMEM_LIMIT),
        cost_estimate=HINT,
        name="up_grad",
    )(me, nlow, dinn, dinn)


DOWN_WIDTH = 4608 + 1152 + 128


def down_grad_kernel(me, act, dbr, ctx, datt, vec, send, keep, scr, wo_s):
    j = pl.program_id(0)

    @pl.when(j == 0)
    def _():
        wo_s[...] = dot_tn(ctx[...], datt[...])

    scr[...] = dot_tn(act[...], dbr[...])
    z = j ^ (me[0] >> 3)
    for half, out in ((0, keep), (1, send)):
        for r in range(4):
            near = block_number(half, r) ^ (me[0] & 7)
            d = z * 8 + near
            for g in range(6):
                rows = pl.ds(pl.multiple_of(96 * near + 16 * g, 16), 16)
                out[r, :, D * g : D * (g + 1)] = scr[rows, :].astype(bf16)
            emit_24(wo_s, 0, d, out, r, 4608)
            small = pltpu.roll(vec[0:8, :], lax.rem(D - 24 * d, D), 1)[:, 0:128]
            wide = pltpu.roll(vec[8:16, :], lax.rem(D - 96 * near, D), 1)[:, 0:128]
            out[r, :, 5760:5888] = jnp.concatenate([small, wide], axis=0).astype(bf16)


def down_grad(me, act, dbr, ctx, datt, vec, tokens):
    out = pl.BlockSpec((4, 16, DOWN_WIDTH), lambda j, m: (j, 0, 0))
    tok = pl.BlockSpec((tokens, D), lambda j, m: (0, 0))
    return pl.pallas_call(
        down_grad_kernel,
        grid_spec=pltpu.PrefetchScalarGridSpec(
            num_scalar_prefetch=1,
            grid=(4,),
            in_specs=[
                pl.BlockSpec((tokens, D), lambda j, m: (0, j ^ (m[0] >> 3))),
                tok,
                tok,
                tok,
                pl.BlockSpec((16, D), lambda j, m: (0, 0)),
            ],
            out_specs=[out, out],
            scratch_shapes=[pltpu.VMEM((D, D), f32), pltpu.VMEM((D, D), f32)],
        ),
        out_shape=[SDS((16, 16, DOWN_WIDTH), bf16)] * 2,
        compiler_params=pltpu.CompilerParams(vmem_limit_bytes=VMEM_LIMIT),
        cost_estimate=HINT,
        name="down_grad",
    )(me, act, dbr, ctx, datt, vec)


def backward_pairs(pairs, place, row, length, q_r, k_r, v_r, g_r, lse, first, dq_o, dk_o, dv_o):
    n = slice(0, length)
    bias = mask_column(place, row, length)
    low = low_lanes()
    for p in range(pairs):
        sl = slice(128 * p, 128 * p + 128)
        q2 = scaled(q_r[n, sl])
        k2 = k_r[n, sl]
        g2 = g_r[n, sl]
        scores = dot_nt(stack_heads(k2, low), q2)
        d_probs = dot_nt(stack_heads(v_r[n, sl], low), g2)
        probs_low = []
        d_scores = []
        for h in range(2):
            part = slice(h * length, (h + 1) * length)
            head = 2 * (first + p) + h
            probs = jnp.exp(scores[part, :] + bias - lse[head : head + 1, n])
            d_part = d_probs[part, :]
            centre = jnp.sum(probs * d_part, axis=0, keepdims=True)
            probs_low.append(probs.astype(bf16))
            d_scores.append((probs * (d_part - centre)).astype(bf16))
        dv_o[n, sl] = jnp.where(low, dot(probs_low[0], g2), dot(probs_low[1], g2)).astype(bf16)
        dk_o[n, sl] = jnp.where(low, dot(d_scores[0], q2), dot(d_scores[1], q2)).astype(bf16)
        upper, lower = split_rows(k2.T)
        turned = dot(upper, d_scores[0]) + dot(lower, d_scores[1])
        dq_o[n, sl] = (turned * 0.125).T.astype(bf16)


def first_row_kernel(s0, s1, s2, s3, q_r, k_r, v_r, g_r, lse, dr1, wq, wk, wv, dq, dk, dv, ig_own, ig_other, *, length):
    backward_pairs(PAIRS, (s0, s1, s2, s3), 0, length, q_r, k_r, v_r, g_r, lse, 0, dq, dk, dv)
    ig = dr1[...] + dot_nt(dq[...], wq[...]) + dot_nt(dk[...], wk[...]) + dot_nt(dv[...], wv[...])
    ig = ig.astype(bf16)
    ig_own[...] = ig[: length // 2]
    ig_other[...] = ig[length // 2 :]


def first_row_backward(place, q, k, v, dctx, lse, dr1, weights, length):
    tok = pl.BlockSpec((length, D), lambda i: (0, 0))
    half = pl.BlockSpec((length // 2, D), lambda i: (0, 0))
    full = pl.BlockSpec((D, D), lambda i: (0, 0))
    return pl.pallas_call(
        functools.partial(first_row_kernel, length=length),
        grid=(1,),
        in_specs=[pl.BlockSpec(memory_space=pltpu.SMEM)] * 4
        + [tok] * 4
        + [pl.BlockSpec((16, 512), lambda i: (0, 0)), tok]
        + [full] * 3,
        out_specs=[tok] * 3 + [half] * 2,
        out_shape=[SDS((length, D), bf16)] * 3 + [SDS((length // 2, D), bf16)] * 2,
        compiler_params=pltpu.CompilerParams(vmem_limit_bytes=VMEM_LIMIT),
        cost_estimate=HINT,
        name="back_first",
    )(*place, q, k, v, dctx, lse, dr1, *weights)


def group_kernel(me, s0, s1, s2, s3, q_r, k_r, v_r, g_r, lse, dq0, dk0, dv0, xt, *rest, lengths, pairs, first, final):
    if final:
        bg_before, rest = rest[0], rest[1:]
    dq, dk, dv, send, keep, bg, every, dw = rest
    width = 128 * pairs
    long, mid = lengths
    step = pl.program_id(0)

    @pl.when(step == 0)
    def _():
        backward_pairs(pairs, (s0, s1, s2, s3), 1, long, q_r, k_r, v_r, g_r, lse, first, dq, dk, dv)
        for a, (old, new) in enumerate(((dq0, dq), (dk0, dk), (dv0, dv))):
            lanes = slice(a * width, (a + 1) * width)
            every[0:long, lanes] = old[...]
            every[long : 2 * long, lanes] = new[...]

    @pl.when(step == 1)
    def _():
        backward_pairs(pairs, (s0, s1, s2, s3), 2, mid, q_r, k_r, v_r, g_r, lse, first, dq, dk, dv)
        for a, new in enumerate((dq, dk, dv)):
            every[2 * long : 2 * long + mid, a * width : (a + 1) * width] = new[0:mid, :]
        count = 2 * long + mid
        for c in range(3 * width // D):
            dw[:, D * c : D * (c + 1)] = dot(xt[:, 0:count], every[:, D * c : D * (c + 1)])
        bg[...] = jnp.zeros_like(bg)
        bg[0:1, :] = column_sum(every[:, 0:width])
        bg[1:2, :] = column_sum(every[:, 2 * width : 3 * width])
        if final:
            sums = jnp.concatenate([bg_before[...], bg[...]], axis=1)
        for half, out in ((0, keep), (1, send)):
            for r in range(16):
                d = block_number(half, r) ^ me[0]
                for c in range(3 * width // D):
                    emit_24(dw, D * c, d, out, r, 1152 * c)
                if final:
                    small = pltpu.roll(sums, lax.rem(D - 24 * d, D), 1)[:, 0:128]
                    small = jnp.concatenate([small, small], axis=0)
                    out[r, :, 1152 * (3 * width // D) :] = small.astype(bf16)


def group_backward(me, place, q, k, v, dctx, lse, before, xt, lengths, pairs, first, bg_before):
    final = bg_before is not None
    width = 128 * pairs
    column = first // pairs
    long, mid = lengths
    count = 2 * long + mid
    tok = pl.BlockSpec((long, width), lambda i, *_: (1 + i, column))
    old = pl.BlockSpec((long, width), lambda i, *_: (0, column))
    new = pl.BlockSpec((long, width), lambda i, *_: (i, 0))
    size = 3 * width * 24 // 16 + (128 if final else 0)
    out = pl.BlockSpec((16, 16, size), lambda i, *_: (0, 0, 0))
    extra = [bg_before] if final else []
    specs = [pl.BlockSpec(a.shape, lambda i, *_: (0, 0)) for a in extra]
    return pl.pallas_call(
        functools.partial(group_kernel, lengths=lengths, pairs=pairs, first=first, final=final),
        grid_spec=pltpu.PrefetchScalarGridSpec(
            num_scalar_prefetch=5,
            grid=(2,),
            in_specs=[tok] * 4
            + [pl.BlockSpec((16, 512), lambda i, *_: (1 + i, 0))]
            + [old] * 3
            + [pl.BlockSpec(xt.shape, lambda i, *_: (0, 0))]
            + specs,
            out_specs=[new] * 3 + [out, out, pl.BlockSpec((8, width), lambda i, *_: (0, 0))],
            scratch_shapes=[pltpu.VMEM((count, 3 * width), bf16), pltpu.VMEM((D, 3 * width), f32)],
        ),
        out_shape=[SDS((2 * long, width), bf16)] * 3
        + [SDS((16, 16, size), bf16)] * 2
        + [SDS((8, width), f32)],
        compiler_params=pltpu.CompilerParams(vmem_limit_bytes=VMEM_LIMIT),
        cost_estimate=HINT,
        name=f"back_group_{first}",
    )(me, *place, q, k, v, dctx, lse, *before, xt, *extra)


def input_grad_kernel(dr1, *rest, lengths, lanes):
    groups = len(lanes)
    blocks, (wq, wk, wv), (own, other) = rest[: 3 * groups], rest[3 * groups : 3 * groups + 3], rest[-2:]
    long, mid = lengths
    n = slice(0, long + mid)
    total = dr1[...]
    for a, w in enumerate((wq, wk, wv)):
        for g, (low, high) in enumerate(lanes):
            total = total + dot_nt(blocks[3 * g + a][n, :], w[:, low:high])
    total = total.astype(bf16)
    own[0 : long // 2, :] = total[0 : long // 2]
    other[0 : long // 2, :] = total[long // 2 : long]
    own[long // 2 :, :] = total[long : long + mid // 2]
    other[long // 2 :, :] = total[long + mid // 2 :]


def input_grad(dr1, groups, lanes, weights, lengths):
    long, mid = lengths
    flat = [a for g in groups for a in g]
    whole = lambda a: pl.BlockSpec(a.shape, lambda i: (0, 0))
    side = pl.BlockSpec(((long + mid) // 2, D), lambda i: (0, 0))
    return pl.pallas_call(
        functools.partial(input_grad_kernel, lengths=lengths, lanes=lanes),
        grid=(1,),
        in_specs=[pl.BlockSpec((pl.Element(long + mid), pl.Element(D)), lambda i: (long, 0))]
        + [whole(a) for a in flat + list(weights)],
        out_specs=[side, side],
        out_shape=[SDS(((long + mid) // 2, D), bf16)] * 2,
        compiler_params=pltpu.CompilerParams(vmem_limit_bytes=VMEM_LIMIT),
        cost_estimate=HINT,
        name="input_grad",
    )(dr1, *flat, *weights)


def swap_seq(v):
    return lax.ppermute(v, "seq", [(0, 1), (1, 0)])


def swap_dp(v, bit):
    n = lax.axis_size("dp")
    return lax.ppermute(v, "dp", [(i, i ^ bit) for i in range(n)])


STEPS = {"x": (3, swap_seq), "y": (2, lambda v: swap_dp(v, 2)), "z": (1, lambda v: swap_dp(v, 4)), "w": (0, lambda v: swap_dp(v, 8))}


def later(value, *others):
    return lax.optimization_barrier((value, *others))[0]


class Halving:
    def __init__(self, groups, order):
        self.groups = groups
        self.order = order

    def total(self, groups):
        sums = [functools.reduce(lambda a, b: a + b, [p.astype(f32) for p in g]) for g in groups]
        return jnp.concatenate(sums, axis=5)

    def send(self):
        axis, self.swap = STEPS[self.order[0]]
        self.order = self.order[1:]
        half = lambda i: [[lax.index_in_dim(p, i, axis, keepdims=True) for p in g] for g in self.groups]
        self.outgoing = self.total(half(1)).astype(bf16)
        self.groups = half(0)
        return self

    def receive(self, after=None):
        received = self.swap(self.outgoing)
        if after is not None:
            received = later(received, after)
        low = 0
        for g in self.groups:
            width = g[0].shape[5]
            g.append(lax.slice_in_dim(received, low, low + width, axis=5))
            low += width
        return self

    def result(self):
        return self.total(self.groups).reshape(16, -1)


def join(*sums):
    return Halving([g for h in sums for g in h.groups], sums[0].order)


def across_cores(pair, after, widths, orders):
    send, keep = pair
    received = swap_dp(send, 1)
    if after is not None:
        received = later(received, after)
    both = [v.reshape(2, 2, 2, 2, 16, -1) for v in (keep, received)]
    parts = []
    low = 0
    for width, order in zip(widths, orders):
        parts.append(Halving([[lax.slice_in_dim(v, low, low + width, axis=5) for v in both]], order).send())
        low += width
    return parts


def rows_24(block):
    return block.reshape(2, 8, 3, 384).transpose(2, 1, 0, 3).reshape(24, D)


def unpack_up(block):
    return block.reshape(2, 8, 4, 3, 384).transpose(3, 1, 0, 2, 4).reshape(24, FF)


def unpack_down(block):
    return block[:, :4608].reshape(16, 6, D).transpose(1, 0, 2).reshape(96, D), rows_24(block[:, 4608:5760])


def unpack_qkv(blocks):
    wide, narrow = blocks
    left = jnp.concatenate([rows_24(wide[:, :1152]), rows_24(wide[:, 1152:])], axis=1)
    right = rows_24(narrow[:, :1152])
    return [
        jnp.concatenate([left[:, 512 * a : 512 * (a + 1)], right[:, 256 * a : 256 * (a + 1)]], axis=1) for a in range(3)
    ]


def finish_sums(up, down, qkv, me):
    w_up = unpack_up(up)
    w_down, w_out = unpack_down(down)
    w_query, w_key, w_value = unpack_qkv(qkv)
    vec = down[:8, 5760:5784]
    b_up = lax.dynamic_slice(down, (8 + (me >> 3), 5760), (1, 96))[0]
    bq, bv = qkv[1][0, 1152:1176], qkv[1][1, 1152:1176]
    return w_query, bq, w_key, w_value, bv, w_out, vec, w_up, b_up, w_down


def reduce_plain(up_pair, down_pair, qkv_pairs, vec, bg):
    def ordered(pair):
        send, keep = pair
        both = jnp.stack([keep.reshape(8, 2, 16, -1), send.reshape(8, 2, 16, -1)], axis=1)
        return both.reshape(BLOCKS, 16, -1).astype(f32)

    scatter = lambda v: lax.psum_scatter(v, ("dp", "seq"), scatter_dimension=0, tiled=True)
    w_up = jax.vmap(unpack_up)(ordered(up_pair)).reshape(D, FF)
    w_down, w_out = (a.reshape(-1, D) for a in jax.vmap(unpack_down)(ordered(down_pair)))
    qkv = [a.reshape(D, D) for a in jax.vmap(unpack_qkv)([ordered(p) for p in qkv_pairs])]
    small = [scatter(vec[i]) for i in range(6)]
    return (
        scatter(qkv[0]), scatter(bg[0]), scatter(qkv[1]), scatter(qkv[2]), scatter(bg[1]), scatter(w_out),
        small, scatter(w_up), scatter(vec[8:12].reshape(FF)), scatter(w_down),
    )


def per_device(
    tokens_short, tokens_middle, tokens_long, length_short, length_middle, length_long,
    query_weight, query_bias, key_weight, value_weight, value_bias, output_weight, output_bias,
    attention_gain, attention_shift, up_weight, up_bias, down_weight, down_bias, output_gain, output_shift,
    upstream_short, upstream_middle, upstream_long,
):
    seq = lax.axis_index("seq")
    first = seq == 0
    device = (lax.axis_index("dp") * 2 + seq).astype(jnp.int32)
    fast = lax.axis_size("dp") * lax.axis_size("seq") == BLOCKS
    me = device if fast else jnp.int32(0)
    me_ref = me.reshape(1)
    count, half, _ = tokens_long.shape
    mine = count // 2
    mid = tokens_middle.shape[1]
    short = tokens_short.shape[1]
    lengths = (2 * half,) * mine + (2 * mid,)
    tokens = sum(lengths)
    rows = 2 * half * (mine + 1)

    def own_rows(v):
        return lax.dynamic_slice_in_dim(v, mine * seq, mine, 0)

    def other_rows(v):
        return lax.dynamic_slice_in_dim(v, mine * (1 - seq), mine, 0)

    def middle_rows(middle, low):
        low = jnp.pad(low[0], ((0, mid - short), (0, 0)))
        return jnp.where(first, middle[0], low), jnp.where(first, low, middle[0])

    x_mid, x_mid_out = middle_rows(tokens_middle, tokens_short)
    x_mid_in = swap_seq(x_mid_out)
    x_own, x_out = own_rows(tokens_long), other_rows(tokens_long)
    x_in = [swap_seq(x_out[i]) for i in range(mine)]
    u_mid, u_mid_out = middle_rows(upstream_middle, upstream_short)
    u_out = jnp.concatenate([other_rows(upstream_long).reshape(mine * half, D), u_mid_out], axis=0)

    place = (seq.astype(jnp.int32).reshape(1), length_short, length_middle, length_long)
    qkv = [query_weight, key_weight, value_weight]
    projections = qkv + [query_bias, value_bias]
    chain = attention_forward(place, x_mid, x_mid_in, projections, mine, 2 * mid, mine * half // mid, None, rows)
    for i in range(mine):
        chain = attention_forward(place, x_own[i], x_in[i], projections, i, 2 * half, i, chain, rows)
    x, q, k, v, ctx, lse, xt = chain
    u_in = swap_seq(later(u_out, lse))

    mats = [output_weight, up_weight, down_weight]
    dense = functools.partial(
        dense_steps, place[0], ctx, x, tokens=tokens, rows=rows, mats=mats,
        vecs=[up_bias, output_bias, attention_gain, attention_shift, down_bias, output_gain, output_shift],
    )
    res_long, *before = dense(ups=[upstream_long], before=None)
    res_other, res_mid, act, dinn, nlow, dbr, datt, dr1, dctx, vec = dense(ups=[u_in, u_in, u_mid], before=before)

    def give_back(own, got):
        body = mine * half
        here, there = (a[:body].reshape(mine, half, D) for a in (own, got))
        long = jnp.concatenate([jnp.where(first, here, there), jnp.where(first, there, here)], axis=0)
        low, middle = jnp.where(first, got[body:], own[body:]), jnp.where(first, own[body:], got[body:])
        return low[None, :short], middle[None], long

    body = half
    first_got = swap_seq(res_other[:body])
    up_pair = up_grad(me_ref, nlow, dinn, tokens)
    first_got = later(first_got, up_pair[0])
    rest_got = swap_seq(later(res_other[body:], first_got))
    down_pair = down_grad(later(me_ref, up_pair[0]), act, dbr, ctx, datt, vec, tokens)

    def ready(value, *sums):
        return later(value, *[h.outgoing for h in sums])

    after_sums = ready if fast else lambda value, *sums: value
    at = lambda before, *sums: (after_sums(later(place[0], before), *sums), *place[1:])
    up = down = wide_sum = []
    if fast:
        up = across_cores(up_pair, down_pair[0], [2304, 2304], ["zxyw", "yxzw"])
    *before, ig_own, ig_other = first_row_backward(
        at(down_pair[0], *up), q, k, v, dctx, lse, dr1, qkv, 2 * half
    )
    if fast:
        up = [h.receive(ig_own).send() for h in up]
        down = across_cores(down_pair, ig_own, [3072, 2816], ["zyxw", "yzxw"])
    rest_got = later(rest_got, ig_own)
    later_rows = (2 * half, 2 * mid)
    *wide, send, keep, bg = group_backward(
        me_ref, at(ig_own, *up, *down), q, k, v, dctx, lse, before, xt, later_rows, 4, 0, None
    )
    wide_pair = (send, keep)
    if fast:
        up = [h.receive(bg).send() for h in up]
        down = [h.receive(bg).send() for h in down]
    ig_got = [swap_seq(later(ig_other, bg))]
    *narrow, send, keep, bg_last = group_backward(
        me_ref, at(bg, *up, *down), q, k, v, dctx, lse, before, xt, later_rows, 2, 4, bg
    )
    narrow_pair = (send, keep)
    ig_got[0] = later(ig_got[0], bg_last)
    if fast:
        up = [join(*[h.receive(bg_last) for h in up]).send()]
        down = [join(*[h.receive(bg_last) for h in down]).send()]
        wide_sum = across_cores(wide_pair, bg_last, [1152, 1152], ["yzxw", "zyxw"])
    own, other = input_grad(
        after_sums(later(dr1, ig_got[0]), *up, *down, *wide_sum), [wide, narrow], [(0, 512), (512, 768)], qkv, later_rows
    )
    ig_got.append(swap_seq(other))
    results = give_back(later(jnp.concatenate([res_long, res_mid], axis=0), own), jnp.concatenate([first_got, rest_got], axis=0))
    if fast:
        up_block = up[0].receive(own).result()
        down = down[0].receive(own).send()
        wide_sum = [h.receive(own).send() for h in wide_sum]
        (narrow_sum,) = across_cores(narrow_pair, own, [1280], ["yzxw"])
        wide_sum = join(*[h.receive() for h in wide_sum]).send()
        narrow_sum.receive().send()
        down_block = down.receive().result()
        narrow_sum.receive().send()
        last = join(wide_sum.receive(), narrow_sum.receive()).send().receive().result()
        done = finish_sums(up_block, down_block, [last[:, :2304], last[:, 2304:]], me)
    else:
        done = reduce_plain(up_pair, down_pair, [wide_pair, narrow_pair], vec, jnp.concatenate([bg, bg_last], axis=1))
    input_grads = give_back(jnp.concatenate([ig_own, own], axis=0), jnp.concatenate(ig_got, axis=0))
    w_query, bq, w_key, w_value, bv, w_out, small, w_up, b_up, w_down = done
    return (
        *results, *input_grads,
        w_query, bq, w_key, w_value, bv, w_out, small[5], small[3], small[4],
        w_up, b_up, w_down, small[2], small[0], small[1],
    )


def solution(mesh):
    tokens = P("dp", "seq", None)
    wide = P(("dp", "seq"), None)
    flat = P(("dp", "seq"))
    in_specs = (tokens,) * 3 + (P("dp"),) * 3 + (P(),) * 15 + (tokens,) * 3
    out_specs = (tokens,) * 6 + (
        wide, flat, wide, wide, flat, wide, flat, flat, flat, wide, flat, wide, flat, flat, flat,
    )
    return jax.shard_map(per_device, mesh=mesh, in_specs=in_specs, out_specs=out_specs, check_vma=False)
```

```python
import functools

import jax
import jax.numpy as jnp
from jax import lax
from jax.experimental import pallas as pl
from jax.experimental.pallas import tpu as pltpu
from jax.sharding import PartitionSpec as P

D = 768
FF = 3072
HEADS = 12
PAIRS = HEADS // 2
EPS = 1e-12
NEG = -1e30
SHORT_HALF = 64
BLOCKS = 32
VMEM_LIMIT = 60 * 2**20

bf16 = jnp.bfloat16
f32 = jnp.float32
SDS = jax.ShapeDtypeStruct
ANY = pl.BlockSpec(memory_space=pl.ANY)
LONG = pl.CostEstimate(flops=4 * 10**10, bytes_accessed=10**8, transcendentals=0)


def dot(a, b):
    return lax.dot_general(a, b, (((1,), (0,)), ((), ())), preferred_element_type=f32)


def dot_nt(a, b):
    return lax.dot_general(a, b, (((1,), (1,)), ((), ())), preferred_element_type=f32)


def dot_tn(a, b):
    return lax.dot_general(a, b, (((0,), (0,)), ((), ())), preferred_element_type=f32)


def wide(vector):
    return vector[...].reshape(1, -1)


def mean(v):
    return jnp.mean(v, axis=-1, keepdims=True)


def column_sum(v):
    return jnp.sum(v.astype(f32), axis=0, keepdims=True)


A1, A2, A3, A4, A5 = 0.254829592, -0.284496736, 1.421413741, -1.453152027, 1.061405429
P_SCALED = 0.3275911 * 0.7071067811865476
INV_SQRT_2PI = 0.3989422804014327


def gelu_and_slope(v):
    t = 1.0 / (1.0 + P_SCALED * jnp.abs(v))
    e = jnp.exp(v * v * -0.5)
    tail = t * (A1 + t * (A2 + t * (A3 + t * (A4 + t * A5)))) * (0.5 * e)
    cdf = jnp.where(v < 0, tail, 1.0 - tail)
    return v * cdf, cdf + v * (e * INV_SQRT_2PI)


def mask_column(place, row, length):
    seq, short, middle, long = place
    half = length // 2
    mine = long.shape[0] // 2
    s = seq[0]
    if row < mine:
        count, valid, own, other = long[mine * s + row], half, half * s, half * (1 - s)
    else:
        is_first = s == 0
        count = jnp.where(is_first, middle[0], short[0])
        valid = jnp.where(is_first, half, SHORT_HALF)
        own, other = jnp.where(is_first, 0, SHORT_HALF), jnp.where(is_first, half, 0)
    i = lax.broadcasted_iota(jnp.int32, (length, 1), 0)
    inner = jnp.where(i < half, i, i - half)
    live = (inner + jnp.where(i < half, own, other) < count) & (inner < valid)
    return jnp.where(live, 0.0, NEG).astype(f32)


def low_lanes():
    return lax.broadcasted_iota(jnp.int32, (1, 128), 1) < 64


def stack_heads(pair, low):
    zero = jnp.zeros_like(pair)
    return jnp.concatenate([jnp.where(low, pair, zero), jnp.where(low, zero, pair)], axis=0)


def split_rows(pair_t):
    row = lax.broadcasted_iota(jnp.int32, (128, 1), 0) < 64
    zero = jnp.zeros_like(pair_t)
    return jnp.where(row, pair_t, zero), jnp.where(row, zero, pair_t)


def scaled(q):
    return (q.astype(f32) * 0.125).astype(bf16)


def emit_24(scr, lane, d, out, r, base):
    for g in range(3):
        rows = pl.ds(pl.multiple_of(24 * d + 8 * g, 8), 8)
        both = jnp.concatenate(
            [scr[rows, lane : lane + 384], scr[rows, lane + 384 : lane + 768]], axis=0
        )
        out[r, :, base + 384 * g : base + 384 * (g + 1)] = both.astype(bf16)


def block_number(half, r):
    return ((r >> 1) << 2) | (half << 1) | (r & 1)


def forward_kernel(s0, s1, s2, s3, xl, xr, wq, wk, wv, bq, bv, *rest, length, row, chained):
    x_o, q_o, k_o, v_o, c_o, lse_o, xt_o = rest[7:] if chained else rest
    x = jnp.concatenate([xl[...], xr[...]], axis=0)
    x_o[...] = x
    xt_o[...] = x.T
    q_o[...] = (dot(x, wq[...]) + wide(bq)).astype(bf16)
    k_o[...] = dot(x, wk[...]).astype(bf16)
    v_o[...] = (dot(x, wv[...]) + wide(bv)).astype(bf16)
    bias = mask_column((s0, s1, s2, s3), row, length)
    low = low_lanes()
    row_low = lax.broadcasted_iota(jnp.int32, (128, 1), 0) < 64
    for p in range(PAIRS):
        sl = slice(128 * p, 128 * p + 128)
        scores = dot_nt(stack_heads(k_o[:, sl], low), scaled(q_o[:, sl]))
        parts = []
        inverse = []
        for h in range(2):
            s = scores[h * length : (h + 1) * length, :] + bias
            top = jnp.max(s, axis=0, keepdims=True)
            raised = jnp.exp(s - top)
            total = jnp.sum(raised, axis=0, keepdims=True)
            lse_o[2 * p + h : 2 * p + h + 1, 0:length] = top + jnp.log(total)
            parts.append(raised.astype(bf16))
            inverse.append(1.0 / total)
        upper, lower = split_rows(v_o[:, sl].T)
        context = dot(upper, parts[0]) + dot(lower, parts[1])
        context = context * jnp.where(row_low, inverse[0], inverse[1])
        c_o[:, sl] = context.T.astype(bf16)


def attention_forward(place, own, other, weights, row, length, block, chain, rows):
    half = pl.BlockSpec((length // 2, D), lambda i: (0, 0))
    full = lambda a: pl.BlockSpec(a.shape, lambda i: (0,) * a.ndim)
    tok = pl.BlockSpec((length, D), lambda i: (block, 0))
    lse = pl.BlockSpec((16, 512), lambda i: (row, 0))
    turned = pl.BlockSpec((D, length), lambda i: (0, block))
    chained = chain is not None
    extra = list(chain) if chained else []
    return pl.pallas_call(
        functools.partial(forward_kernel, length=length, row=row, chained=chained),
        grid=(1,),
        in_specs=[pl.BlockSpec(memory_space=pltpu.SMEM)] * 4
        + [half, half]
        + [full(w) for w in weights]
        + [ANY] * len(extra),
        out_specs=[tok] * 5 + [lse, turned],
        out_shape=[SDS((rows, D), bf16)] * 5 + [SDS((48, 512), f32), SDS((D, rows), bf16)],
        input_output_aliases={11 + i: i for i in range(7)} if chained else {},
        compiler_params=pltpu.CompilerParams(vmem_limit_bytes=VMEM_LIMIT),
        cost_estimate=LONG,
        name=f"attend_{row}",
    )(*place, own, other, *weights, *extra)


def drop_first(kernel):
    return lambda _, *refs, **options: kernel(*refs, **options)


def dense_kernel(*refs, chunks, own):
    ctx, x = refs[0], refs[1]
    step = pl.program_id(0)
    last = step == pl.num_programs(0) - 1
    if own:
        up_refs, refs = refs[2:3], refs[3:]
        up = up_refs[0][0]
    else:
        up_refs, refs = refs[2:5], refs[5:]
        up = jnp.concatenate([jnp.where(last, up_refs[2][...], up_refs[0][...]), up_refs[1][...]], axis=0)
    wo, wup, wdn, bup, bo, g1, s1, bdn, g2, s2 = refs[:10]
    bup, bo, g1, s1, bdn, g2, s2 = (wide(v) for v in (bup, bo, g1, s1, bdn, g2, s2))
    if own:
        res_own, act, dinn, nlow_o, dbr, datt, dr1_o, dctx, vec, slope_s = refs[10:]
    else:
        vec_in = refs[10]
        res_other, res_mid, act, dinn, nlow_o, dbr, datt, dr1_o, dctx, vec, slope_s = refs[18:]

    @pl.when(step == 0)
    def _():
        vec[...] = jnp.zeros_like(vec) if own else vec_in[...]

    r1 = x[...].astype(f32) + dot(ctx[...], wo[...]) + bo
    c1 = r1 - mean(r1)
    rs1 = lax.rsqrt(mean(c1 * c1) + EPS)
    n1 = c1 * rs1
    normed = n1 * g1 + s1
    nlow = normed.astype(bf16)
    nlow_o[...] = nlow
    acc = normed + bdn
    width = FF // chunks
    for j in range(chunks):
        sl = slice(j * width, (j + 1) * width)
        value, slope = gelu_and_slope(dot(nlow, wup[:, sl]) + bup[:, sl])
        value = value.astype(bf16)
        act[:, sl] = value
        slope_s[:, sl] = slope
        acc = acc + dot(value, wdn[sl, :])
    c2 = acc - mean(acc)
    rs2 = lax.rsqrt(mean(c2 * c2) + EPS)
    n2 = c2 * rs2
    result = (n2 * g2 + s2).astype(bf16)
    if own:
        res_own[0] = result
    else:
        size = result.shape[0]

        @pl.when(jnp.logical_not(last))
        def _():
            res_other[pl.ds(pl.multiple_of(step * size, size), size), :] = result

        @pl.when(last)
        def _():
            res_mid[...] = result[: size // 2]
            res_other[res_other.shape[0] - size // 2 :, :] = result[size // 2 :]

    upstream = up.astype(f32)
    u = upstream * g2
    dr2 = (u - mean(u) - n2 * mean(u * n2)) * rs2
    branch = dr2.astype(bf16)
    dbr[...] = branch
    vec[0:1, :] += column_sum(upstream * n2)
    vec[1:2, :] += column_sum(upstream)
    vec[2:3, :] += column_sum(branch)
    acc = dr2
    for j in range(chunks):
        sl = slice(j * width, (j + 1) * width)
        d_inner = (dot_nt(branch, wdn[sl, :]) * slope_s[:, sl]).astype(bf16)
        dinn[:, sl] = d_inner
        vec[8 + j : 9 + j, :] += column_sum(d_inner)
        acc = acc + dot_nt(d_inner, wup[:, sl])
    vec[3:4, :] += column_sum(acc * n1)
    vec[4:5, :] += column_sum(acc)
    u1 = acc * g1
    d1 = (u1 - mean(u1) - n1 * mean(u1 * n1)) * rs1
    d_attn = d1.astype(bf16)
    datt[...] = d_attn
    dr1_o[...] = d1
    vec[5:6, :] += column_sum(d_attn)
    dctx[...] = dot_nt(d_attn, wo[...]).astype(bf16)


def dense_steps(seq, ctx, x, ups, mats, vecs, tokens, rows, before):
    tile = 256
    half = tile // 2
    mine = tokens // tile // 2
    own = before is None
    full = lambda a: pl.BlockSpec(a.shape, lambda i, s: (0,) * a.ndim, pipeline_mode=pl.Buffered(1))
    whole = lambda n: pl.BlockSpec((n, D), lambda i, s: (0, 0))
    if own:
        place = lambda i: 2 * i
        steps = mine
        up_specs = [pl.BlockSpec((1, tile, D), lambda i, s: (s[0] * mine + i, 0, 0))]
        res_specs = [pl.BlockSpec((1, tile, D), lambda i, s: (s[0] * mine + i, 0, 0))]
        res_shapes = [SDS((2 * mine, tile, D), bf16)]
        extra, extra_specs, aliases = [], [], {}
    else:
        place = lambda i: jnp.minimum(2 * i + 1, 2 * mine)
        steps = mine + 1
        up_specs = [
            pl.BlockSpec((half, D), lambda i, s: (jnp.minimum(2 * i, 2 * mine - 2), 0)),
            pl.BlockSpec((half, D), lambda i, s: (jnp.minimum(2 * i + 1, 2 * mine), 0)),
            whole(half),
        ]
        res_specs = [whole(tokens // 2), whole(half)]
        res_shapes = [SDS((tokens // 2, D), bf16), SDS((half, D), bf16)]
        *arrays, vec = before
        extra = [vec] + arrays
        extra_specs = [whole(16)] + [ANY] * len(arrays)
        first = 1 + 2 + len(ups) + len(mats) + len(vecs) + 1
        aliases = {first + i: 2 + i for i in range(len(arrays))}
    tok = pl.BlockSpec((tile, D), lambda i, s: (place(i), 0))
    ffs = pl.BlockSpec((tile, FF), lambda i, s: (place(i), 0))
    return pl.pallas_call(
        functools.partial(drop_first(dense_kernel), chunks=4, own=own),
        grid_spec=pltpu.PrefetchScalarGridSpec(
            num_scalar_prefetch=1,
            grid=(steps,),
            in_specs=[tok, tok] + up_specs + [full(a) for a in mats + vecs] + extra_specs,
            out_specs=res_specs + [ffs, ffs] + [tok] * 5 + [whole(16)],
            scratch_shapes=[pltpu.VMEM((tile, FF), f32)],
        ),
        out_shape=res_shapes
        + [SDS((tokens, FF), bf16)] * 2
        + [SDS((tokens, D), bf16)] * 3
        + [SDS((rows, D), f32), SDS((rows, D), bf16), SDS((16, D), f32)],
        input_output_aliases=aliases,
        compiler_params=pltpu.CompilerParams(vmem_limit_bytes=VMEM_LIMIT),
        cost_estimate=LONG,
        name="dense_own" if own else "dense_rest",
    )(seq, ctx, x, *ups, *mats, *vecs, *extra)


def up_grad_kernel(me, nlow, left, right, send, keep, turned, scr):

    @pl.when(pl.program_id(0) == 0)
    def _():
        turned[...] = nlow[...].T

    scr[:, 0:384] = dot(turned[...], left[...])
    scr[:, 384:768] = dot(turned[...], right[...])
    for half, out in ((0, keep), (1, send)):
        for r in range(16):
            emit_24(scr, 0, block_number(half, r) ^ me[0], out, r, 0)


def up_grad(me, nlow, dinn, tokens):
    out = pl.BlockSpec((16, 16, 1152), lambda j, m: (0, 0, j))
    return pl.pallas_call(
        up_grad_kernel,
        grid_spec=pltpu.PrefetchScalarGridSpec(
            num_scalar_prefetch=1,
            grid=(4,),
            in_specs=[
                pl.BlockSpec((tokens, D), lambda j, m: (0, 0)),
                pl.BlockSpec((tokens, 384), lambda j, m: (0, j)),
                pl.BlockSpec((tokens, 384), lambda j, m: (0, j + 4)),
            ],
            out_specs=[out, out],
            scratch_shapes=[pltpu.VMEM((D, tokens), bf16), pltpu.VMEM((D, D), f32)],
        ),
        out_shape=[SDS((16, 16, 4608), bf16)] * 2,
        compiler_params=pltpu.CompilerParams(vmem_limit_bytes=VMEM_LIMIT),
        cost_estimate=LONG,
        name="up_grad",
    )(me, nlow, dinn, dinn)


DOWN_WIDTH = 4608 + 1152 + 128


def down_grad_kernel(me, act, dbr, ctx, datt, vec, send, keep, scr, wo_s):
    j = pl.program_id(0)

    @pl.when(j == 0)
    def _():
        wo_s[...] = dot_tn(ctx[...], datt[...])

    scr[...] = dot_tn(act[...], dbr[...])
    z = j ^ (me[0] >> 3)
    for half, out in ((0, keep), (1, send)):
        for r in range(4):
            near = block_number(half, r) ^ (me[0] & 7)
            d = z * 8 + near
            for g in range(6):
                rows = pl.ds(pl.multiple_of(96 * near + 16 * g, 16), 16)
                out[r, :, D * g : D * (g + 1)] = scr[rows, :].astype(bf16)
            emit_24(wo_s, 0, d, out, r, 4608)
            small = pltpu.roll(vec[0:8, :], lax.rem(D - 24 * d, D), 1)[:, 0:128]
            wide = pltpu.roll(vec[8:16, :], lax.rem(D - 96 * near, D), 1)[:, 0:128]
            out[r, :, 5760:5888] = jnp.concatenate([small, wide], axis=0).astype(bf16)


def down_grad(me, act, dbr, ctx, datt, vec, tokens):
    out = pl.BlockSpec((4, 16, DOWN_WIDTH), lambda j, m: (j, 0, 0))
    tok = pl.BlockSpec((tokens, D), lambda j, m: (0, 0))
    return pl.pallas_call(
        down_grad_kernel,
        grid_spec=pltpu.PrefetchScalarGridSpec(
            num_scalar_prefetch=1,
            grid=(4,),
            in_specs=[
                pl.BlockSpec((tokens, D), lambda j, m: (0, j ^ (m[0] >> 3))),
                tok,
                tok,
                tok,
                pl.BlockSpec((16, D), lambda j, m: (0, 0)),
            ],
            out_specs=[out, out],
            scratch_shapes=[pltpu.VMEM((D, D), f32), pltpu.VMEM((D, D), f32)],
        ),
        out_shape=[SDS((16, 16, DOWN_WIDTH), bf16)] * 2,
        compiler_params=pltpu.CompilerParams(vmem_limit_bytes=VMEM_LIMIT),
        cost_estimate=LONG,
        name="down_grad",
    )(me, act, dbr, ctx, datt, vec)


def backward_pairs(pairs, place, row, length, q_r, k_r, v_r, g_r, lse, first, dq_o, dk_o, dv_o):
    n = slice(0, length)
    bias = mask_column(place, row, length)
    low = low_lanes()
    for p in range(pairs):
        sl = slice(128 * p, 128 * p + 128)
        q2 = scaled(q_r[n, sl])
        k2 = k_r[n, sl]
        g2 = g_r[n, sl]
        scores = dot_nt(stack_heads(k2, low), q2)
        d_probs = dot_nt(stack_heads(v_r[n, sl], low), g2)
        probs_low = []
        d_scores = []
        for h in range(2):
            part = slice(h * length, (h + 1) * length)
            head = 2 * (first + p) + h
            probs = jnp.exp(scores[part, :] + bias - lse[head : head + 1, n])
            d_part = d_probs[part, :]
            centre = jnp.sum(probs * d_part, axis=0, keepdims=True)
            probs_low.append(probs.astype(bf16))
            d_scores.append((probs * (d_part - centre)).astype(bf16))
        dv_o[n, sl] = jnp.where(low, dot(probs_low[0], g2), dot(probs_low[1], g2)).astype(bf16)
        dk_o[n, sl] = jnp.where(low, dot(d_scores[0], q2), dot(d_scores[1], q2)).astype(bf16)
        upper, lower = split_rows(k2.T)
        turned = dot(upper, d_scores[0]) + dot(lower, d_scores[1])
        dq_o[n, sl] = (turned * 0.125).T.astype(bf16)


def first_row_kernel(s0, s1, s2, s3, q_r, k_r, v_r, g_r, lse, dr1, wq, wk, wv, dq, dk, dv, ig_own, ig_other, *, length):
    backward_pairs(PAIRS, (s0, s1, s2, s3), 0, length, q_r, k_r, v_r, g_r, lse, 0, dq, dk, dv)
    ig = dr1[...] + dot_nt(dq[...], wq[...]) + dot_nt(dk[...], wk[...]) + dot_nt(dv[...], wv[...])
    ig = ig.astype(bf16)
    ig_own[0] = ig[: length // 2]
    ig_other[...] = ig[length // 2 :]


def first_row_backward(place, q, k, v, dctx, lse, dr1, weights, length):
    tok = pl.BlockSpec((length, D), lambda i, *_: (0, 0))
    half = length // 2
    mine = place[3].shape[0] // 2
    full = pl.BlockSpec((D, D), lambda i, *_: (0, 0))
    return pl.pallas_call(
        functools.partial(first_row_kernel, length=length),
        grid_spec=pltpu.PrefetchScalarGridSpec(
            num_scalar_prefetch=4,
            grid=(1,),
            in_specs=[tok] * 4 + [pl.BlockSpec((16, 512), lambda i, *_: (0, 0)), tok] + [full] * 3,
            out_specs=[tok] * 3
            + [
                pl.BlockSpec((1, half, D), lambda i, s, *_: (mine * s[0], 0, 0)),
                pl.BlockSpec((half, D), lambda i, *_: (0, 0)),
            ],
        ),
        out_shape=[SDS((length, D), bf16)] * 3 + [SDS((2 * mine, half, D), bf16), SDS((half, D), bf16)],
        compiler_params=pltpu.CompilerParams(vmem_limit_bytes=VMEM_LIMIT),
        cost_estimate=LONG,
        name="back_first",
    )(*place, q, k, v, dctx, lse, dr1, *weights)


def group_kernel(me, s0, s1, s2, s3, q_r, k_r, v_r, g_r, lse, dq0, dk0, dv0, xt, *rest, lengths, pairs, first, final):
    if final:
        bg_before, rest = rest[0], rest[1:]
    dq, dk, dv, send, keep, bg, every, dw = rest
    width = 128 * pairs
    long, mid = lengths
    step = pl.program_id(0)

    @pl.when(step == 0)
    def _():
        backward_pairs(pairs, (s0, s1, s2, s3), 1, long, q_r, k_r, v_r, g_r, lse, first, dq, dk, dv)
        for a, (old, new) in enumerate(((dq0, dq), (dk0, dk), (dv0, dv))):
            lanes = slice(a * width, (a + 1) * width)
            every[0:long, lanes] = old[...]
            every[long : 2 * long, lanes] = new[...]

    @pl.when(step == 1)
    def _():
        backward_pairs(pairs, (s0, s1, s2, s3), 2, mid, q_r, k_r, v_r, g_r, lse, first, dq, dk, dv)
        for a, new in enumerate((dq, dk, dv)):
            every[2 * long : 2 * long + mid, a * width : (a + 1) * width] = new[0:mid, :]
        count = 2 * long + mid
        for c in range(3 * width // D):
            dw[:, D * c : D * (c + 1)] = dot(xt[:, 0:count], every[:, D * c : D * (c + 1)])
        bg[...] = jnp.zeros_like(bg)
        bg[0:1, :] = column_sum(every[:, 0:width])
        bg[1:2, :] = column_sum(every[:, 2 * width : 3 * width])
        if final:
            sums = jnp.concatenate([bg_before[...], bg[...]], axis=1)
        for half, out in ((0, keep), (1, send)):
            for r in range(16):
                d = block_number(half, r) ^ me[0]
                for c in range(3 * width // D):
                    emit_24(dw, D * c, d, out, r, 1152 * c)
                if final:
                    small = pltpu.roll(sums, lax.rem(D - 24 * d, D), 1)[:, 0:128]
                    small = jnp.concatenate([small, small], axis=0)
                    out[r, :, 1152 * (3 * width // D) :] = small.astype(bf16)


def group_backward(me, place, q, k, v, dctx, lse, before, xt, lengths, pairs, first, bg_before):
    final = bg_before is not None
    width = 128 * pairs
    column = first // pairs
    long, mid = lengths
    count = 2 * long + mid
    tok = pl.BlockSpec((long, width), lambda i, *_: (1 + i, column))
    old = pl.BlockSpec((long, width), lambda i, *_: (0, column))
    new = pl.BlockSpec((long, width), lambda i, *_: (i, 0))
    size = 3 * width * 24 // 16 + (128 if final else 0)
    out = pl.BlockSpec((16, 16, size), lambda i, *_: (0, 0, 0))
    extra = [bg_before] if final else []
    specs = [pl.BlockSpec(a.shape, lambda i, *_: (0, 0)) for a in extra]
    return pl.pallas_call(
        functools.partial(group_kernel, lengths=lengths, pairs=pairs, first=first, final=final),
        grid_spec=pltpu.PrefetchScalarGridSpec(
            num_scalar_prefetch=5,
            grid=(2,),
            in_specs=[tok] * 4
            + [pl.BlockSpec((16, 512), lambda i, *_: (1 + i, 0))]
            + [old] * 3
            + [pl.BlockSpec(xt.shape, lambda i, *_: (0, 0))]
            + specs,
            out_specs=[new] * 3 + [out, out, pl.BlockSpec((8, width), lambda i, *_: (0, 0))],
            scratch_shapes=[pltpu.VMEM((count, 3 * width), bf16), pltpu.VMEM((D, 3 * width), f32)],
        ),
        out_shape=[SDS((2 * long, width), bf16)] * 3
        + [SDS((16, 16, size), bf16)] * 2
        + [SDS((8, width), f32)],
        compiler_params=pltpu.CompilerParams(vmem_limit_bytes=VMEM_LIMIT),
        cost_estimate=LONG,
        name=f"back_group_{first}",
    )(me, *place, q, k, v, dctx, lse, *before, xt, *extra)


def input_grad_kernel(seq, dr1, *rest, lengths, lanes):
    groups = len(lanes)
    blocks, (wq, wk, wv), (_, own, own_mid, other) = rest[: 3 * groups], rest[3 * groups : 3 * groups + 3], rest[-4:]
    long, mid = lengths
    n = slice(0, long + mid)
    total = dr1[...]
    for a, w in enumerate((wq, wk, wv)):
        for g, (low, high) in enumerate(lanes):
            total = total + dot_nt(blocks[3 * g + a][n, :], w[:, low:high])
    total = total.astype(bf16)
    own[0] = total[0 : long // 2]
    other[0 : long // 2, :] = total[long // 2 : long]
    own_mid[...] = total[long : long + mid // 2]
    other[long // 2 :, :] = total[long + mid // 2 :]


def input_grad(seq, dr1, groups, lanes, weights, lengths, before):
    long, mid = lengths
    flat = [a for g in groups for a in g]
    mine = before.shape[0] // 2
    whole = lambda a: pl.BlockSpec(a.shape, lambda i, s: (0, 0))
    ins = flat + list(weights)
    return pl.pallas_call(
        functools.partial(input_grad_kernel, lengths=lengths, lanes=lanes),
        grid_spec=pltpu.PrefetchScalarGridSpec(
            num_scalar_prefetch=1,
            grid=(1,),
            in_specs=[pl.BlockSpec((pl.Element(long + mid), pl.Element(D)), lambda i, s: (long, 0))]
            + [whole(a) for a in ins]
            + [ANY],
            out_specs=[
                pl.BlockSpec((1, long // 2, D), lambda i, s: (mine * s[0] + 1, 0, 0)),
                pl.BlockSpec((mid // 2, D), lambda i, s: (0, 0)),
                pl.BlockSpec(((long + mid) // 2, D), lambda i, s: (0, 0)),
            ],
        ),
        out_shape=[SDS(before.shape, bf16), SDS((mid // 2, D), bf16), SDS(((long + mid) // 2, D), bf16)],
        input_output_aliases={2 + len(ins): 0},
        compiler_params=pltpu.CompilerParams(vmem_limit_bytes=VMEM_LIMIT),
        cost_estimate=LONG,
        name="input_grad",
    )(seq, dr1, *ins, before)


def swap_seq(v):
    return lax.ppermute(v, "seq", [(0, 1), (1, 0)])


def later(value, *others):
    return lax.optimization_barrier((value, *others))[0]


AXES = {"w": (0, 16), "z": (1, 8), "y": (2, 4), "x": (3, 1)}
CORE = 2


def swap(v, mask):
    return lax.ppermute(v, ("dp", "seq"), [(i, i ^ mask) for i in range(BLOCKS)])


class Payload:
    def __init__(self, groups, order):
        self.groups = groups
        self.order = order

    def specs(self, bits):
        todo = {AXES[a][0] for a in "".join(self.order)}
        found = []
        for width, arrays in self.groups:
            for array, lane in arrays:
                shape = tuple(2 if d in todo and d not in bits else 1 for d in range(4))
                index = tuple(bits.get(d, 0) if array.shape[d] == 2 else 0 for d in range(4))
                found.append((array, pl.BlockSpec(shape + (16, width), functools.partial(fixed, index + (0, lane)))))
        return found

    def receive(self, after=None):
        for outgoing, mask in zip(self.outgoing, self.masks):
            received = swap(outgoing, mask)
            if after is not None:
                received = later(received, after)
            low = 0
            for width, arrays in self.groups:
                arrays.append((received, low // width))
                low += width
        return self


def fixed(index, *_):
    return index


def join(*sums):
    return Payload([g for h in sums for g in h.groups], sums[0].order)


def load_sum(refs):
    total = refs[0][...].astype(f32)
    for r in refs[1:]:
        total = total + r[...].astype(f32)
    return total


def add_kernel(*refs, plan):
    outs = refs[len(refs) - len(plan) :]
    at = 0
    for out, groups in zip(outs, plan):
        low = 0
        for count, width in groups:
            out[:, :, :, :, :, low : low + width] = load_sum(refs[at : at + count]).astype(bf16)
            at += count
            low += width


def send(*sums):
    arrays, specs, plan, shapes = [], [], [], []
    for h in sums:
        step, rest = h.order[0], h.order[1:]
        h.masks, h.count = [], 0
        for which in range(1, 2 ** len(step)):
            bits = {AXES[a][0]: which >> i & 1 for i, a in enumerate(step)}
            h.masks.append(sum(AXES[a][1] for i, a in enumerate(step) if which >> i & 1))
            found = h.specs(bits)
            arrays += [f[0] for f in found]
            specs += [f[1] for f in found]
            plan.append([(len(g[1]), g[0]) for g in h.groups])
            left = {AXES[a][0] for a in "".join(rest)}
            shapes.append(tuple(2 if d in left else 1 for d in range(4)) + (16, sum(g[0] for g in h.groups)))
            h.count += 1
        h.order = rest
    outs = pl.pallas_call(
        functools.partial(add_kernel, plan=plan),
        grid=(1,),
        in_specs=specs,
        out_specs=[pl.BlockSpec(n, functools.partial(fixed, (0,) * 6)) for n in shapes],
        out_shape=[SDS(n, bf16) for n in shapes],
        compiler_params=pltpu.CompilerParams(vmem_limit_bytes=VMEM_LIMIT),
        cost_estimate=LONG,
        name="add_parts",
    )(*arrays)
    at = 0
    for h in sums:
        h.outgoing = outs[at : at + h.count]
        at += h.count


def across_cores(pair, after, ranges, order):
    leaving, keep = pair
    received = later(swap(leaving, CORE), after)
    both = [v.reshape(2, 2, 2, 2, 16, -1) for v in (keep, received)]
    return [
        Payload([(width, [(v, lane) for v in both]) for width, lane in groups], axes) for axes, groups in zip(order, ranges)
    ]


def store_24(block, out, column, lanes=D):
    for g in range(3):
        for t in range(2):
            piece = block[8 * t : 8 * t + 8, 384 * g : 384 * (g + 1)]
            out[8 * g : 8 * g + 8, column + lanes // 2 * t : column + lanes // 2 * t + 384] = piece


def last_dense_kernel(seq, *refs, plan):
    (*ins, w_up, w_down, w_out, small) = refs
    blocks = []
    at = 0
    for count in plan:
        blocks.append(load_sum(ins[at : at + count])[0, 0, 0, 0])
        at += count
    up = jnp.concatenate(blocks[:2], axis=1)
    down = jnp.concatenate(blocks[2:], axis=1)
    for j in range(4):
        store_24(up[:, 1152 * j : 1152 * (j + 1)], w_up, 384 * j, FF)
    for g in range(6):
        w_down[16 * g : 16 * (g + 1), :] = down[:, D * g : D * (g + 1)]
    store_24(down[:, 4608:5760], w_out, 0)
    small[...] = down[:, 5760:5888]


def last_qkv_kernel(seq, *refs, plan):
    (*ins, w_query, w_key, w_value, small, scr) = refs
    blocks = []
    at = 0
    for count in plan:
        blocks.append(load_sum(ins[at : at + count])[0, 0, 0, 0])
        at += count
    left, right, tail = blocks
    for c in range(2):
        store_24(left[:, 1152 * c : 1152 * (c + 1)], scr, D * c)
    store_24(right, scr, 2 * D)
    for a, out in enumerate((w_query, w_key, w_value)):
        out[:, 0:512] = scr[:, 512 * a : 512 * (a + 1)]
        out[:, 512:768] = scr[:, 2 * D + 256 * a : 2 * D + 256 * (a + 1)]
    small[...] = tail


def last_sums(kernel, seq, sums, shapes, scratch):
    found = [f for h in sums for f in h.specs({})]
    plan = [len(g[1]) for h in sums for g in h.groups]
    return pl.pallas_call(
        functools.partial(kernel, plan=plan),
        grid=(1,),
        in_specs=[pl.BlockSpec(memory_space=pltpu.SMEM)] + [f[1] for f in found],
        out_specs=[pl.BlockSpec(n, functools.partial(fixed, (0, 0))) for n in shapes],
        out_shape=[SDS(n, f32) for n in shapes],
        scratch_shapes=[pltpu.VMEM(n, f32) for n in scratch],
        compiler_params=pltpu.CompilerParams(vmem_limit_bytes=VMEM_LIMIT),
        cost_estimate=LONG,
        name="last_sums",
    )(seq, *[f[0] for f in found])


def rows_24(block):
    return block.reshape(2, 8, 3, 384).transpose(2, 1, 0, 3).reshape(24, D)


def unpack_up(block):
    return block.reshape(2, 8, 4, 3, 384).transpose(3, 1, 0, 2, 4).reshape(24, FF)


def unpack_down(block):
    return block[:, :4608].reshape(16, 6, D).transpose(1, 0, 2).reshape(96, D), rows_24(block[:, 4608:5760])


def unpack_qkv(blocks):
    wide, narrow = blocks
    left = jnp.concatenate([rows_24(wide[:, :1152]), rows_24(wide[:, 1152:])], axis=1)
    right = rows_24(narrow[:, :1152])
    return [
        jnp.concatenate([left[:, 512 * a : 512 * (a + 1)], right[:, 256 * a : 256 * (a + 1)]], axis=1) for a in range(3)
    ]


def reduce_plain(up_pair, down_pair, qkv_pairs, vec, bg):
    def ordered(pair):
        send, keep = pair
        both = jnp.stack([keep.reshape(8, 2, 16, -1), send.reshape(8, 2, 16, -1)], axis=1)
        return both.reshape(BLOCKS, 16, -1).astype(f32)

    scatter = lambda v: lax.psum_scatter(v, ("dp", "seq"), scatter_dimension=0, tiled=True)
    w_up = jax.vmap(unpack_up)(ordered(up_pair)).reshape(D, FF)
    w_down, w_out = (a.reshape(-1, D) for a in jax.vmap(unpack_down)(ordered(down_pair)))
    qkv = [a.reshape(D, D) for a in jax.vmap(unpack_qkv)([ordered(p) for p in qkv_pairs])]
    small = [scatter(vec[i]) for i in range(6)]
    return (
        scatter(qkv[0]), scatter(bg[0]), scatter(qkv[1]), scatter(qkv[2]), scatter(bg[1]), scatter(w_out),
        small, scatter(w_up), scatter(vec[8:12].reshape(FF)), scatter(w_down),
    )


def give_back_kernel(seq, here, got, got_end, long_in, long, middle, short):
    long[0] = got[...]

    @pl.when(seq[0] == 0)
    def _():
        middle[0] = here[...]
        short[0] = got_end[: short.shape[1], :]

    @pl.when(seq[0] != 0)
    def _():
        middle[0] = got_end[...]
        short[0] = here[: short.shape[1], :]


def give_back(seq, long, here, got, short):
    count, half, _ = long.shape
    mid = here.shape[0]
    other = lambda i, s: (count // 2 * (1 - s[0]) + i, 0, 0)
    return pl.pallas_call(
        give_back_kernel,
        grid_spec=pltpu.PrefetchScalarGridSpec(
            num_scalar_prefetch=1,
            grid=(count // 2,),
            in_specs=[
                pl.BlockSpec((mid, D), lambda i, s: (0, 0)),
                pl.BlockSpec((half, D), lambda i, s: (i, 0)),
                pl.BlockSpec((mid, D), lambda i, s: (count // 2 * half // mid, 0)),
                ANY,
            ],
            out_specs=[
                pl.BlockSpec((1, half, D), other),
                pl.BlockSpec((1, mid, D), lambda i, s: (0, 0, 0)),
                pl.BlockSpec((1, short, D), lambda i, s: (0, 0, 0)),
            ],
        ),
        out_shape=[SDS(long.shape, bf16), SDS((1, mid, D), bf16), SDS((1, short, D), bf16)],
        input_output_aliases={4: 0},
        compiler_params=pltpu.CompilerParams(vmem_limit_bytes=VMEM_LIMIT),
        cost_estimate=LONG,
        name="add_halves",
    )(seq, here, got, got, long)


def per_device(
    tokens_short, tokens_middle, tokens_long, length_short, length_middle, length_long,
    query_weight, query_bias, key_weight, value_weight, value_bias, output_weight, output_bias,
    attention_gain, attention_shift, up_weight, up_bias, down_weight, down_bias, output_gain, output_shift,
    upstream_short, upstream_middle, upstream_long,
):
    seq = lax.axis_index("seq")
    first = seq == 0
    device = (lax.axis_index("dp") * 2 + seq).astype(jnp.int32)
    fast = lax.axis_size("dp") * lax.axis_size("seq") == BLOCKS
    me = device if fast else jnp.int32(0)
    me_ref = me.reshape(1)
    count, half, _ = tokens_long.shape
    mine = count // 2
    mid = tokens_middle.shape[1]
    short = tokens_short.shape[1]
    lengths = (2 * half,) * mine + (2 * mid,)
    tokens = sum(lengths)
    rows = 2 * half * (mine + 1)

    def own_rows(v):
        return lax.dynamic_slice_in_dim(v, mine * seq, mine, 0)

    def other_rows(v):
        return lax.dynamic_slice_in_dim(v, mine * (1 - seq), mine, 0)

    def middle_rows(middle, low):
        low = jnp.pad(low[0], ((0, mid - short), (0, 0)))
        return jnp.where(first, middle[0], low), jnp.where(first, low, middle[0])

    x_mid, x_mid_out = middle_rows(tokens_middle, tokens_short)
    x_mid_in = swap_seq(x_mid_out)
    x_own, x_out = own_rows(tokens_long), other_rows(tokens_long)
    x_in = [swap_seq(x_out[i]) for i in range(mine)]
    u_mid, u_mid_out = middle_rows(upstream_middle, upstream_short)
    u_out = jnp.concatenate([other_rows(upstream_long).reshape(mine * half, D), u_mid_out], axis=0)

    place = (seq.astype(jnp.int32).reshape(1), length_short, length_middle, length_long)
    qkv = [query_weight, key_weight, value_weight]
    projections = qkv + [query_bias, value_bias]
    chain = attention_forward(place, x_mid, x_mid_in, projections, mine, 2 * mid, mine * half // mid, None, rows)
    for i in range(mine):
        chain = attention_forward(place, x_own[i], x_in[i], projections, i, 2 * half, i, chain, rows)
    x, q, k, v, ctx, lse, xt = chain
    u_in = swap_seq(later(u_out, lse))

    mats = [output_weight, up_weight, down_weight]
    dense = functools.partial(
        dense_steps, place[0], ctx, x, tokens=tokens, rows=rows, mats=mats,
        vecs=[up_bias, output_bias, attention_gain, attention_shift, down_bias, output_gain, output_shift],
    )
    res_long, *before = dense(ups=[upstream_long], before=None)
    res_other, res_mid, act, dinn, nlow, dbr, datt, dr1, dctx, vec = dense(ups=[u_in, u_in, u_mid], before=before)

    up_pair = up_grad(me_ref, nlow, dinn, tokens)
    part = half
    res_got = [swap_seq(later(res_other[:part], up_pair[0]))]
    down_pair = down_grad(later(me_ref, up_pair[0]), act, dbr, ctx, datt, vec, tokens)
    res_got[0] = later(res_got[0], down_pair[0])
    res_got.append(swap_seq(later(res_other[part:], res_got[0])))

    def at(before, *sums, done=()):
        going = [v for h in sums for v in h.outgoing] if fast else []
        return (later(place[0], before, *going, *done), *place[1:])

    up = down = all_sum = ()
    if fast:
        up = across_cores(
            up_pair, down_pair[0], [[(2304, 0)], [(2304, 1)]], [["z", "x", "y", "w"], ["y", "x", "z", "w"]]
        )
        send(*up)
    *before, ig_long, ig_other = first_row_backward(
        at(down_pair[0], *up), q, k, v, dctx, lse, dr1, qkv, 2 * half
    )
    if fast:
        for h in up:
            h.receive(ig_other)
        down = across_cores(
            down_pair, ig_other, [[(2944, 0)], [(2944, 1)]], [["z", "y", "x", "w"], ["y", "z", "x", "w"]]
        )
        send(*up, *down)
    res_got[1] = later(res_got[1], ig_other)
    later_rows = (2 * half, 2 * mid)
    *wide, leaving, keep, bg = group_backward(
        me_ref, at(ig_other, *up, *down, done=res_got), q, k, v, dctx, lse, before, xt, later_rows, 4, 0, None
    )
    wide_pair = (leaving, keep)
    if fast:
        for h in (*up, *down):
            h.receive(bg)
        send(*up, *down)
    ig_got = [swap_seq(later(ig_other, bg))]
    *narrow, leaving, keep, bg_last = group_backward(
        me_ref, at(bg, *up, *down), q, k, v, dctx, lse, before, xt, later_rows, 2, 4, bg
    )
    narrow_pair = (leaving, keep)
    ig_got[0] = later(ig_got[0], bg_last)
    if fast:
        for h in (*up, *down):
            h.receive(bg_last)
        up = (join(*up),)
        down = (join(*down),)
        send(*up, *down)
        wide_sum = across_cores(wide_pair, bg_last, [[(2304, 0)]], [["yz", "xw"]])
        narrow_sum = across_cores(narrow_pair, up[0].outgoing[0], [[(1152, 0), (128, 9)]], [["yz", "xw"]])
        all_sum = (join(*wide_sum, *narrow_sum),)
        send(*all_sum)
    ig_long, ig_mid, ig_rest = input_grad(
        at(bg_last, *up, *down, *all_sum)[0], later(dr1, ig_got[0]), [wide, narrow], [(0, 512), (512, 768)], qkv, later_rows, ig_long
    )
    ig_got.append(swap_seq(ig_rest))
    if fast:
        up[0].receive(ig_rest)
        down[0].receive(ig_rest)
        send(*down)
        all_sum[0].receive(down[0].outgoing[0])
        send(*all_sum)
        spare = all_sum[0].outgoing[0]
        down[0].receive()
        w_up, w_down, w_out, small = last_sums(
            last_dense_kernel, later(place[0], spare), [*up, *down], [(24, FF), (96, D), (24, D), (16, 128)], []
        )
        all_sum[0].receive()
        w_query, w_key, w_value, ends = last_sums(
            last_qkv_kernel, place[0], all_sum, [(24, D)] * 3 + [(16, 128)], [(24, 3 * D)]
        )
        b_up = lax.dynamic_slice(small, (8 + (me >> 3), 0), (1, 96))[0]
        done = w_query, ends[0, :24], w_key, w_value, ends[1, :24], w_out, small[:8, :24], w_up, b_up, w_down
    else:
        spare = ig_rest
        done = reduce_plain(up_pair, down_pair, [wide_pair, narrow_pair], vec, jnp.concatenate([bg, bg_last], axis=1))
    res_long, res_middle, res_short = give_back(
        later(place[0], spare), res_long, res_mid, jnp.concatenate(res_got, axis=0), short
    )
    ig_long, ig_middle, ig_short = give_back(place[0], ig_long, ig_mid, jnp.concatenate(ig_got, axis=0), short)
    results = (res_short, res_middle, res_long)
    input_grads = (ig_short, ig_middle, ig_long)
    w_query, bq, w_key, w_value, bv, w_out, small, w_up, b_up, w_down = done
    return (
        *results, *input_grads,
        w_query, bq, w_key, w_value, bv, w_out, small[5], small[3], small[4],
        w_up, b_up, w_down, small[2], small[0], small[1],
    )


def solution(mesh):
    tokens = P("dp", "seq", None)
    wide = P(("dp", "seq"), None)
    flat = P(("dp", "seq"))
    in_specs = (tokens,) * 3 + (P("dp"),) * 3 + (P(),) * 15 + (tokens,) * 3
    out_specs = (tokens,) * 6 + (
        wide, flat, wide, wide, flat, wide, flat, flat, flat, wide, flat, wide, flat, flat, flat,
    )
    return jax.shard_map(per_device, mesh=mesh, in_specs=in_specs, out_specs=out_specs, check_vma=False)
```

```python
import functools

import jax
import jax.numpy as jnp
from jax import lax
from jax.experimental import pallas as pl
from jax.experimental.pallas import tpu as pltpu
from jax.sharding import PartitionSpec as P

D = 768
FF = 3072
HEADS = 12
PAIRS = HEADS // 2
EPS = 1e-12
NEG = -1e30
SHORT_HALF = 64
BLOCKS = 32
VMEM_LIMIT = 60 * 2**20
SMALL_LIMIT = 12 * 2**20

bf16 = jnp.bfloat16
f32 = jnp.float32
SDS = jax.ShapeDtypeStruct
ANY = pl.BlockSpec(memory_space=pl.ANY)
LONG = pl.CostEstimate(flops=4 * 10**10, bytes_accessed=10**8, transcendentals=0)


def dot(a, b):
    return lax.dot_general(a, b, (((1,), (0,)), ((), ())), preferred_element_type=f32)


def dot_nt(a, b):
    return lax.dot_general(a, b, (((1,), (1,)), ((), ())), preferred_element_type=f32)


def dot_tn(a, b):
    return lax.dot_general(a, b, (((0,), (0,)), ((), ())), preferred_element_type=f32)


def wide(vector):
    return vector[...].reshape(1, -1)


def mean(v):
    return jnp.mean(v, axis=-1, keepdims=True)


def column_sum(v):
    return jnp.sum(v.astype(f32), axis=0, keepdims=True)


A1, A2, A3, A4, A5 = 0.254829592, -0.284496736, 1.421413741, -1.453152027, 1.061405429
P_SCALED = 0.3275911 * 0.7071067811865476
INV_SQRT_2PI = 0.3989422804014327


def gelu_and_slope(v):
    t = 1.0 / (1.0 + P_SCALED * jnp.abs(v))
    e = jnp.exp(v * v * -0.5)
    tail = t * (A1 + t * (A2 + t * (A3 + t * (A4 + t * A5)))) * (0.5 * e)
    cdf = jnp.where(v < 0, tail, 1.0 - tail)
    return v * cdf, cdf + v * (e * INV_SQRT_2PI)


def mask_column(place, row, length):
    seq, short, middle, long = place
    half = length // 2
    mine = long.shape[0] // 2
    s = seq[0]
    if row < mine:
        count, valid, own, other = long[mine * s + row], half, half * s, half * (1 - s)
    else:
        is_first = s == 0
        count = jnp.where(is_first, middle[0], short[0])
        valid = jnp.where(is_first, half, SHORT_HALF)
        own, other = jnp.where(is_first, 0, SHORT_HALF), jnp.where(is_first, half, 0)
    i = lax.broadcasted_iota(jnp.int32, (length, 1), 0)
    inner = jnp.where(i < half, i, i - half)
    live = (inner + jnp.where(i < half, own, other) < count) & (inner < valid)
    return jnp.where(live, 0.0, NEG).astype(f32)


def low_lanes():
    return lax.broadcasted_iota(jnp.int32, (1, 128), 1) < 64


def stack_heads(pair, low):
    zero = jnp.zeros_like(pair)
    return jnp.concatenate([jnp.where(low, pair, zero), jnp.where(low, zero, pair)], axis=0)


def split_rows(pair_t):
    row = lax.broadcasted_iota(jnp.int32, (128, 1), 0) < 64
    zero = jnp.zeros_like(pair_t)
    return jnp.where(row, pair_t, zero), jnp.where(row, zero, pair_t)


def scaled(q):
    return (q.astype(f32) * 0.125).astype(bf16)


def emit_24(scr, lane, d, out, r, base):
    for g in range(3):
        rows = pl.ds(pl.multiple_of(24 * d + 8 * g, 8), 8)
        both = jnp.concatenate(
            [scr[rows, lane : lane + 384], scr[rows, lane + 384 : lane + 768]], axis=0
        )
        out[r, :, base + 384 * g : base + 384 * (g + 1)] = both.astype(bf16)


def block_number(half, r):
    return ((r >> 1) << 2) | (half << 1) | (r & 1)


def forward_kernel(s0, s1, s2, s3, xl, xr, wq, wk, wv, bq, bv, *rest, length, row, chained):
    x_o, q_o, k_o, v_o, c_o, lse_o, xt_o = rest[7:] if chained else rest
    x = jnp.concatenate([xl[...], xr[...]], axis=0)
    x_o[...] = x
    xt_o[...] = x.T
    q_o[...] = (dot(x, wq[...]) + wide(bq)).astype(bf16)
    k_o[...] = dot(x, wk[...]).astype(bf16)
    v_o[...] = (dot(x, wv[...]) + wide(bv)).astype(bf16)
    bias = mask_column((s0, s1, s2, s3), row, length)
    low = low_lanes()
    row_low = lax.broadcasted_iota(jnp.int32, (128, 1), 0) < 64
    for p in range(PAIRS):
        sl = slice(128 * p, 128 * p + 128)
        scores = dot_nt(stack_heads(k_o[:, sl], low), scaled(q_o[:, sl]))
        parts = []
        inverse = []
        for h in range(2):
            s = scores[h * length : (h + 1) * length, :] + bias
            top = jnp.max(s, axis=0, keepdims=True)
            raised = jnp.exp(s - top)
            total = jnp.sum(raised, axis=0, keepdims=True)
            lse_o[2 * p + h : 2 * p + h + 1, 0:length] = top + jnp.log(total)
            parts.append(raised.astype(bf16))
            inverse.append(1.0 / total)
        upper, lower = split_rows(v_o[:, sl].T)
        context = dot(upper, parts[0]) + dot(lower, parts[1])
        context = context * jnp.where(row_low, inverse[0], inverse[1])
        c_o[:, sl] = context.T.astype(bf16)


def attention_forward(place, own, other, weights, row, length, block, chain, rows):
    half = pl.BlockSpec((length // 2, D), lambda i: (0, 0))
    full = lambda a: pl.BlockSpec(a.shape, lambda i: (0,) * a.ndim)
    tok = pl.BlockSpec((length, D), lambda i: (block, 0))
    lse = pl.BlockSpec((16, 512), lambda i: (row, 0))
    turned = pl.BlockSpec((D, length), lambda i: (0, block))
    chained = chain is not None
    extra = list(chain) if chained else []
    return pl.pallas_call(
        functools.partial(forward_kernel, length=length, row=row, chained=chained),
        grid=(1,),
        in_specs=[pl.BlockSpec(memory_space=pltpu.SMEM)] * 4
        + [half, half]
        + [full(w) for w in weights]
        + [ANY] * len(extra),
        out_specs=[tok] * 5 + [lse, turned],
        out_shape=[SDS((rows, D), bf16)] * 5 + [SDS((48, 512), f32), SDS((D, rows), bf16)],
        input_output_aliases={11 + i: i for i in range(7)} if chained else {},
        compiler_params=pltpu.CompilerParams(vmem_limit_bytes=57 * 2**20),
        cost_estimate=LONG,
        name=f"attend_{row}",
    )(*place, own, other, *weights, *extra)


def drop_first(kernel):
    return lambda _, *refs, **options: kernel(*refs, **options)


def dense_kernel(*refs, chunks, own):
    ctx, x = refs[0], refs[1]
    step = pl.program_id(0)
    last = step == pl.num_programs(0) - 1
    if own:
        up_refs, refs = refs[2:3], refs[3:]
        up = up_refs[0][0]
    else:
        up_refs, refs = refs[2:5], refs[5:]
        up = jnp.concatenate([jnp.where(last, up_refs[2][...], up_refs[0][...]), up_refs[1][...]], axis=0)
    wo, wup, wdn, bup, bo, g1, s1, bdn, g2, s2 = refs[:10]
    bup, bo, g1, s1, bdn, g2, s2 = (wide(v) for v in (bup, bo, g1, s1, bdn, g2, s2))
    if own:
        res_own, act, dinn, nlow_o, dbr, datt, dr1_o, dctx, vec, slope_s = refs[10:]
    else:
        vec_in = refs[10]
        res_other, res_mid, act, dinn, nlow_o, dbr, datt, dr1_o, dctx, vec, slope_s = refs[18:]

    @pl.when(step == 0)
    def _():
        vec[...] = jnp.zeros_like(vec) if own else vec_in[...]

    r1 = x[...].astype(f32) + dot(ctx[...], wo[...]) + bo
    c1 = r1 - mean(r1)
    rs1 = lax.rsqrt(mean(c1 * c1) + EPS)
    n1 = c1 * rs1
    normed = n1 * g1 + s1
    nlow = normed.astype(bf16)
    nlow_o[...] = nlow
    acc = normed + bdn
    width = FF // chunks
    for j in range(chunks):
        sl = slice(j * width, (j + 1) * width)
        value, slope = gelu_and_slope(dot(nlow, wup[:, sl]) + bup[:, sl])
        value = value.astype(bf16)
        act[:, sl] = value
        slope_s[:, sl] = slope
        acc = acc + dot(value, wdn[sl, :])
    c2 = acc - mean(acc)
    rs2 = lax.rsqrt(mean(c2 * c2) + EPS)
    n2 = c2 * rs2
    result = (n2 * g2 + s2).astype(bf16)
    if own:
        res_own[0] = result
    else:
        size = result.shape[0]

        @pl.when(jnp.logical_not(last))
        def _():
            res_other[pl.ds(pl.multiple_of(step * size, size), size), :] = result

        @pl.when(last)
        def _():
            res_mid[...] = result[: size // 2]
            res_other[res_other.shape[0] - size // 2 :, :] = result[size // 2 :]

    upstream = up.astype(f32)
    u = upstream * g2
    dr2 = (u - mean(u) - n2 * mean(u * n2)) * rs2
    branch = dr2.astype(bf16)
    dbr[...] = branch
    vec[0:1, :] += column_sum(upstream * n2)
    vec[1:2, :] += column_sum(upstream)
    vec[2:3, :] += column_sum(branch)
    acc = dr2
    for j in range(chunks):
        sl = slice(j * width, (j + 1) * width)
        d_inner = (dot_nt(branch, wdn[sl, :]) * slope_s[:, sl]).astype(bf16)
        dinn[:, sl] = d_inner
        vec[8 + j : 9 + j, :] += column_sum(d_inner)
        acc = acc + dot_nt(d_inner, wup[:, sl])
    vec[3:4, :] += column_sum(acc * n1)
    vec[4:5, :] += column_sum(acc)
    u1 = acc * g1
    d1 = (u1 - mean(u1) - n1 * mean(u1 * n1)) * rs1
    d_attn = d1.astype(bf16)
    datt[...] = d_attn
    dr1_o[...] = d1
    vec[5:6, :] += column_sum(d_attn)
    dctx[...] = dot_nt(d_attn, wo[...]).astype(bf16)


def dense_steps(seq, ctx, x, ups, mats, vecs, tokens, rows, before):
    tile = 256
    half = tile // 2
    mine = tokens // tile // 2
    own = before is None
    full = lambda a: pl.BlockSpec(a.shape, lambda i, s: (0,) * a.ndim, pipeline_mode=pl.Buffered(1))
    whole = lambda n: pl.BlockSpec((n, D), lambda i, s: (0, 0))
    if own:
        place = lambda i: 2 * i
        steps = mine
        up_specs = [pl.BlockSpec((1, tile, D), lambda i, s: (s[0] * mine + i, 0, 0))]
        res_specs = [pl.BlockSpec((1, tile, D), lambda i, s: (s[0] * mine + i, 0, 0))]
        res_shapes = [SDS((2 * mine, tile, D), bf16)]
        extra, extra_specs, aliases = [], [], {}
    else:
        place = lambda i: jnp.minimum(2 * i + 1, 2 * mine)
        steps = mine + 1
        up_specs = [
            pl.BlockSpec((half, D), lambda i, s: (jnp.minimum(2 * i, 2 * mine - 2), 0)),
            pl.BlockSpec((half, D), lambda i, s: (jnp.minimum(2 * i + 1, 2 * mine), 0)),
            whole(half),
        ]
        res_specs = [whole(tokens // 2), whole(half)]
        res_shapes = [SDS((tokens // 2, D), bf16), SDS((half, D), bf16)]
        *arrays, vec = before
        extra = [vec] + arrays
        extra_specs = [whole(16)] + [ANY] * len(arrays)
        first = 1 + 2 + len(ups) + len(mats) + len(vecs) + 1
        aliases = {first + i: 2 + i for i in range(len(arrays))}
    tok = pl.BlockSpec((tile, D), lambda i, s: (place(i), 0))
    ffs = pl.BlockSpec((tile, FF), lambda i, s: (place(i), 0))
    return pl.pallas_call(
        functools.partial(drop_first(dense_kernel), chunks=4, own=own),
        grid_spec=pltpu.PrefetchScalarGridSpec(
            num_scalar_prefetch=1,
            grid=(steps,),
            in_specs=[tok, tok] + up_specs + [full(a) for a in mats + vecs] + extra_specs,
            out_specs=res_specs + [ffs, ffs] + [tok] * 5 + [whole(16)],
            scratch_shapes=[pltpu.VMEM((tile, FF), f32)],
        ),
        out_shape=res_shapes
        + [SDS((tokens, FF), bf16)] * 2
        + [SDS((tokens, D), bf16)] * 3
        + [SDS((rows, D), f32), SDS((rows, D), bf16), SDS((16, D), f32)],
        input_output_aliases=aliases,
        compiler_params=pltpu.CompilerParams(vmem_limit_bytes=VMEM_LIMIT),
        cost_estimate=LONG,
        name="dense_own" if own else "dense_rest",
    )(seq, ctx, x, *ups, *mats, *vecs, *extra)


def up_grad_kernel(me, nlow, left, right, send, keep, turned, scr):

    @pl.when(pl.program_id(0) == 0)
    def _():
        turned[...] = nlow[...].T

    scr[:, 0:384] = dot(turned[...], left[...])
    scr[:, 384:768] = dot(turned[...], right[...])
    for half, out in ((0, keep), (1, send)):
        for r in range(16):
            emit_24(scr, 0, block_number(half, r) ^ me[0], out, r, 0)


def up_grad(me, nlow, dinn, tokens):
    out = pl.BlockSpec((16, 16, 1152), lambda j, m: (0, 0, j))
    return pl.pallas_call(
        up_grad_kernel,
        grid_spec=pltpu.PrefetchScalarGridSpec(
            num_scalar_prefetch=1,
            grid=(4,),
            in_specs=[
                pl.BlockSpec((tokens, D), lambda j, m: (0, 0)),
                pl.BlockSpec((tokens, 384), lambda j, m: (0, j)),
                pl.BlockSpec((tokens, 384), lambda j, m: (0, j + 4)),
            ],
            out_specs=[out, out],
            scratch_shapes=[pltpu.VMEM((D, tokens), bf16), pltpu.VMEM((D, D), f32)],
        ),
        out_shape=[SDS((16, 16, 4608), bf16)] * 2,
        compiler_params=pltpu.CompilerParams(vmem_limit_bytes=VMEM_LIMIT),
        cost_estimate=LONG,
        name="up_grad",
    )(me, nlow, dinn, dinn)


DOWN_WIDTH = 4608 + 1152 + 128


def down_grad_kernel(me, act, dbr, ctx, datt, vec, send, keep, scr, wo_s):
    j = pl.program_id(0)

    @pl.when(j == 0)
    def _():
        wo_s[...] = dot_tn(ctx[...], datt[...])

    scr[...] = dot_tn(act[...], dbr[...])
    z = j ^ (me[0] >> 3)
    for half, out in ((0, keep), (1, send)):
        for r in range(4):
            near = block_number(half, r) ^ (me[0] & 7)
            d = z * 8 + near
            for g in range(6):
                rows = pl.ds(pl.multiple_of(96 * near + 16 * g, 16), 16)
                out[r, :, D * g : D * (g + 1)] = scr[rows, :].astype(bf16)
            emit_24(wo_s, 0, d, out, r, 4608)
            small = pltpu.roll(vec[0:8, :], lax.rem(D - 24 * d, D), 1)[:, 0:128]
            wide = pltpu.roll(vec[8:16, :], lax.rem(D - 96 * near, D), 1)[:, 0:128]
            out[r, :, 5760:5888] = jnp.concatenate([small, wide], axis=0).astype(bf16)


def down_grad(me, act, dbr, ctx, datt, vec, tokens):
    out = pl.BlockSpec((4, 16, DOWN_WIDTH), lambda j, m: (j, 0, 0))
    tok = pl.BlockSpec((tokens, D), lambda j, m: (0, 0))
    return pl.pallas_call(
        down_grad_kernel,
        grid_spec=pltpu.PrefetchScalarGridSpec(
            num_scalar_prefetch=1,
            grid=(4,),
            in_specs=[
                pl.BlockSpec((tokens, D), lambda j, m: (0, j ^ (m[0] >> 3))),
                tok,
                tok,
                tok,
                pl.BlockSpec((16, D), lambda j, m: (0, 0)),
            ],
            out_specs=[out, out],
            scratch_shapes=[pltpu.VMEM((D, D), f32), pltpu.VMEM((D, D), f32)],
        ),
        out_shape=[SDS((16, 16, DOWN_WIDTH), bf16)] * 2,
        compiler_params=pltpu.CompilerParams(vmem_limit_bytes=VMEM_LIMIT),
        cost_estimate=LONG,
        name="down_grad",
    )(me, act, dbr, ctx, datt, vec)


def backward_pairs(pairs, place, row, length, q_r, k_r, v_r, g_r, lse, first, dq_o, dk_o, dv_o):
    n = slice(0, length)
    bias = mask_column(place, row, length)
    low = low_lanes()
    for p in range(pairs):
        sl = slice(128 * p, 128 * p + 128)
        q2 = scaled(q_r[n, sl])
        k2 = k_r[n, sl]
        g2 = g_r[n, sl]
        scores = dot_nt(stack_heads(k2, low), q2)
        d_probs = dot_nt(stack_heads(v_r[n, sl], low), g2)
        probs_low = []
        d_scores = []
        for h in range(2):
            part = slice(h * length, (h + 1) * length)
            head = 2 * (first + p) + h
            probs = jnp.exp(scores[part, :] + bias - lse[head : head + 1, n])
            d_part = d_probs[part, :]
            centre = jnp.sum(probs * d_part, axis=0, keepdims=True)
            probs_low.append(probs.astype(bf16))
            d_scores.append((probs * (d_part - centre)).astype(bf16))
        dv_o[n, sl] = jnp.where(low, dot(probs_low[0], g2), dot(probs_low[1], g2)).astype(bf16)
        dk_o[n, sl] = jnp.where(low, dot(d_scores[0], q2), dot(d_scores[1], q2)).astype(bf16)
        upper, lower = split_rows(k2.T)
        turned = dot(upper, d_scores[0]) + dot(lower, d_scores[1])
        dq_o[n, sl] = (turned * 0.125).T.astype(bf16)


def first_row_kernel(s0, s1, s2, s3, q_r, k_r, v_r, g_r, lse, dr1, wq, wk, wv, dq, dk, dv, ig_own, ig_other, *, length):
    backward_pairs(PAIRS, (s0, s1, s2, s3), 0, length, q_r, k_r, v_r, g_r, lse, 0, dq, dk, dv)
    ig = dr1[...] + dot_nt(dq[...], wq[...]) + dot_nt(dk[...], wk[...]) + dot_nt(dv[...], wv[...])
    ig = ig.astype(bf16)
    ig_own[0] = ig[: length // 2]
    ig_other[...] = ig[length // 2 :]


def first_row_backward(place, q, k, v, dctx, lse, dr1, weights, length):
    tok = pl.BlockSpec((length, D), lambda i, *_: (0, 0))
    half = length // 2
    mine = place[3].shape[0] // 2
    full = pl.BlockSpec((D, D), lambda i, *_: (0, 0))
    return pl.pallas_call(
        functools.partial(first_row_kernel, length=length),
        grid_spec=pltpu.PrefetchScalarGridSpec(
            num_scalar_prefetch=4,
            grid=(1,),
            in_specs=[tok] * 4 + [pl.BlockSpec((16, 512), lambda i, *_: (0, 0)), tok] + [full] * 3,
            out_specs=[tok] * 3
            + [
                pl.BlockSpec((1, half, D), lambda i, s, *_: (mine * s[0], 0, 0)),
                pl.BlockSpec((half, D), lambda i, *_: (0, 0)),
            ],
        ),
        out_shape=[SDS((length, D), bf16)] * 3 + [SDS((2 * mine, half, D), bf16), SDS((half, D), bf16)],
        compiler_params=pltpu.CompilerParams(vmem_limit_bytes=VMEM_LIMIT),
        cost_estimate=LONG,
        name="back_first",
    )(*place, q, k, v, dctx, lse, dr1, *weights)


def group_kernel(me, s0, s1, s2, s3, q_r, k_r, v_r, g_r, lse, dq0, dk0, dv0, xt, *rest, lengths, pairs, first, final):
    if final:
        bg_before, rest = rest[0], rest[1:]
    dq, dk, dv, send, keep, bg, every, dw = rest
    width = 128 * pairs
    long, mid = lengths
    step = pl.program_id(0)

    @pl.when(step == 0)
    def _():
        backward_pairs(pairs, (s0, s1, s2, s3), 1, long, q_r, k_r, v_r, g_r, lse, first, dq, dk, dv)
        for a, (old, new) in enumerate(((dq0, dq), (dk0, dk), (dv0, dv))):
            lanes = slice(a * width, (a + 1) * width)
            every[0:long, lanes] = old[...]
            every[long : 2 * long, lanes] = new[...]

    @pl.when(step == 1)
    def _():
        backward_pairs(pairs, (s0, s1, s2, s3), 2, mid, q_r, k_r, v_r, g_r, lse, first, dq, dk, dv)
        for a, new in enumerate((dq, dk, dv)):
            every[2 * long : 2 * long + mid, a * width : (a + 1) * width] = new[0:mid, :]
        count = 2 * long + mid
        for c in range(3 * width // D):
            dw[:, D * c : D * (c + 1)] = dot(xt[:, 0:count], every[:, D * c : D * (c + 1)])
        bg[...] = jnp.zeros_like(bg)
        bg[0:1, :] = column_sum(every[:, 0:width])
        bg[1:2, :] = column_sum(every[:, 2 * width : 3 * width])
        if final:
            sums = jnp.concatenate([bg_before[...], bg[...]], axis=1)
        for half, out in ((0, keep), (1, send)):
            for r in range(16):
                d = block_number(half, r) ^ me[0]
                for c in range(3 * width // D):
                    emit_24(dw, D * c, d, out, r, 1152 * c)
                if final:
                    small = pltpu.roll(sums, lax.rem(D - 24 * d, D), 1)[:, 0:128]
                    small = jnp.concatenate([small, small], axis=0)
                    out[r, :, 1152 * (3 * width // D) :] = small.astype(bf16)


def group_backward(me, place, q, k, v, dctx, lse, before, xt, lengths, pairs, first, bg_before):
    final = bg_before is not None
    width = 128 * pairs
    column = first // pairs
    long, mid = lengths
    count = 2 * long + mid
    tok = pl.BlockSpec((long, width), lambda i, *_: (1 + i, column))
    old = pl.BlockSpec((long, width), lambda i, *_: (0, column))
    new = pl.BlockSpec((long, width), lambda i, *_: (i, 0))
    size = 3 * width * 24 // 16 + (128 if final else 0)
    out = pl.BlockSpec((16, 16, size), lambda i, *_: (0, 0, 0))
    extra = [bg_before] if final else []
    specs = [pl.BlockSpec(a.shape, lambda i, *_: (0, 0)) for a in extra]
    return pl.pallas_call(
        functools.partial(group_kernel, lengths=lengths, pairs=pairs, first=first, final=final),
        grid_spec=pltpu.PrefetchScalarGridSpec(
            num_scalar_prefetch=5,
            grid=(2,),
            in_specs=[tok] * 4
            + [pl.BlockSpec((16, 512), lambda i, *_: (1 + i, 0))]
            + [old] * 3
            + [pl.BlockSpec(xt.shape, lambda i, *_: (0, 0))]
            + specs,
            out_specs=[new] * 3 + [out, out, pl.BlockSpec((8, width), lambda i, *_: (0, 0))],
            scratch_shapes=[pltpu.VMEM((count, 3 * width), bf16), pltpu.VMEM((D, 3 * width), f32)],
        ),
        out_shape=[SDS((2 * long, width), bf16)] * 3
        + [SDS((16, 16, size), bf16)] * 2
        + [SDS((8, width), f32)],
        compiler_params=pltpu.CompilerParams(vmem_limit_bytes=45 * 2**20),
        cost_estimate=LONG,
        name=f"back_group_{first}",
    )(me, *place, q, k, v, dctx, lse, *before, xt, *extra)


def input_grad_kernel(seq, dr1, *rest, lengths, lanes):
    groups = len(lanes)
    blocks, (wq, wk, wv), (_, own, own_mid, other) = rest[: 3 * groups], rest[3 * groups : 3 * groups + 3], rest[-4:]
    long, mid = lengths
    n = slice(0, long + mid)
    total = dr1[...]
    for a, w in enumerate((wq, wk, wv)):
        for g, (low, high) in enumerate(lanes):
            total = total + dot_nt(blocks[3 * g + a][n, :], w[:, low:high])
    total = total.astype(bf16)
    own[0] = total[0 : long // 2]
    other[0 : long // 2, :] = total[long // 2 : long]
    own_mid[...] = total[long : long + mid // 2]
    other[long // 2 :, :] = total[long + mid // 2 :]


def input_grad(seq, dr1, groups, lanes, weights, lengths, before):
    long, mid = lengths
    flat = [a for g in groups for a in g]
    mine = before.shape[0] // 2
    whole = lambda a: pl.BlockSpec(a.shape, lambda i, s: (0, 0))
    ins = flat + list(weights)
    return pl.pallas_call(
        functools.partial(input_grad_kernel, lengths=lengths, lanes=lanes),
        grid_spec=pltpu.PrefetchScalarGridSpec(
            num_scalar_prefetch=1,
            grid=(1,),
            in_specs=[pl.BlockSpec((pl.Element(long + mid), pl.Element(D)), lambda i, s: (long, 0))]
            + [whole(a) for a in ins]
            + [ANY],
            out_specs=[
                pl.BlockSpec((1, long // 2, D), lambda i, s: (mine * s[0] + 1, 0, 0)),
                pl.BlockSpec((mid // 2, D), lambda i, s: (0, 0)),
                pl.BlockSpec(((long + mid) // 2, D), lambda i, s: (0, 0)),
            ],
        ),
        out_shape=[SDS(before.shape, bf16), SDS((mid // 2, D), bf16), SDS(((long + mid) // 2, D), bf16)],
        input_output_aliases={2 + len(ins): 0},
        compiler_params=pltpu.CompilerParams(vmem_limit_bytes=24 * 2**20),
        cost_estimate=LONG,
        name="input_grad",
    )(seq, dr1, *ins, before)


def swap_seq(v):
    return lax.ppermute(v, "seq", [(0, 1), (1, 0)])


def later(value, *others):
    return lax.optimization_barrier((value, *others))[0]


AXES = {"w": (0, 16), "z": (1, 8), "y": (2, 4), "x": (3, 1)}
CORE = 2


def swap(v, mask):
    return lax.ppermute(v, ("dp", "seq"), [(i, i ^ mask) for i in range(BLOCKS)])


class Payload:
    def __init__(self, groups, order):
        self.groups = groups
        self.order = order

    def specs(self, bits):
        todo = {AXES[a][0] for a in "".join(self.order)}
        found = []
        for width, arrays in self.groups:
            for array, lane in arrays:
                shape = tuple(2 if d in todo and d not in bits else 1 for d in range(4))
                index = tuple(bits.get(d, 0) if array.shape[d] == 2 else 0 for d in range(4))
                found.append((array, pl.BlockSpec(shape + (16, width), functools.partial(fixed, index + (0, lane)))))
        return found

    def receive(self, after=None):
        for outgoing, mask in zip(self.outgoing, self.masks):
            received = swap(outgoing, mask)
            if after is not None:
                received = later(received, after)
            low = 0
            for width, arrays in self.groups:
                arrays.append((received, low // width))
                low += width
        return self


def fixed(index, *_):
    return index


def join(*sums):
    return Payload([g for h in sums for g in h.groups], sums[0].order)


def load_sum(refs):
    total = refs[0][...].astype(f32)
    for r in refs[1:]:
        total = total + r[...].astype(f32)
    return total


def add_kernel(*refs, plan):
    outs = refs[len(refs) - len(plan) :]
    at = 0
    for out, groups in zip(outs, plan):
        low = 0
        for count, width in groups:
            out[:, :, :, :, :, low : low + width] = load_sum(refs[at : at + count]).astype(bf16)
            at += count
            low += width


def send(*sums):
    arrays, specs, plan, shapes = [], [], [], []
    for h in sums:
        step, rest = h.order[0], h.order[1:]
        h.masks, h.count = [], 0
        for which in range(1, 2 ** len(step)):
            bits = {AXES[a][0]: which >> i & 1 for i, a in enumerate(step)}
            h.masks.append(sum(AXES[a][1] for i, a in enumerate(step) if which >> i & 1))
            found = h.specs(bits)
            arrays += [f[0] for f in found]
            specs += [f[1] for f in found]
            plan.append([(len(g[1]), g[0]) for g in h.groups])
            left = {AXES[a][0] for a in "".join(rest)}
            shapes.append(tuple(2 if d in left else 1 for d in range(4)) + (16, sum(g[0] for g in h.groups)))
            h.count += 1
        h.order = rest
    outs = pl.pallas_call(
        functools.partial(add_kernel, plan=plan),
        grid=(1,),
        in_specs=specs,
        out_specs=[pl.BlockSpec(n, functools.partial(fixed, (0,) * 6)) for n in shapes],
        out_shape=[SDS(n, bf16) for n in shapes],
        compiler_params=pltpu.CompilerParams(vmem_limit_bytes=SMALL_LIMIT),
        cost_estimate=LONG,
        name="add_parts",
    )(*arrays)
    at = 0
    for h in sums:
        h.outgoing = outs[at : at + h.count]
        at += h.count


def across_cores(pair, after, ranges, order):
    leaving, keep = pair
    received = later(swap(leaving, CORE), after)
    both = [v.reshape(2, 2, 2, 2, 16, -1) for v in (keep, received)]
    return [
        Payload([(width, [(v, lane) for v in both]) for width, lane in groups], axes) for axes, groups in zip(order, ranges)
    ]


def store_24(block, out, column, lanes=D):
    for g in range(3):
        for t in range(2):
            piece = block[8 * t : 8 * t + 8, 384 * g : 384 * (g + 1)]
            out[8 * g : 8 * g + 8, column + lanes // 2 * t : column + lanes // 2 * t + 384] = piece


def last_dense_kernel(seq, *refs, plan):
    (*ins, w_up, w_down, w_out, small) = refs
    blocks = []
    at = 0
    for count in plan:
        blocks.append(load_sum(ins[at : at + count])[0, 0, 0, 0])
        at += count
    up = jnp.concatenate(blocks[:2], axis=1)
    down = jnp.concatenate(blocks[2:], axis=1)
    for j in range(4):
        store_24(up[:, 1152 * j : 1152 * (j + 1)], w_up, 384 * j, FF)
    for g in range(6):
        w_down[16 * g : 16 * (g + 1), :] = down[:, D * g : D * (g + 1)]
    store_24(down[:, 4608:5760], w_out, 0)
    small[...] = down[:, 5760:5888]


def last_qkv_kernel(seq, *refs, plan):
    (*ins, w_query, w_key, w_value, small, scr) = refs
    blocks = []
    at = 0
    for count in plan:
        blocks.append(load_sum(ins[at : at + count])[0, 0, 0, 0])
        at += count
    left, right, tail = blocks
    for c in range(2):
        store_24(left[:, 1152 * c : 1152 * (c + 1)], scr, D * c)
    store_24(right, scr, 2 * D)
    for a, out in enumerate((w_query, w_key, w_value)):
        out[:, 0:512] = scr[:, 512 * a : 512 * (a + 1)]
        out[:, 512:768] = scr[:, 2 * D + 256 * a : 2 * D + 256 * (a + 1)]
    small[...] = tail


def last_sums(kernel, seq, sums, shapes, scratch):
    found = [f for h in sums for f in h.specs({})]
    plan = [len(g[1]) for h in sums for g in h.groups]
    return pl.pallas_call(
        functools.partial(kernel, plan=plan),
        grid=(1,),
        in_specs=[pl.BlockSpec(memory_space=pltpu.SMEM)] + [f[1] for f in found],
        out_specs=[pl.BlockSpec(n, functools.partial(fixed, (0, 0))) for n in shapes],
        out_shape=[SDS(n, f32) for n in shapes],
        scratch_shapes=[pltpu.VMEM(n, f32) for n in scratch],
        compiler_params=pltpu.CompilerParams(vmem_limit_bytes=SMALL_LIMIT),
        cost_estimate=LONG,
        name="last_sums",
    )(seq, *[f[0] for f in found])


def rows_24(block):
    return block.reshape(2, 8, 3, 384).transpose(2, 1, 0, 3).reshape(24, D)


def unpack_up(block):
    return block.reshape(2, 8, 4, 3, 384).transpose(3, 1, 0, 2, 4).reshape(24, FF)


def unpack_down(block):
    return block[:, :4608].reshape(16, 6, D).transpose(1, 0, 2).reshape(96, D), rows_24(block[:, 4608:5760])


def unpack_qkv(blocks):
    wide, narrow = blocks
    left = jnp.concatenate([rows_24(wide[:, :1152]), rows_24(wide[:, 1152:])], axis=1)
    right = rows_24(narrow[:, :1152])
    return [
        jnp.concatenate([left[:, 512 * a : 512 * (a + 1)], right[:, 256 * a : 256 * (a + 1)]], axis=1) for a in range(3)
    ]


def reduce_plain(up_pair, down_pair, qkv_pairs, vec, bg):
    def ordered(pair):
        send, keep = pair
        both = jnp.stack([keep.reshape(8, 2, 16, -1), send.reshape(8, 2, 16, -1)], axis=1)
        return both.reshape(BLOCKS, 16, -1).astype(f32)

    scatter = lambda v: lax.psum_scatter(v, ("dp", "seq"), scatter_dimension=0, tiled=True)
    w_up = jax.vmap(unpack_up)(ordered(up_pair)).reshape(D, FF)
    w_down, w_out = (a.reshape(-1, D) for a in jax.vmap(unpack_down)(ordered(down_pair)))
    qkv = [a.reshape(D, D) for a in jax.vmap(unpack_qkv)([ordered(p) for p in qkv_pairs])]
    small = [scatter(vec[i]) for i in range(6)]
    return (
        scatter(qkv[0]), scatter(bg[0]), scatter(qkv[1]), scatter(qkv[2]), scatter(bg[1]), scatter(w_out),
        small, scatter(w_up), scatter(vec[8:12].reshape(FF)), scatter(w_down),
    )


def give_back_kernel(seq, here, got_first, got, got_end, long_in, long, middle, short):
    long[0] = jnp.where(pl.program_id(0) == 0, got_first[...], got[...])

    @pl.when(seq[0] == 0)
    def _():
        middle[0] = here[...]
        short[0] = got_end[: short.shape[1], :]

    @pl.when(seq[0] != 0)
    def _():
        middle[0] = got_end[...]
        short[0] = here[: short.shape[1], :]


def give_back(seq, long, here, got, short):
    count, half, _ = long.shape
    mid = here.shape[0]
    mine = count // 2
    return pl.pallas_call(
        give_back_kernel,
        grid_spec=pltpu.PrefetchScalarGridSpec(
            num_scalar_prefetch=1,
            grid=(mine,),
            in_specs=[
                pl.BlockSpec((mid, D), lambda i, s: (0, 0)),
                pl.BlockSpec((half, D), lambda i, s: (0, 0)),
                pl.BlockSpec((half, D), lambda i, s: (jnp.maximum(i - 1, 0), 0)),
                pl.BlockSpec((mid, D), lambda i, s: ((mine - 1) * half // mid, 0)),
                ANY,
            ],
            out_specs=[
                pl.BlockSpec((1, half, D), lambda i, s: (mine * (1 - s[0]) + i, 0, 0)),
                pl.BlockSpec((1, mid, D), lambda i, s: (0, 0, 0)),
                pl.BlockSpec((1, short, D), lambda i, s: (0, 0, 0)),
            ],
        ),
        out_shape=[SDS(long.shape, bf16), SDS((1, mid, D), bf16), SDS((1, short, D), bf16)],
        input_output_aliases={5: 0},
        compiler_params=pltpu.CompilerParams(vmem_limit_bytes=SMALL_LIMIT),
        cost_estimate=LONG,
        name="add_halves",
    )(seq, here, got[0], got[1], got[1], long)


def per_device(
    tokens_short, tokens_middle, tokens_long, length_short, length_middle, length_long,
    query_weight, query_bias, key_weight, value_weight, value_bias, output_weight, output_bias,
    attention_gain, attention_shift, up_weight, up_bias, down_weight, down_bias, output_gain, output_shift,
    upstream_short, upstream_middle, upstream_long,
):
    seq = lax.axis_index("seq")
    first = seq == 0
    device = (lax.axis_index("dp") * 2 + seq).astype(jnp.int32)
    fast = lax.axis_size("dp") * lax.axis_size("seq") == BLOCKS
    me = device if fast else jnp.int32(0)
    me_ref = me.reshape(1)
    count, half, _ = tokens_long.shape
    mine = count // 2
    mid = tokens_middle.shape[1]
    short = tokens_short.shape[1]
    lengths = (2 * half,) * mine + (2 * mid,)
    tokens = sum(lengths)
    rows = 2 * half * (mine + 1)

    def own_rows(v):
        return lax.dynamic_slice_in_dim(v, mine * seq, mine, 0)

    def other_rows(v):
        return lax.dynamic_slice_in_dim(v, mine * (1 - seq), mine, 0)

    def middle_rows(middle, low):
        low = jnp.pad(low[0], ((0, mid - short), (0, 0)))
        return jnp.where(first, middle[0], low), jnp.where(first, low, middle[0])

    x_mid, x_mid_out = middle_rows(tokens_middle, tokens_short)
    x_mid_in = swap_seq(x_mid_out)
    x_own, x_out = own_rows(tokens_long), other_rows(tokens_long)
    x_in = [swap_seq(later(x_out[0], x_mid_in))]
    u_mid, u_mid_out = middle_rows(upstream_middle, upstream_short)
    u_out = jnp.concatenate([other_rows(upstream_long).reshape(mine * half, D), u_mid_out], axis=0)

    place = (seq.astype(jnp.int32).reshape(1), length_short, length_middle, length_long)
    qkv = [query_weight, key_weight, value_weight]
    projections = qkv + [query_bias, value_bias]
    chain = attention_forward(place, x_mid, x_mid_in, projections, mine, 2 * mid, mine * half // mid, None, rows)
    x_in += [swap_seq(later(x_out[i], chain[5])) for i in range(1, mine)]
    for i in range(mine):
        chain = attention_forward(place, x_own[i], x_in[i], projections, i, 2 * half, i, chain, rows)
    x, q, k, v, ctx, lse, xt = chain
    u_in = swap_seq(later(u_out, lse))

    mats = [output_weight, up_weight, down_weight]
    dense = functools.partial(
        dense_steps, place[0], ctx, x, tokens=tokens, rows=rows, mats=mats,
        vecs=[up_bias, output_bias, attention_gain, attention_shift, down_bias, output_gain, output_shift],
    )
    res_long, *before = dense(ups=[upstream_long], before=None)
    res_other, res_mid, act, dinn, nlow, dbr, datt, dr1, dctx, vec = dense(ups=[u_in, u_in, u_mid], before=before)

    up_pair = up_grad(me_ref, nlow, dinn, tokens)
    part = half
    res_got = [swap_seq(later(res_other[:part], up_pair[0]))]
    down_pair = down_grad(later(me_ref, up_pair[0]), act, dbr, ctx, datt, vec, tokens)
    res_got[0] = later(res_got[0], down_pair[0])
    res_got.append(swap_seq(later(res_other[part:], res_got[0])))

    def at(before, *sums, done=()):
        going = [v for h in sums for v in h.outgoing] if fast else []
        return (later(place[0], before, *going, *done), *place[1:])

    up = down = all_sum = ()
    if fast:
        up = across_cores(
            up_pair, down_pair[0], [[(2304, 0)], [(2304, 1)]], [["z", "x", "y", "w"], ["y", "x", "z", "w"]]
        )
        send(*up)
    *before, ig_long, ig_other = first_row_backward(
        at(down_pair[0], *up), q, k, v, dctx, lse, dr1, qkv, 2 * half
    )
    if fast:
        for h in up:
            h.receive(ig_other)
        down = across_cores(
            down_pair, ig_other, [[(2944, 0)], [(2944, 1)]], [["z", "y", "x", "w"], ["y", "z", "x", "w"]]
        )
        send(*up, *down)
    res_got[1] = later(res_got[1], ig_other)
    later_rows = (2 * half, 2 * mid)
    *wide, leaving, keep, bg = group_backward(
        me_ref, at(ig_other, *up, *down, done=res_got), q, k, v, dctx, lse, before, xt, later_rows, 4, 0, None
    )
    wide_pair = (leaving, keep)
    if fast:
        for h in (*up, *down):
            h.receive(bg)
        send(*up, *down)
    ig_got = [swap_seq(later(ig_other, bg))]
    *narrow, leaving, keep, bg_last = group_backward(
        me_ref, at(bg, *up, *down), q, k, v, dctx, lse, before, xt, later_rows, 2, 4, bg
    )
    narrow_pair = (leaving, keep)
    ig_got[0] = later(ig_got[0], bg_last)
    if fast:
        for h in (*up, *down):
            h.receive(bg_last)
        up = (join(*up),)
        down = (join(*down),)
        send(*up, *down)
        wide_sum = across_cores(wide_pair, bg_last, [[(2304, 0)]], [["yz", "xw"]])
        narrow_sum = across_cores(narrow_pair, up[0].outgoing[0], [[(1152, 0), (128, 9)]], [["yz", "xw"]])
        all_sum = (join(*wide_sum, *narrow_sum),)
        send(*all_sum)
    ig_long, ig_mid, ig_rest = input_grad(
        at(bg_last, *up, *down, *all_sum)[0], later(dr1, ig_got[0]), [wide, narrow], [(0, 512), (512, 768)], qkv, later_rows, ig_long
    )
    ig_got.append(swap_seq(ig_rest))
    if fast:
        up[0].receive(ig_rest)
        down[0].receive(ig_rest)
        send(*down)
        all_sum[0].receive(down[0].outgoing[0])
        send(*all_sum)
        spare = all_sum[0].outgoing[0]
    else:
        spare = ig_rest
    res_long, res_middle, res_short = give_back(
        later(place[0], spare), res_long, res_mid, res_got, short
    )
    ig_long, ig_middle, ig_short = give_back(place[0], ig_long, ig_mid, ig_got, short)
    if fast:
        down[0].receive()
        w_up, w_down, w_out, small = last_sums(
            last_dense_kernel, later(place[0], spare), [*up, *down], [(24, FF), (96, D), (24, D), (16, 128)], []
        )
        all_sum[0].receive(ig_middle)
        w_query, w_key, w_value, ends = last_sums(
            last_qkv_kernel, place[0], all_sum, [(24, D)] * 3 + [(16, 128)], [(24, 3 * D)]
        )
        b_up = lax.dynamic_slice(small, (8 + (me >> 3), 0), (1, 96))[0]
        done = w_query, ends[0, :24], w_key, w_value, ends[1, :24], w_out, small[:8, :24], w_up, b_up, w_down
    else:
        done = reduce_plain(up_pair, down_pair, [wide_pair, narrow_pair], vec, jnp.concatenate([bg, bg_last], axis=1))
    results = (res_short, res_middle, res_long)
    input_grads = (ig_short, ig_middle, ig_long)
    w_query, bq, w_key, w_value, bv, w_out, small, w_up, b_up, w_down = done
    return (
        *results, *input_grads,
        w_query, bq, w_key, w_value, bv, w_out, small[5], small[3], small[4],
        w_up, b_up, w_down, small[2], small[0], small[1],
    )


def solution(mesh):
    tokens = P("dp", "seq", None)
    wide = P(("dp", "seq"), None)
    flat = P(("dp", "seq"))
    in_specs = (tokens,) * 3 + (P("dp"),) * 3 + (P(),) * 15 + (tokens,) * 3
    out_specs = (tokens,) * 6 + (
        wide, flat, wide, wide, flat, wide, flat, flat, flat, wide, flat, wide, flat, flat, flat,
    )
    return jax.shard_map(per_device, mesh=mesh, in_specs=in_specs, out_specs=out_specs, check_vma=False)
```

```python
import functools

import jax
import jax.numpy as jnp
from jax import lax
from jax.experimental import pallas as pl
from jax.experimental.pallas import tpu as pltpu
from jax.sharding import PartitionSpec as P

D = 768
FF = 3072
HEADS = 12
PAIRS = HEADS // 2
EPS = 1e-12
NEG = -1e30
SHORT_HALF = 64
BLOCKS = 32
VMEM_LIMIT = 60 * 2**20
SMALL_LIMIT = 12 * 2**20

bf16 = jnp.bfloat16
f32 = jnp.float32
SDS = jax.ShapeDtypeStruct
ANY = pl.BlockSpec(memory_space=pl.ANY)
LONG = pl.CostEstimate(flops=4 * 10**10, bytes_accessed=10**8, transcendentals=0)


def dot(a, b):
    return lax.dot_general(a, b, (((1,), (0,)), ((), ())), preferred_element_type=f32)


def dot_nt(a, b):
    return lax.dot_general(a, b, (((1,), (1,)), ((), ())), preferred_element_type=f32)


def dot_tn(a, b):
    return lax.dot_general(a, b, (((0,), (0,)), ((), ())), preferred_element_type=f32)


def wide(vector):
    return vector[...].reshape(1, -1)


def mean(v):
    return jnp.mean(v, axis=-1, keepdims=True)


def column_sum(v):
    return jnp.sum(v.astype(f32), axis=0, keepdims=True)


A1, A2, A3, A4, A5 = 0.254829592, -0.284496736, 1.421413741, -1.453152027, 1.061405429
P_SCALED = 0.3275911 * 0.7071067811865476
INV_SQRT_2PI = 0.3989422804014327


def gelu_and_slope(v):
    t = 1.0 / (1.0 + P_SCALED * jnp.abs(v))
    e = jnp.exp(v * v * -0.5)
    tail = t * (A1 + t * (A2 + t * (A3 + t * (A4 + t * A5)))) * (0.5 * e)
    cdf = jnp.where(v < 0, tail, 1.0 - tail)
    return v * cdf, cdf + v * (e * INV_SQRT_2PI)


def mask_column(place, row, length):
    seq, short, middle, long = place
    half = length // 2
    mine = long.shape[0] // 2
    s = seq[0]
    if row < mine:
        count, valid, own, other = long[mine * s + row], half, half * s, half * (1 - s)
    else:
        is_first = s == 0
        count = jnp.where(is_first, middle[0], short[0])
        valid = jnp.where(is_first, half, SHORT_HALF)
        own, other = jnp.where(is_first, 0, SHORT_HALF), jnp.where(is_first, half, 0)
    i = lax.broadcasted_iota(jnp.int32, (length, 1), 0)
    inner = jnp.where(i < half, i, i - half)
    live = (inner + jnp.where(i < half, own, other) < count) & (inner < valid)
    return jnp.where(live, 0.0, NEG).astype(f32)


def low_lanes():
    return lax.broadcasted_iota(jnp.int32, (1, 128), 1) < 64


def stack_heads(pair, low):
    zero = jnp.zeros_like(pair)
    return jnp.concatenate([jnp.where(low, pair, zero), jnp.where(low, zero, pair)], axis=0)


def split_rows(pair_t):
    row = lax.broadcasted_iota(jnp.int32, (128, 1), 0) < 64
    zero = jnp.zeros_like(pair_t)
    return jnp.where(row, pair_t, zero), jnp.where(row, zero, pair_t)


def scaled(q):
    return (q.astype(f32) * 0.125).astype(bf16)


def emit_24(scr, lane, d, out, r, base):
    for g in range(3):
        rows = pl.ds(pl.multiple_of(24 * d + 8 * g, 8), 8)
        both = jnp.concatenate(
            [scr[rows, lane : lane + 384], scr[rows, lane + 384 : lane + 768]], axis=0
        )
        out[r, :, base + 384 * g : base + 384 * (g + 1)] = both.astype(bf16)


def block_number(half, r):
    return ((r >> 1) << 2) | (half << 1) | (r & 1)


def forward_kernel(s0, s1, s2, s3, xl, xr, wq, wk, wv, bq, bv, *rest, length, row, chained):
    x_o, q_o, k_o, v_o, c_o, lse_o, xt_o = rest[7:] if chained else rest
    x = jnp.concatenate([xl[...], xr[...]], axis=0)
    x_o[...] = x
    xt_o[...] = x.T
    q_o[...] = (dot(x, wq[...]) + wide(bq)).astype(bf16)
    k_o[...] = dot(x, wk[...]).astype(bf16)
    v_o[...] = (dot(x, wv[...]) + wide(bv)).astype(bf16)
    bias = mask_column((s0, s1, s2, s3), row, length)
    low = low_lanes()
    row_low = lax.broadcasted_iota(jnp.int32, (128, 1), 0) < 64
    for p in range(PAIRS):
        sl = slice(128 * p, 128 * p + 128)
        scores = dot_nt(stack_heads(k_o[:, sl], low), scaled(q_o[:, sl]))
        parts = []
        inverse = []
        for h in range(2):
            s = scores[h * length : (h + 1) * length, :] + bias
            top = jnp.max(s, axis=0, keepdims=True)
            raised = jnp.exp(s - top)
            total = jnp.sum(raised, axis=0, keepdims=True)
            lse_o[2 * p + h : 2 * p + h + 1, 0:length] = top + jnp.log(total)
            parts.append(raised.astype(bf16))
            inverse.append(1.0 / total)
        upper, lower = split_rows(v_o[:, sl].T)
        context = dot(upper, parts[0]) + dot(lower, parts[1])
        context = context * jnp.where(row_low, inverse[0], inverse[1])
        c_o[:, sl] = context.T.astype(bf16)


def attention_forward(place, own, other, weights, row, length, block, chain, rows):
    half = pl.BlockSpec((length // 2, D), lambda i: (0, 0))
    full = lambda a: pl.BlockSpec(a.shape, lambda i: (0,) * a.ndim)
    tok = pl.BlockSpec((length, D), lambda i: (block, 0))
    lse = pl.BlockSpec((16, 512), lambda i: (row, 0))
    turned = pl.BlockSpec((D, length), lambda i: (0, block))
    chained = chain is not None
    extra = list(chain) if chained else []
    return pl.pallas_call(
        functools.partial(forward_kernel, length=length, row=row, chained=chained),
        grid=(1,),
        in_specs=[pl.BlockSpec(memory_space=pltpu.SMEM)] * 4
        + [half, half]
        + [full(w) for w in weights]
        + [ANY] * len(extra),
        out_specs=[tok] * 5 + [lse, turned],
        out_shape=[SDS((rows, D), bf16)] * 5 + [SDS((48, 512), f32), SDS((D, rows), bf16)],
        input_output_aliases={11 + i: i for i in range(7)} if chained else {},
        compiler_params=pltpu.CompilerParams(vmem_limit_bytes=57 * 2**20),
        cost_estimate=LONG,
        name=f"attend_{row}",
    )(*place, own, other, *weights, *extra)


def drop_first(kernel):
    return lambda _, *refs, **options: kernel(*refs, **options)


def dense_kernel(*refs, chunks, own):
    ctx, x = refs[0], refs[1]
    step = pl.program_id(0)
    last = step == pl.num_programs(0) - 1
    if own:
        up_refs, refs = refs[2:3], refs[3:]
        up = up_refs[0][0]
    else:
        up_refs, refs = refs[2:5], refs[5:]
        up = jnp.concatenate([jnp.where(last, up_refs[2][...], up_refs[0][...]), up_refs[1][...]], axis=0)
    wo, wup, wdn, bup, bo, g1, s1, bdn, g2, s2 = refs[:10]
    bup, bo, g1, s1, bdn, g2, s2 = (wide(v) for v in (bup, bo, g1, s1, bdn, g2, s2))
    if own:
        res_own, act, dinn, nlow_o, dbr, datt, dr1_o, dctx, vec, slope_s = refs[10:]
    else:
        vec_in = refs[10]
        res_first, res_rest, res_mid, act, dinn, nlow_o, dbr, datt, dr1_o, dctx, vec, slope_s = refs[18:]

    @pl.when(step == 0)
    def _():
        vec[...] = jnp.zeros_like(vec) if own else vec_in[...]

    r1 = x[...].astype(f32) + dot(ctx[...], wo[...]) + bo
    c1 = r1 - mean(r1)
    rs1 = lax.rsqrt(mean(c1 * c1) + EPS)
    n1 = c1 * rs1
    normed = n1 * g1 + s1
    nlow = normed.astype(bf16)
    nlow_o[...] = nlow
    acc = normed + bdn
    width = FF // chunks
    for j in range(chunks):
        sl = slice(j * width, (j + 1) * width)
        value, slope = gelu_and_slope(dot(nlow, wup[:, sl]) + bup[:, sl])
        value = value.astype(bf16)
        act[:, sl] = value
        slope_s[:, sl] = slope
        acc = acc + dot(value, wdn[sl, :])
    c2 = acc - mean(acc)
    rs2 = lax.rsqrt(mean(c2 * c2) + EPS)
    n2 = c2 * rs2
    result = (n2 * g2 + s2).astype(bf16)
    if own:
        res_own[0] = result
    else:
        size = result.shape[0]

        @pl.when(step == 0)
        def _():
            res_first[...] = result

        @pl.when((step > 0) & jnp.logical_not(last))
        def _():
            res_rest[pl.ds(pl.multiple_of((step - 1) * size, size), size), :] = result

        @pl.when(last)
        def _():
            res_mid[...] = result[: size // 2]
            res_rest[res_rest.shape[0] - size // 2 :, :] = result[size // 2 :]

    upstream = up.astype(f32)
    u = upstream * g2
    dr2 = (u - mean(u) - n2 * mean(u * n2)) * rs2
    branch = dr2.astype(bf16)
    dbr[...] = branch
    vec[0:1, :] += column_sum(upstream * n2)
    vec[1:2, :] += column_sum(upstream)
    vec[2:3, :] += column_sum(branch)
    acc = dr2
    for j in range(chunks):
        sl = slice(j * width, (j + 1) * width)
        d_inner = (dot_nt(branch, wdn[sl, :]) * slope_s[:, sl]).astype(bf16)
        dinn[:, sl] = d_inner
        vec[8 + j : 9 + j, :] += column_sum(d_inner)
        acc = acc + dot_nt(d_inner, wup[:, sl])
    vec[3:4, :] += column_sum(acc * n1)
    vec[4:5, :] += column_sum(acc)
    u1 = acc * g1
    d1 = (u1 - mean(u1) - n1 * mean(u1 * n1)) * rs1
    d_attn = d1.astype(bf16)
    datt[...] = d_attn
    dr1_o[...] = d1
    vec[5:6, :] += column_sum(d_attn)
    dctx[...] = dot_nt(d_attn, wo[...]).astype(bf16)


def dense_steps(seq, ctx, x, ups, mats, vecs, tokens, rows, before):
    tile = 256
    half = tile // 2
    mine = tokens // tile // 2
    own = before is None
    full = lambda a: pl.BlockSpec(a.shape, lambda i, s: (0,) * a.ndim, pipeline_mode=pl.Buffered(1))
    whole = lambda n: pl.BlockSpec((n, D), lambda i, s: (0, 0))
    if own:
        place = lambda i: 2 * i
        steps = mine
        up_specs = [pl.BlockSpec((1, tile, D), lambda i, s: (s[0] * mine + i, 0, 0))]
        res_specs = [pl.BlockSpec((1, tile, D), lambda i, s: (s[0] * mine + i, 0, 0))]
        res_shapes = [SDS((2 * mine, tile, D), bf16)]
        extra, extra_specs, aliases = [], [], {}
    else:
        place = lambda i: jnp.minimum(2 * i + 1, 2 * mine)
        steps = mine + 1
        up_specs = [
            pl.BlockSpec((half, D), lambda i, s: (jnp.minimum(2 * i, 2 * mine - 2), 0)),
            pl.BlockSpec((half, D), lambda i, s: (jnp.minimum(2 * i + 1, 2 * mine), 0)),
            whole(half),
        ]
        sizes = (tile, tokens // 2 - tile, half)
        res_specs = [whole(n) for n in sizes]
        res_shapes = [SDS((n, D), bf16) for n in sizes]
        *arrays, vec = before
        extra = [vec] + arrays
        extra_specs = [whole(16)] + [ANY] * len(arrays)
        first = 1 + 2 + len(ups) + len(mats) + len(vecs) + 1
        aliases = {first + i: 3 + i for i in range(len(arrays))}
    tok = pl.BlockSpec((tile, D), lambda i, s: (place(i), 0))
    ffs = pl.BlockSpec((tile, FF), lambda i, s: (place(i), 0))
    return pl.pallas_call(
        functools.partial(drop_first(dense_kernel), chunks=4, own=own),
        grid_spec=pltpu.PrefetchScalarGridSpec(
            num_scalar_prefetch=1,
            grid=(steps,),
            in_specs=[tok, tok] + up_specs + [full(a) for a in mats + vecs] + extra_specs,
            out_specs=res_specs + [ffs, ffs] + [tok] * 5 + [whole(16)],
            scratch_shapes=[pltpu.VMEM((tile, FF), f32)],
        ),
        out_shape=res_shapes
        + [SDS((tokens, FF), bf16)] * 2
        + [SDS((tokens, D), bf16)] * 3
        + [SDS((rows, D), f32), SDS((rows, D), bf16), SDS((16, D), f32)],
        input_output_aliases=aliases,
        compiler_params=pltpu.CompilerParams(vmem_limit_bytes=VMEM_LIMIT),
        cost_estimate=LONG,
        name="dense_own" if own else "dense_rest",
    )(seq, ctx, x, *ups, *mats, *vecs, *extra)


def up_grad_kernel(me, nlow, left, right, send, keep, turned, scr):

    @pl.when(pl.program_id(0) == 0)
    def _():
        turned[...] = nlow[...].T

    scr[:, 0:384] = dot(turned[...], left[...])
    scr[:, 384:768] = dot(turned[...], right[...])
    for half, out in ((0, keep), (1, send)):
        for r in range(16):
            emit_24(scr, 0, block_number(half, r) ^ me[0], out, r, 0)


def up_grad(me, nlow, dinn, tokens):
    out = pl.BlockSpec((16, 16, 1152), lambda j, m: (0, 0, j))
    return pl.pallas_call(
        up_grad_kernel,
        grid_spec=pltpu.PrefetchScalarGridSpec(
            num_scalar_prefetch=1,
            grid=(4,),
            in_specs=[
                pl.BlockSpec((tokens, D), lambda j, m: (0, 0)),
                pl.BlockSpec((tokens, 384), lambda j, m: (0, j)),
                pl.BlockSpec((tokens, 384), lambda j, m: (0, j + 4)),
            ],
            out_specs=[out, out],
            scratch_shapes=[pltpu.VMEM((D, tokens), bf16), pltpu.VMEM((D, D), f32)],
        ),
        out_shape=[SDS((16, 16, 4608), bf16)] * 2,
        compiler_params=pltpu.CompilerParams(vmem_limit_bytes=VMEM_LIMIT),
        cost_estimate=LONG,
        name="up_grad",
    )(me, nlow, dinn, dinn)


DOWN_WIDTH = 4608 + 1152 + 128


def down_grad_kernel(me, act, dbr, ctx, datt, vec, send, keep, scr, wo_s):
    j = pl.program_id(0)

    @pl.when(j == 0)
    def _():
        wo_s[...] = dot_tn(ctx[...], datt[...])

    scr[...] = dot_tn(act[...], dbr[...])
    z = j ^ (me[0] >> 3)
    for half, out in ((0, keep), (1, send)):
        for r in range(4):
            near = block_number(half, r) ^ (me[0] & 7)
            d = z * 8 + near
            for g in range(6):
                rows = pl.ds(pl.multiple_of(96 * near + 16 * g, 16), 16)
                out[r, :, D * g : D * (g + 1)] = scr[rows, :].astype(bf16)
            emit_24(wo_s, 0, d, out, r, 4608)
            small = pltpu.roll(vec[0:8, :], lax.rem(D - 24 * d, D), 1)[:, 0:128]
            wide = pltpu.roll(vec[8:16, :], lax.rem(D - 96 * near, D), 1)[:, 0:128]
            out[r, :, 5760:5888] = jnp.concatenate([small, wide], axis=0).astype(bf16)


def down_grad(me, act, dbr, ctx, datt, vec, tokens):
    out = pl.BlockSpec((4, 16, DOWN_WIDTH), lambda j, m: (j, 0, 0))
    tok = pl.BlockSpec((tokens, D), lambda j, m: (0, 0))
    return pl.pallas_call(
        down_grad_kernel,
        grid_spec=pltpu.PrefetchScalarGridSpec(
            num_scalar_prefetch=1,
            grid=(4,),
            in_specs=[
                pl.BlockSpec((tokens, D), lambda j, m: (0, j ^ (m[0] >> 3))),
                tok,
                tok,
                tok,
                pl.BlockSpec((16, D), lambda j, m: (0, 0)),
            ],
            out_specs=[out, out],
            scratch_shapes=[pltpu.VMEM((D, D), f32), pltpu.VMEM((D, D), f32)],
        ),
        out_shape=[SDS((16, 16, DOWN_WIDTH), bf16)] * 2,
        compiler_params=pltpu.CompilerParams(vmem_limit_bytes=VMEM_LIMIT),
        cost_estimate=LONG,
        name="down_grad",
    )(me, act, dbr, ctx, datt, vec)


def backward_pairs(pairs, place, row, length, q_r, k_r, v_r, g_r, lse, first, dq_o, dk_o, dv_o):
    n = slice(0, length)
    bias = mask_column(place, row, length)
    low = low_lanes()
    for p in range(pairs):
        sl = slice(128 * p, 128 * p + 128)
        q2 = scaled(q_r[n, sl])
        k2 = k_r[n, sl]
        g2 = g_r[n, sl]
        scores = dot_nt(stack_heads(k2, low), q2)
        d_probs = dot_nt(stack_heads(v_r[n, sl], low), g2)
        probs_low = []
        d_scores = []
        for h in range(2):
            part = slice(h * length, (h + 1) * length)
            head = 2 * (first + p) + h
            probs = jnp.exp(scores[part, :] + bias - lse[head : head + 1, n])
            d_part = d_probs[part, :]
            centre = jnp.sum(probs * d_part, axis=0, keepdims=True)
            probs_low.append(probs.astype(bf16))
            d_scores.append((probs * (d_part - centre)).astype(bf16))
        dv_o[n, sl] = jnp.where(low, dot(probs_low[0], g2), dot(probs_low[1], g2)).astype(bf16)
        dk_o[n, sl] = jnp.where(low, dot(d_scores[0], q2), dot(d_scores[1], q2)).astype(bf16)
        upper, lower = split_rows(k2.T)
        turned = dot(upper, d_scores[0]) + dot(lower, d_scores[1])
        dq_o[n, sl] = (turned * 0.125).T.astype(bf16)


def first_row_kernel(s0, s1, s2, s3, q_r, k_r, v_r, g_r, lse, dr1, wq, wk, wv, dq, dk, dv, ig_own, ig_other, *, length):
    backward_pairs(PAIRS, (s0, s1, s2, s3), 0, length, q_r, k_r, v_r, g_r, lse, 0, dq, dk, dv)
    ig = dr1[...] + dot_nt(dq[...], wq[...]) + dot_nt(dk[...], wk[...]) + dot_nt(dv[...], wv[...])
    ig = ig.astype(bf16)
    ig_own[0] = ig[: length // 2]
    ig_other[...] = ig[length // 2 :]


def first_row_backward(place, q, k, v, dctx, lse, dr1, weights, length):
    tok = pl.BlockSpec((length, D), lambda i, *_: (0, 0))
    half = length // 2
    mine = place[3].shape[0] // 2
    full = pl.BlockSpec((D, D), lambda i, *_: (0, 0))
    return pl.pallas_call(
        functools.partial(first_row_kernel, length=length),
        grid_spec=pltpu.PrefetchScalarGridSpec(
            num_scalar_prefetch=4,
            grid=(1,),
            in_specs=[tok] * 4 + [pl.BlockSpec((16, 512), lambda i, *_: (0, 0)), tok] + [full] * 3,
            out_specs=[tok] * 3
            + [
                pl.BlockSpec((1, half, D), lambda i, s, *_: (mine * s[0], 0, 0)),
                pl.BlockSpec((half, D), lambda i, *_: (0, 0)),
            ],
        ),
        out_shape=[SDS((length, D), bf16)] * 3 + [SDS((2 * mine, half, D), bf16), SDS((half, D), bf16)],
        compiler_params=pltpu.CompilerParams(vmem_limit_bytes=VMEM_LIMIT),
        cost_estimate=LONG,
        name="back_first",
    )(*place, q, k, v, dctx, lse, dr1, *weights)


def group_kernel(me, s0, s1, s2, s3, q_r, k_r, v_r, g_r, lse, dq0, dk0, dv0, xt, *rest, lengths, pairs, first, final):
    if final:
        bg_before, rest = rest[0], rest[1:]
    dq, dk, dv, send, keep, bg, every, dw = rest
    width = 128 * pairs
    long, mid = lengths
    step = pl.program_id(0)

    @pl.when(step == 0)
    def _():
        backward_pairs(pairs, (s0, s1, s2, s3), 1, long, q_r, k_r, v_r, g_r, lse, first, dq, dk, dv)
        for a, (old, new) in enumerate(((dq0, dq), (dk0, dk), (dv0, dv))):
            lanes = slice(a * width, (a + 1) * width)
            every[0:long, lanes] = old[...]
            every[long : 2 * long, lanes] = new[...]

    @pl.when(step == 1)
    def _():
        backward_pairs(pairs, (s0, s1, s2, s3), 2, mid, q_r, k_r, v_r, g_r, lse, first, dq, dk, dv)
        for a, new in enumerate((dq, dk, dv)):
            every[2 * long : 2 * long + mid, a * width : (a + 1) * width] = new[0:mid, :]
        count = 2 * long + mid
        for c in range(3 * width // D):
            dw[:, D * c : D * (c + 1)] = dot(xt[:, 0:count], every[:, D * c : D * (c + 1)])
        bg[...] = jnp.zeros_like(bg)
        bg[0:1, :] = column_sum(every[:, 0:width])
        bg[1:2, :] = column_sum(every[:, 2 * width : 3 * width])
        if final:
            sums = jnp.concatenate([bg_before[...], bg[...]], axis=1)
        for half, out in ((0, keep), (1, send)):
            for r in range(16):
                d = block_number(half, r) ^ me[0]
                for c in range(3 * width // D):
                    emit_24(dw, D * c, d, out, r, 1152 * c)
                if final:
                    small = pltpu.roll(sums, lax.rem(D - 24 * d, D), 1)[:, 0:128]
                    small = jnp.concatenate([small, small], axis=0)
                    out[r, :, 1152 * (3 * width // D) :] = small.astype(bf16)


def group_backward(me, place, q, k, v, dctx, lse, before, xt, lengths, pairs, first, bg_before):
    final = bg_before is not None
    width = 128 * pairs
    column = first // pairs
    long, mid = lengths
    count = 2 * long + mid
    tok = pl.BlockSpec((long, width), lambda i, *_: (1 + i, column))
    old = pl.BlockSpec((long, width), lambda i, *_: (0, column))
    new = pl.BlockSpec((long, width), lambda i, *_: (i, 0))
    size = 3 * width * 24 // 16 + (128 if final else 0)
    out = pl.BlockSpec((16, 16, size), lambda i, *_: (0, 0, 0))
    extra = [bg_before] if final else []
    specs = [pl.BlockSpec(a.shape, lambda i, *_: (0, 0)) for a in extra]
    return pl.pallas_call(
        functools.partial(group_kernel, lengths=lengths, pairs=pairs, first=first, final=final),
        grid_spec=pltpu.PrefetchScalarGridSpec(
            num_scalar_prefetch=5,
            grid=(2,),
            in_specs=[tok] * 4
            + [pl.BlockSpec((16, 512), lambda i, *_: (1 + i, 0))]
            + [old] * 3
            + [pl.BlockSpec(xt.shape, lambda i, *_: (0, 0))]
            + specs,
            out_specs=[new] * 3 + [out, out, pl.BlockSpec((8, width), lambda i, *_: (0, 0))],
            scratch_shapes=[pltpu.VMEM((count, 3 * width), bf16), pltpu.VMEM((D, 3 * width), f32)],
        ),
        out_shape=[SDS((2 * long, width), bf16)] * 3
        + [SDS((16, 16, size), bf16)] * 2
        + [SDS((8, width), f32)],
        compiler_params=pltpu.CompilerParams(vmem_limit_bytes=45 * 2**20),
        cost_estimate=LONG,
        name=f"back_group_{first}",
    )(me, *place, q, k, v, dctx, lse, *before, xt, *extra)


def input_grad_kernel(seq, dr1, *rest, lengths, lanes):
    groups = len(lanes)
    blocks, (wq, wk, wv), (_, own, own_mid, other) = rest[: 3 * groups], rest[3 * groups : 3 * groups + 3], rest[-4:]
    long, mid = lengths
    n = slice(0, long + mid)
    total = dr1[...]
    for a, w in enumerate((wq, wk, wv)):
        for g, (low, high) in enumerate(lanes):
            total = total + dot_nt(blocks[3 * g + a][n, :], w[:, low:high])
    total = total.astype(bf16)
    own[0] = total[0 : long // 2]
    other[0 : long // 2, :] = total[long // 2 : long]
    own_mid[...] = total[long : long + mid // 2]
    other[long // 2 :, :] = total[long + mid // 2 :]


def input_grad(seq, dr1, groups, lanes, weights, lengths, before):
    long, mid = lengths
    flat = [a for g in groups for a in g]
    mine = before.shape[0] // 2
    whole = lambda a: pl.BlockSpec(a.shape, lambda i, s: (0, 0))
    ins = flat + list(weights)
    return pl.pallas_call(
        functools.partial(input_grad_kernel, lengths=lengths, lanes=lanes),
        grid_spec=pltpu.PrefetchScalarGridSpec(
            num_scalar_prefetch=1,
            grid=(1,),
            in_specs=[pl.BlockSpec((pl.Element(long + mid), pl.Element(D)), lambda i, s: (long, 0))]
            + [whole(a) for a in ins]
            + [ANY],
            out_specs=[
                pl.BlockSpec((1, long // 2, D), lambda i, s: (mine * s[0] + 1, 0, 0)),
                pl.BlockSpec((mid // 2, D), lambda i, s: (0, 0)),
                pl.BlockSpec(((long + mid) // 2, D), lambda i, s: (0, 0)),
            ],
        ),
        out_shape=[SDS(before.shape, bf16), SDS((mid // 2, D), bf16), SDS(((long + mid) // 2, D), bf16)],
        input_output_aliases={2 + len(ins): 0},
        compiler_params=pltpu.CompilerParams(vmem_limit_bytes=24 * 2**20),
        cost_estimate=LONG,
        name="input_grad",
    )(seq, dr1, *ins, before)


def swap_seq(v):
    return lax.ppermute(v, "seq", [(0, 1), (1, 0)])


def later(value, *others):
    return lax.optimization_barrier((value, *others))[0]


AXES = {"w": (0, 16), "z": (1, 8), "y": (2, 4), "x": (3, 1)}
CORE = 2


def swap(v, mask):
    return lax.ppermute(v, ("dp", "seq"), [(i, i ^ mask) for i in range(BLOCKS)])


class Payload:
    def __init__(self, groups, order, whole=False):
        self.groups = groups
        self.order = order
        self.whole = whole

    def specs(self, bits):
        todo = {AXES[a][0] for a in "".join(self.order)}
        found = []
        for width, arrays in self.groups:
            for array, lane in arrays:
                shape = tuple(2 if d in todo and d not in bits else 1 for d in range(4))
                index = tuple(bits.get(d, 0) if array.shape[d] == 2 else 0 for d in range(4))
                found.append((array, pl.BlockSpec(shape + (16, width), functools.partial(fixed, index + (0, lane)))))
        return found

    def receive(self, after=None):
        for outgoing, mask in zip(self.outgoing, self.masks):
            received = swap(outgoing, mask)
            if after is not None:
                received = later(received, after)
            low = 0
            for width, arrays in self.groups:
                arrays.append((received, low // width))
                low += width
        return self


def fixed(index, *_):
    return index


def join(*sums):
    return Payload([g for h in sums for g in h.groups], sums[0].order)


def load_sum(refs):
    total = refs[0][...].astype(f32)
    for r in refs[1:]:
        total = total + r[...].astype(f32)
    return total


def add_kernel(*refs, plan):
    outs = refs[len(refs) - len(plan) :]
    at = 0
    for out, groups in zip(outs, plan):
        low = 0
        for count, width in groups:
            out[:, :, :, :, :, low : low + width] = load_sum(refs[at : at + count]).astype(bf16)
            at += count
            low += width


def send(*sums):
    arrays, specs, plan, shapes = [], [], [], []
    for h in sums:
        step, rest = h.order[0], h.order[1:]
        h.masks, h.count = [], 0
        left = {AXES[a][0] for a in "".join(rest)}
        shape = tuple(2 if d in left else 1 for d in range(4)) + (16, sum(g[0] for g in h.groups))
        for which in range(0 if h.whole else 1, 2 ** len(step)):
            bits = {AXES[a][0]: which >> i & 1 for i, a in enumerate(step)}
            h.masks.append(sum(AXES[a][1] for i, a in enumerate(step) if which >> i & 1))
            found = h.specs(bits)
            arrays += [f[0] for f in found]
            specs += [f[1] for f in found]
            plan.append([(len(g[1]), g[0]) for g in h.groups])
            shapes.append(shape)
            h.count += 1
        h.order = rest
    outs = pl.pallas_call(
        functools.partial(add_kernel, plan=plan),
        grid=(1,),
        in_specs=specs,
        out_specs=[pl.BlockSpec(n, functools.partial(fixed, (0,) * 6)) for n in shapes],
        out_shape=[SDS(n, bf16) for n in shapes],
        compiler_params=pltpu.CompilerParams(vmem_limit_bytes=SMALL_LIMIT),
        cost_estimate=LONG,
        name="add_parts",
    )(*arrays)
    at = 0
    for h in sums:
        h.outgoing = outs[at : at + h.count]
        at += h.count
        if h.whole:
            h.whole = False
            stays, h.outgoing, h.masks = h.outgoing[0], h.outgoing[1:], h.masks[1:]
            low = 0
            for n, (width, _) in enumerate(h.groups):
                h.groups[n] = (width, [(stays, low // width)])
                low += width


def across_cores(pair, after, ranges, order):
    leaving, keep = pair
    received = later(swap(leaving, CORE), after)
    both = [v.reshape(2, 2, 2, 2, 16, -1) for v in (keep, received)]
    return [
        Payload([(width, [(v, lane) for v in both]) for width, lane in groups], axes, len(axes[0]) == 1)
        for axes, groups in zip(order, ranges)
    ]


def store_24(block, out, column, lanes=D):
    for g in range(3):
        for t in range(2):
            piece = block[8 * t : 8 * t + 8, 384 * g : 384 * (g + 1)]
            out[8 * g : 8 * g + 8, column + lanes // 2 * t : column + lanes // 2 * t + 384] = piece


def last_dense_kernel(seq, *refs, plan):
    (*ins, w_up, w_down, w_out, small) = refs
    blocks = []
    at = 0
    for count in plan:
        blocks.append(load_sum(ins[at : at + count])[0, 0, 0, 0])
        at += count
    up = jnp.concatenate(blocks[:2], axis=1)
    down = jnp.concatenate(blocks[2:], axis=1)
    for j in range(4):
        store_24(up[:, 1152 * j : 1152 * (j + 1)], w_up, 384 * j, FF)
    for g in range(6):
        w_down[16 * g : 16 * (g + 1), :] = down[:, D * g : D * (g + 1)]
    store_24(down[:, 4608:5760], w_out, 0)
    small[...] = down[:, 5760:5888]


def last_qkv_kernel(seq, *refs, plan):
    (*ins, w_query, w_key, w_value, small, scr) = refs
    blocks = []
    at = 0
    for count in plan:
        blocks.append(load_sum(ins[at : at + count])[0, 0, 0, 0])
        at += count
    left, right, tail = blocks
    for c in range(2):
        store_24(left[:, 1152 * c : 1152 * (c + 1)], scr, D * c)
    store_24(right, scr, 2 * D)
    for a, out in enumerate((w_query, w_key, w_value)):
        out[:, 0:512] = scr[:, 512 * a : 512 * (a + 1)]
        out[:, 512:768] = scr[:, 2 * D + 256 * a : 2 * D + 256 * (a + 1)]
    small[...] = tail


def last_sums(kernel, seq, sums, shapes, scratch):
    found = [f for h in sums for f in h.specs({})]
    plan = [len(g[1]) for h in sums for g in h.groups]
    return pl.pallas_call(
        functools.partial(kernel, plan=plan),
        grid=(1,),
        in_specs=[pl.BlockSpec(memory_space=pltpu.SMEM)] + [f[1] for f in found],
        out_specs=[pl.BlockSpec(n, functools.partial(fixed, (0, 0))) for n in shapes],
        out_shape=[SDS(n, f32) for n in shapes],
        scratch_shapes=[pltpu.VMEM(n, f32) for n in scratch],
        compiler_params=pltpu.CompilerParams(vmem_limit_bytes=SMALL_LIMIT),
        cost_estimate=LONG,
        name="last_sums",
    )(seq, *[f[0] for f in found])


def rows_24(block):
    return block.reshape(2, 8, 3, 384).transpose(2, 1, 0, 3).reshape(24, D)


def unpack_up(block):
    return block.reshape(2, 8, 4, 3, 384).transpose(3, 1, 0, 2, 4).reshape(24, FF)


def unpack_down(block):
    return block[:, :4608].reshape(16, 6, D).transpose(1, 0, 2).reshape(96, D), rows_24(block[:, 4608:5760])


def unpack_qkv(blocks):
    wide, narrow = blocks
    left = jnp.concatenate([rows_24(wide[:, :1152]), rows_24(wide[:, 1152:])], axis=1)
    right = rows_24(narrow[:, :1152])
    return [
        jnp.concatenate([left[:, 512 * a : 512 * (a + 1)], right[:, 256 * a : 256 * (a + 1)]], axis=1) for a in range(3)
    ]


def reduce_plain(up_pair, down_pair, qkv_pairs, vec, bg):
    def ordered(pair):
        send, keep = pair
        both = jnp.stack([keep.reshape(8, 2, 16, -1), send.reshape(8, 2, 16, -1)], axis=1)
        return both.reshape(BLOCKS, 16, -1).astype(f32)

    scatter = lambda v: lax.psum_scatter(v, ("dp", "seq"), scatter_dimension=0, tiled=True)
    w_up = jax.vmap(unpack_up)(ordered(up_pair)).reshape(D, FF)
    w_down, w_out = (a.reshape(-1, D) for a in jax.vmap(unpack_down)(ordered(down_pair)))
    qkv = [a.reshape(D, D) for a in jax.vmap(unpack_qkv)([ordered(p) for p in qkv_pairs])]
    small = [scatter(vec[i]) for i in range(6)]
    return (
        scatter(qkv[0]), scatter(bg[0]), scatter(qkv[1]), scatter(qkv[2]), scatter(bg[1]), scatter(w_out),
        small, scatter(w_up), scatter(vec[8:12].reshape(FF)), scatter(w_down),
    )


def give_back_kernel(seq, here, got_first, got, got_end, long_in, long, middle, short):
    long[0] = jnp.where(pl.program_id(0) == 0, got_first[...], got[...])

    @pl.when(seq[0] == 0)
    def _():
        middle[0] = here[...]
        short[0] = got_end[: short.shape[1], :]

    @pl.when(seq[0] != 0)
    def _():
        middle[0] = got_end[...]
        short[0] = here[: short.shape[1], :]


def give_back(seq, long, here, got, short):
    count, half, _ = long.shape
    mid = here.shape[0]
    mine = count // 2
    return pl.pallas_call(
        give_back_kernel,
        grid_spec=pltpu.PrefetchScalarGridSpec(
            num_scalar_prefetch=1,
            grid=(mine,),
            in_specs=[
                pl.BlockSpec((mid, D), lambda i, s: (0, 0)),
                pl.BlockSpec((half, D), lambda i, s: (0, 0)),
                pl.BlockSpec((half, D), lambda i, s: (jnp.maximum(i - 1, 0), 0)),
                pl.BlockSpec((mid, D), lambda i, s: ((mine - 1) * half // mid, 0)),
                ANY,
            ],
            out_specs=[
                pl.BlockSpec((1, half, D), lambda i, s: (mine * (1 - s[0]) + i, 0, 0)),
                pl.BlockSpec((1, mid, D), lambda i, s: (0, 0, 0)),
                pl.BlockSpec((1, short, D), lambda i, s: (0, 0, 0)),
            ],
        ),
        out_shape=[SDS(long.shape, bf16), SDS((1, mid, D), bf16), SDS((1, short, D), bf16)],
        input_output_aliases={5: 0},
        compiler_params=pltpu.CompilerParams(vmem_limit_bytes=SMALL_LIMIT),
        cost_estimate=LONG,
        name="add_halves",
    )(seq, here, got[0], got[1], got[1], long)


def per_device(
    tokens_short, tokens_middle, tokens_long, length_short, length_middle, length_long,
    query_weight, query_bias, key_weight, value_weight, value_bias, output_weight, output_bias,
    attention_gain, attention_shift, up_weight, up_bias, down_weight, down_bias, output_gain, output_shift,
    upstream_short, upstream_middle, upstream_long,
):
    seq = lax.axis_index("seq")
    first = seq == 0
    device = (lax.axis_index("dp") * 2 + seq).astype(jnp.int32)
    fast = lax.axis_size("dp") * lax.axis_size("seq") == BLOCKS
    me = device if fast else jnp.int32(0)
    me_ref = me.reshape(1)
    count, half, _ = tokens_long.shape
    mine = count // 2
    mid = tokens_middle.shape[1]
    short = tokens_short.shape[1]
    lengths = (2 * half,) * mine + (2 * mid,)
    tokens = sum(lengths)
    rows = 2 * half * (mine + 1)

    def own_rows(v):
        return lax.dynamic_slice_in_dim(v, mine * seq, mine, 0)

    def other_rows(v):
        return lax.dynamic_slice_in_dim(v, mine * (1 - seq), mine, 0)

    def middle_rows(middle, low):
        low = jnp.pad(low[0], ((0, mid - short), (0, 0)))
        return jnp.where(first, middle[0], low), jnp.where(first, low, middle[0])

    x_mid, x_mid_out = middle_rows(tokens_middle, tokens_short)
    x_mid_in = swap_seq(x_mid_out)
    x_own, x_out = own_rows(tokens_long), other_rows(tokens_long)
    x_in = [swap_seq(x_out[0])]
    u_mid, u_mid_out = middle_rows(upstream_middle, upstream_short)
    u_out = jnp.concatenate([other_rows(upstream_long).reshape(mine * half, D), u_mid_out], axis=0)

    place = (seq.astype(jnp.int32).reshape(1), length_short, length_middle, length_long)
    qkv = [query_weight, key_weight, value_weight]
    projections = qkv + [query_bias, value_bias]
    chain = attention_forward(place, x_mid, x_mid_in, projections, mine, 2 * mid, mine * half // mid, None, rows)
    x_in += [swap_seq(later(x_out[i], chain[5])) for i in range(1, mine)]
    for i in range(mine):
        chain = attention_forward(place, x_own[i], x_in[i], projections, i, 2 * half, i, chain, rows)
    x, q, k, v, ctx, lse, xt = chain
    u_in = swap_seq(later(u_out, lse))

    mats = [output_weight, up_weight, down_weight]
    dense = functools.partial(
        dense_steps, place[0], ctx, x, tokens=tokens, rows=rows, mats=mats,
        vecs=[up_bias, output_bias, attention_gain, attention_shift, down_bias, output_gain, output_shift],
    )
    res_long, *before = dense(ups=[upstream_long], before=None)
    res_first, res_rest, res_mid, act, dinn, nlow, dbr, datt, dr1, dctx, vec = dense(ups=[u_in, u_in, u_mid], before=before)

    up_pair = up_grad(me_ref, nlow, dinn, tokens)
    res_got = [swap_seq(later(res_first, up_pair[0]))]
    down_pair = down_grad(later(me_ref, up_pair[0]), act, dbr, ctx, datt, vec, tokens)
    res_got[0] = later(res_got[0], down_pair[0])
    res_got.append(swap_seq(later(res_rest, res_got[0])))

    def at(before, *sums, done=()):
        going = [v for h in sums for v in h.outgoing] if fast else []
        return (later(place[0], before, *going, *done), *place[1:])

    up = down = all_sum = ()
    if fast:
        up = across_cores(
            up_pair, down_pair[0], [[(2304, 0)], [(2304, 1)]], [["z", "x", "y", "w"], ["y", "x", "z", "w"]]
        )
        send(*up)
    *before, ig_long, ig_other = first_row_backward(
        at(down_pair[0], *up), q, k, v, dctx, lse, dr1, qkv, 2 * half
    )
    if fast:
        for h in up:
            h.receive(ig_other)
        down = across_cores(
            down_pair, ig_other, [[(2944, 0)], [(2944, 1)]], [["z", "y", "x", "w"], ["y", "z", "x", "w"]]
        )
        send(*up, *down)
    res_got[1] = later(res_got[1], ig_other)
    later_rows = (2 * half, 2 * mid)
    *wide, leaving, keep, bg = group_backward(
        me_ref, at(ig_other, *up, *down, done=res_got), q, k, v, dctx, lse, before, xt, later_rows, 4, 0, None
    )
    wide_pair = (leaving, keep)
    if fast:
        for h in (*up, *down):
            h.receive(bg)
        send(*up, *down)
    ig_got = [swap_seq(later(ig_other, bg))]
    *narrow, leaving, keep, bg_last = group_backward(
        me_ref, at(bg, *up, *down), q, k, v, dctx, lse, before, xt, later_rows, 2, 4, bg
    )
    narrow_pair = (leaving, keep)
    ig_got[0] = later(ig_got[0], bg_last)
    if fast:
        for h in (*up, *down):
            h.receive(bg_last)
        up = (join(*up),)
        down = (join(*down),)
        send(*up, *down)
        wide_sum = across_cores(wide_pair, bg_last, [[(2304, 0)]], [["yz", "xw"]])
        narrow_sum = across_cores(narrow_pair, up[0].outgoing[0], [[(1152, 0), (128, 9)]], [["yz", "xw"]])
        all_sum = (join(*wide_sum, *narrow_sum),)
        send(*all_sum)
    ig_long, ig_mid, ig_rest = input_grad(
        at(bg_last, *up, *down, *all_sum)[0], later(dr1, ig_got[0]), [wide, narrow], [(0, 512), (512, 768)], qkv, later_rows, ig_long
    )
    ig_got.append(swap_seq(ig_rest))
    if fast:
        up[0].receive(ig_rest)
        down[0].receive(ig_rest)
        send(*down)
        all_sum[0].receive(down[0].outgoing[0])
        send(*all_sum)
        spare = all_sum[0].outgoing[0]
    else:
        spare = ig_rest
    res_long, res_middle, res_short = give_back(
        later(place[0], spare), res_long, res_mid, res_got, short
    )
    ig_long, ig_middle, ig_short = give_back(place[0], ig_long, ig_mid, ig_got, short)
    if fast:
        down[0].receive()
        w_up, w_down, w_out, small = last_sums(
            last_dense_kernel, later(place[0], spare), [*up, *down], [(24, FF), (96, D), (24, D), (16, 128)], []
        )
        all_sum[0].receive(ig_middle)
        w_query, w_key, w_value, ends = last_sums(
            last_qkv_kernel, place[0], all_sum, [(24, D)] * 3 + [(16, 128)], [(24, 3 * D)]
        )
        b_up = lax.dynamic_slice(small, (8 + (me >> 3), 0), (1, 96))[0]
        done = w_query, ends[0, :24], w_key, w_value, ends[1, :24], w_out, small[:8, :24], w_up, b_up, w_down
    else:
        done = reduce_plain(up_pair, down_pair, [wide_pair, narrow_pair], vec, jnp.concatenate([bg, bg_last], axis=1))
    results = (res_short, res_middle, res_long)
    input_grads = (ig_short, ig_middle, ig_long)
    w_query, bq, w_key, w_value, bv, w_out, small, w_up, b_up, w_down = done
    return (
        *results, *input_grads,
        w_query, bq, w_key, w_value, bv, w_out, small[5], small[3], small[4],
        w_up, b_up, w_down, small[2], small[0], small[1],
    )


def solution(mesh):
    tokens = P("dp", "seq", None)
    wide = P(("dp", "seq"), None)
    flat = P(("dp", "seq"))
    in_specs = (tokens,) * 3 + (P("dp"),) * 3 + (P(),) * 15 + (tokens,) * 3
    out_specs = (tokens,) * 6 + (
        wide, flat, wide, wide, flat, wide, flat, flat, flat, wide, flat, wide, flat, flat, flat,
    )
    return jax.shard_map(per_device, mesh=mesh, in_specs=in_specs, out_specs=out_specs, check_vma=False)
```

```python
import functools

import jax
import jax.numpy as jnp
from jax import lax
from jax.experimental import pallas as pl
from jax.experimental.pallas import tpu as pltpu
from jax.sharding import PartitionSpec as P

D = 768
FF = 3072
HEADS = 12
PAIRS = HEADS // 2
EPS = 1e-12
NEG = -1e30
SHORT_HALF = 64
BLOCKS = 32
VMEM_LIMIT = 60 * 2**20
SMALL_LIMIT = 12 * 2**20

bf16 = jnp.bfloat16
f32 = jnp.float32
SDS = jax.ShapeDtypeStruct
ANY = pl.BlockSpec(memory_space=pl.ANY)
LONG = pl.CostEstimate(flops=4 * 10**10, bytes_accessed=10**8, transcendentals=0)


def dot(a, b):
    return lax.dot_general(a, b, (((1,), (0,)), ((), ())), preferred_element_type=f32)


def dot_nt(a, b):
    return lax.dot_general(a, b, (((1,), (1,)), ((), ())), preferred_element_type=f32)


def dot_tn(a, b):
    return lax.dot_general(a, b, (((0,), (0,)), ((), ())), preferred_element_type=f32)


def wide(vector):
    return vector[...].reshape(1, -1)


def mean(v):
    return jnp.mean(v, axis=-1, keepdims=True)


def column_sum(v):
    return jnp.sum(v.astype(f32), axis=0, keepdims=True)


A1, A2, A3, A4, A5 = 0.254829592, -0.284496736, 1.421413741, -1.453152027, 1.061405429
P_SCALED = 0.3275911 * 0.7071067811865476
INV_SQRT_2PI = 0.3989422804014327


def gelu_and_slope(v):
    t = 1.0 / (1.0 + P_SCALED * jnp.abs(v))
    e = jnp.exp(v * v * -0.5)
    tail = t * (A1 + t * (A2 + t * (A3 + t * (A4 + t * A5)))) * (0.5 * e)
    cdf = jnp.where(v < 0, tail, 1.0 - tail)
    return v * cdf, cdf + v * (e * INV_SQRT_2PI)


def mask_column(place, row, length):
    seq, short, middle, long = place
    half = length // 2
    mine = long.shape[0] // 2
    s = seq[0]
    if row < mine:
        count, valid, own, other = long[mine * s + row], half, half * s, half * (1 - s)
    else:
        is_first = s == 0
        count = jnp.where(is_first, middle[0], short[0])
        valid = jnp.where(is_first, half, SHORT_HALF)
        own, other = jnp.where(is_first, 0, SHORT_HALF), jnp.where(is_first, half, 0)
    i = lax.broadcasted_iota(jnp.int32, (length, 1), 0)
    inner = jnp.where(i < half, i, i - half)
    live = (inner + jnp.where(i < half, own, other) < count) & (inner < valid)
    return jnp.where(live, 0.0, NEG).astype(f32)


def low_lanes():
    return lax.broadcasted_iota(jnp.int32, (1, 128), 1) < 64


def stack_heads(pair, low):
    zero = jnp.zeros_like(pair)
    return jnp.concatenate([jnp.where(low, pair, zero), jnp.where(low, zero, pair)], axis=0)


def split_rows(pair_t):
    row = lax.broadcasted_iota(jnp.int32, (128, 1), 0) < 64
    zero = jnp.zeros_like(pair_t)
    return jnp.where(row, pair_t, zero), jnp.where(row, zero, pair_t)


def scaled(q):
    return (q.astype(f32) * 0.125).astype(bf16)


def emit_24(scr, lane, d, out, r, base):
    for g in range(3):
        rows = pl.ds(pl.multiple_of(24 * d + 8 * g, 8), 8)
        both = jnp.concatenate(
            [scr[rows, lane : lane + 384], scr[rows, lane + 384 : lane + 768]], axis=0
        )
        out[r, :, base + 384 * g : base + 384 * (g + 1)] = both.astype(bf16)


def block_number(half, r):
    return ((r >> 1) << 2) | (half << 1) | (r & 1)


def forward_kernel(s0, s1, s2, s3, xl, xr, wq, wk, wv, bq, bv, *rest, length, row, chained):
    x_o, q_o, k_o, v_o, c_o, lse_o, xt_o = rest[7:] if chained else rest
    x = jnp.concatenate([xl[...], xr[...]], axis=0)
    x_o[...] = x
    xt_o[...] = x.T
    q_o[...] = (dot(x, wq[...]) + wide(bq)).astype(bf16)
    k_o[...] = dot(x, wk[...]).astype(bf16)
    v_o[...] = (dot(x, wv[...]) + wide(bv)).astype(bf16)
    bias = mask_column((s0, s1, s2, s3), row, length)
    low = low_lanes()
    row_low = lax.broadcasted_iota(jnp.int32, (128, 1), 0) < 64
    for p in range(PAIRS):
        sl = slice(128 * p, 128 * p + 128)
        scores = dot_nt(stack_heads(k_o[:, sl], low), scaled(q_o[:, sl]))
        parts = []
        inverse = []
        for h in range(2):
            s = scores[h * length : (h + 1) * length, :] + bias
            top = jnp.max(s, axis=0, keepdims=True)
            raised = jnp.exp(s - top)
            total = jnp.sum(raised, axis=0, keepdims=True)
            lse_o[2 * p + h : 2 * p + h + 1, 0:length] = top + jnp.log(total)
            parts.append(raised.astype(bf16))
            inverse.append(1.0 / total)
        upper, lower = split_rows(v_o[:, sl].T)
        context = dot(upper, parts[0]) + dot(lower, parts[1])
        context = context * jnp.where(row_low, inverse[0], inverse[1])
        c_o[:, sl] = context.T.astype(bf16)


def attention_forward(place, own, other, weights, row, length, block, chain, rows):
    half = pl.BlockSpec((length // 2, D), lambda i: (0, 0))
    full = lambda a: pl.BlockSpec(a.shape, lambda i: (0,) * a.ndim)
    tok = pl.BlockSpec((length, D), lambda i: (block, 0))
    lse = pl.BlockSpec((16, 512), lambda i: (row, 0))
    turned = pl.BlockSpec((D, length), lambda i: (0, block))
    chained = chain is not None
    extra = list(chain) if chained else []
    return pl.pallas_call(
        functools.partial(forward_kernel, length=length, row=row, chained=chained),
        grid=(1,),
        in_specs=[pl.BlockSpec(memory_space=pltpu.SMEM)] * 4
        + [half, half]
        + [full(w) for w in weights]
        + [ANY] * len(extra),
        out_specs=[tok] * 5 + [lse, turned],
        out_shape=[SDS((rows, D), bf16)] * 5 + [SDS((48, 512), f32), SDS((D, rows), bf16)],
        input_output_aliases={11 + i: i for i in range(7)} if chained else {},
        compiler_params=pltpu.CompilerParams(vmem_limit_bytes=57 * 2**20),
        cost_estimate=LONG,
        name=f"attend_{row}",
    )(*place, own, other, *weights, *extra)


def drop_first(kernel):
    return lambda _, *refs, **options: kernel(*refs, **options)


def dense_kernel(*refs, chunks, own):
    ctx, x = refs[0], refs[1]
    step = pl.program_id(0)
    last = step == pl.num_programs(0) - 1
    if own:
        up_refs, refs = refs[2:3], refs[3:]
        up = up_refs[0][0]
    else:
        up_refs, refs = refs[2:5], refs[5:]
        up = jnp.concatenate([jnp.where(last, up_refs[2][...], up_refs[0][...]), up_refs[1][...]], axis=0)
    wo, wup, wdn, bup, bo, g1, s1, bdn, g2, s2 = refs[:10]
    bup, bo, g1, s1, bdn, g2, s2 = (wide(v) for v in (bup, bo, g1, s1, bdn, g2, s2))
    if own:
        res_own, act, dinn, nlow_o, dbr, datt, dr1_o, dctx, vec, slope_s = refs[10:]
    else:
        vec_in = refs[10]
        res_first, res_rest, res_mid, act, dinn, nlow_o, dbr, datt, dr1_o, dctx, vec, slope_s = refs[18:]

    @pl.when(step == 0)
    def _():
        vec[...] = jnp.zeros_like(vec) if own else vec_in[...]

    r1 = x[...].astype(f32) + dot(ctx[...], wo[...]) + bo
    c1 = r1 - mean(r1)
    rs1 = lax.rsqrt(mean(c1 * c1) + EPS)
    n1 = c1 * rs1
    normed = n1 * g1 + s1
    nlow = normed.astype(bf16)
    nlow_o[...] = nlow
    acc = normed + bdn
    width = FF // chunks
    for j in range(chunks):
        sl = slice(j * width, (j + 1) * width)
        value, slope = gelu_and_slope(dot(nlow, wup[:, sl]) + bup[:, sl])
        value = value.astype(bf16)
        act[:, sl] = value
        slope_s[:, sl] = slope
        acc = acc + dot(value, wdn[sl, :])
    c2 = acc - mean(acc)
    rs2 = lax.rsqrt(mean(c2 * c2) + EPS)
    n2 = c2 * rs2
    result = (n2 * g2 + s2).astype(bf16)
    if own:
        res_own[0] = result
    else:
        size = result.shape[0]

        @pl.when(step == 0)
        def _():
            res_first[...] = result

        @pl.when((step > 0) & jnp.logical_not(last))
        def _():
            res_rest[pl.ds(pl.multiple_of((step - 1) * size, size), size), :] = result

        @pl.when(last)
        def _():
            res_mid[...] = result[: size // 2]
            res_rest[res_rest.shape[0] - size // 2 :, :] = result[size // 2 :]

    upstream = up.astype(f32)
    u = upstream * g2
    dr2 = (u - mean(u) - n2 * mean(u * n2)) * rs2
    branch = dr2.astype(bf16)
    dbr[...] = branch
    vec[0:1, :] += column_sum(upstream * n2)
    vec[1:2, :] += column_sum(upstream)
    vec[2:3, :] += column_sum(branch)
    acc = dr2
    for j in range(chunks):
        sl = slice(j * width, (j + 1) * width)
        d_inner = (dot_nt(branch, wdn[sl, :]) * slope_s[:, sl]).astype(bf16)
        dinn[:, sl] = d_inner
        vec[8 + j : 9 + j, :] += column_sum(d_inner)
        acc = acc + dot_nt(d_inner, wup[:, sl])
    vec[3:4, :] += column_sum(acc * n1)
    vec[4:5, :] += column_sum(acc)
    u1 = acc * g1
    d1 = (u1 - mean(u1) - n1 * mean(u1 * n1)) * rs1
    d_attn = d1.astype(bf16)
    datt[...] = d_attn
    dr1_o[...] = d1
    vec[5:6, :] += column_sum(d_attn)
    dctx[...] = dot_nt(d_attn, wo[...]).astype(bf16)


def dense_steps(seq, ctx, x, ups, mats, vecs, tokens, rows, before):
    tile = 256
    half = tile // 2
    mine = tokens // tile // 2
    own = before is None
    full = lambda a: pl.BlockSpec(a.shape, lambda i, s: (0,) * a.ndim, pipeline_mode=pl.Buffered(1))
    whole = lambda n: pl.BlockSpec((n, D), lambda i, s: (0, 0))
    if own:
        place = lambda i: 2 * i
        steps = mine
        up_specs = [pl.BlockSpec((1, tile, D), lambda i, s: (s[0] * mine + i, 0, 0))]
        res_specs = [pl.BlockSpec((1, tile, D), lambda i, s: (s[0] * mine + i, 0, 0))]
        res_shapes = [SDS((2 * mine, tile, D), bf16)]
        extra, extra_specs, aliases = [], [], {}
    else:
        place = lambda i: jnp.minimum(2 * i + 1, 2 * mine)
        steps = mine + 1
        up_specs = [
            pl.BlockSpec((half, D), lambda i, s: (jnp.minimum(2 * i, 2 * mine - 2), 0)),
            pl.BlockSpec((half, D), lambda i, s: (jnp.minimum(2 * i + 1, 2 * mine), 0)),
            whole(half),
        ]
        sizes = (tile, tokens // 2 - tile, half)
        res_specs = [whole(n) for n in sizes]
        res_shapes = [SDS((n, D), bf16) for n in sizes]
        *arrays, vec = before
        extra = [vec] + arrays
        extra_specs = [whole(16)] + [ANY] * len(arrays)
        first = 1 + 2 + len(ups) + len(mats) + len(vecs) + 1
        aliases = {first + i: 3 + i for i in range(len(arrays))}
    tok = pl.BlockSpec((tile, D), lambda i, s: (place(i), 0))
    ffs = pl.BlockSpec((tile, FF), lambda i, s: (place(i), 0))
    return pl.pallas_call(
        functools.partial(drop_first(dense_kernel), chunks=4, own=own),
        grid_spec=pltpu.PrefetchScalarGridSpec(
            num_scalar_prefetch=1,
            grid=(steps,),
            in_specs=[tok, tok] + up_specs + [full(a) for a in mats + vecs] + extra_specs,
            out_specs=res_specs + [ffs, ffs] + [tok] * 5 + [whole(16)],
            scratch_shapes=[pltpu.VMEM((tile, FF), f32)],
        ),
        out_shape=res_shapes
        + [SDS((tokens, FF), bf16)] * 2
        + [SDS((tokens, D), bf16)] * 3
        + [SDS((rows, D), f32), SDS((rows, D), bf16), SDS((16, D), f32)],
        input_output_aliases=aliases,
        compiler_params=pltpu.CompilerParams(vmem_limit_bytes=VMEM_LIMIT),
        cost_estimate=LONG,
        name="dense_own" if own else "dense_rest",
    )(seq, ctx, x, *ups, *mats, *vecs, *extra)


def up_grad_kernel(me, nlow, left, right, send, keep, turned, scr):

    @pl.when(pl.program_id(0) == 0)
    def _():
        turned[...] = nlow[...].T

    scr[:, 0:384] = dot(turned[...], left[...])
    scr[:, 384:768] = dot(turned[...], right[...])
    for half, out in ((0, keep), (1, send)):
        for r in range(16):
            emit_24(scr, 0, block_number(half, r) ^ me[0], out, r, 0)


def up_grad(me, nlow, dinn, tokens):
    out = pl.BlockSpec((16, 16, 1152), lambda j, m: (0, 0, j))
    return pl.pallas_call(
        up_grad_kernel,
        grid_spec=pltpu.PrefetchScalarGridSpec(
            num_scalar_prefetch=1,
            grid=(4,),
            in_specs=[
                pl.BlockSpec((tokens, D), lambda j, m: (0, 0)),
                pl.BlockSpec((tokens, 384), lambda j, m: (0, j)),
                pl.BlockSpec((tokens, 384), lambda j, m: (0, j + 4)),
            ],
            out_specs=[out, out],
            scratch_shapes=[pltpu.VMEM((D, tokens), bf16), pltpu.VMEM((D, D), f32)],
        ),
        out_shape=[SDS((16, 16, 4608), bf16)] * 2,
        compiler_params=pltpu.CompilerParams(vmem_limit_bytes=VMEM_LIMIT),
        cost_estimate=LONG,
        name="up_grad",
    )(me, nlow, dinn, dinn)


DOWN_WIDTH = 4608 + 1152 + 128


def down_grad_kernel(me, act, dbr, ctx, datt, vec, send, keep, scr, wo_s):
    j = pl.program_id(0)

    @pl.when(j == 0)
    def _():
        wo_s[...] = dot_tn(ctx[...], datt[...])

    scr[...] = dot_tn(act[...], dbr[...])
    z = j ^ (me[0] >> 3)
    for half, out in ((0, keep), (1, send)):
        for r in range(4):
            near = block_number(half, r) ^ (me[0] & 7)
            d = z * 8 + near
            for g in range(6):
                rows = pl.ds(pl.multiple_of(96 * near + 16 * g, 16), 16)
                out[r, :, D * g : D * (g + 1)] = scr[rows, :].astype(bf16)
            emit_24(wo_s, 0, d, out, r, 4608)
            small = pltpu.roll(vec[0:8, :], lax.rem(D - 24 * d, D), 1)[:, 0:128]
            wide = pltpu.roll(vec[8:16, :], lax.rem(D - 96 * near, D), 1)[:, 0:128]
            out[r, :, 5760:5888] = jnp.concatenate([small, wide], axis=0).astype(bf16)


def down_grad(me, act, dbr, ctx, datt, vec, tokens):
    out = pl.BlockSpec((4, 16, DOWN_WIDTH), lambda j, m: (j, 0, 0))
    tok = pl.BlockSpec((tokens, D), lambda j, m: (0, 0))
    return pl.pallas_call(
        down_grad_kernel,
        grid_spec=pltpu.PrefetchScalarGridSpec(
            num_scalar_prefetch=1,
            grid=(4,),
            in_specs=[
                pl.BlockSpec((tokens, D), lambda j, m: (0, j ^ (m[0] >> 3))),
                tok,
                tok,
                tok,
                pl.BlockSpec((16, D), lambda j, m: (0, 0)),
            ],
            out_specs=[out, out],
            scratch_shapes=[pltpu.VMEM((D, D), f32), pltpu.VMEM((D, D), f32)],
        ),
        out_shape=[SDS((16, 16, DOWN_WIDTH), bf16)] * 2,
        compiler_params=pltpu.CompilerParams(vmem_limit_bytes=VMEM_LIMIT),
        cost_estimate=LONG,
        name="down_grad",
    )(me, act, dbr, ctx, datt, vec)


def backward_pairs(pairs, place, row, length, q_r, k_r, v_r, g_r, lse, first, dq_o, dk_o, dv_o):
    n = slice(0, length)
    bias = mask_column(place, row, length)
    low = low_lanes()
    for p in range(pairs):
        sl = slice(128 * p, 128 * p + 128)
        q2 = scaled(q_r[n, sl])
        k2 = k_r[n, sl]
        g2 = g_r[n, sl]
        scores = dot_nt(stack_heads(k2, low), q2)
        d_probs = dot_nt(stack_heads(v_r[n, sl], low), g2)
        probs_low = []
        d_scores = []
        for h in range(2):
            part = slice(h * length, (h + 1) * length)
            head = 2 * (first + p) + h
            probs = jnp.exp(scores[part, :] + bias - lse[head : head + 1, n])
            d_part = d_probs[part, :]
            centre = jnp.sum(probs * d_part, axis=0, keepdims=True)
            probs_low.append(probs.astype(bf16))
            d_scores.append((probs * (d_part - centre)).astype(bf16))
        dv_o[n, sl] = jnp.where(low, dot(probs_low[0], g2), dot(probs_low[1], g2)).astype(bf16)
        dk_o[n, sl] = jnp.where(low, dot(d_scores[0], q2), dot(d_scores[1], q2)).astype(bf16)
        upper, lower = split_rows(k2.T)
        turned = dot(upper, d_scores[0]) + dot(lower, d_scores[1])
        dq_o[n, sl] = (turned * 0.125).T.astype(bf16)


def first_row_kernel(s0, s1, s2, s3, q_r, k_r, v_r, g_r, lse, dq, dk, dv, *, length):
    backward_pairs(PAIRS, (s0, s1, s2, s3), 0, length, q_r, k_r, v_r, g_r, lse, 0, dq, dk, dv)


def first_row_backward(place, q, k, v, dctx, lse, length):
    tok = pl.BlockSpec((length, D), lambda i, *_: (0, 0))
    return pl.pallas_call(
        functools.partial(first_row_kernel, length=length),
        grid_spec=pltpu.PrefetchScalarGridSpec(
            num_scalar_prefetch=4,
            grid=(1,),
            in_specs=[tok] * 4 + [pl.BlockSpec((16, 512), lambda i, *_: (0, 0))],
            out_specs=[tok] * 3,
        ),
        out_shape=[SDS((length, D), bf16)] * 3,
        compiler_params=pltpu.CompilerParams(vmem_limit_bytes=VMEM_LIMIT),
        cost_estimate=LONG,
        name="back_first",
    )(*place, q, k, v, dctx, lse)


def group_kernel(me, s0, s1, s2, s3, q_r, k_r, v_r, g_r, lse, dq0, dk0, dv0, xt, *rest, lengths, pairs, first, final):
    if final:
        bg_before, rest = rest[0], rest[1:]
    dq, dk, dv, send, keep, bg, every, dw = rest
    width = 128 * pairs
    long, mid = lengths
    step = pl.program_id(0)

    @pl.when(step == 0)
    def _():
        backward_pairs(pairs, (s0, s1, s2, s3), 1, long, q_r, k_r, v_r, g_r, lse, first, dq, dk, dv)
        for a, (old, new) in enumerate(((dq0, dq), (dk0, dk), (dv0, dv))):
            lanes = slice(a * width, (a + 1) * width)
            every[0:long, lanes] = old[...]
            every[long : 2 * long, lanes] = new[...]

    @pl.when(step == 1)
    def _():
        backward_pairs(pairs, (s0, s1, s2, s3), 2, mid, q_r, k_r, v_r, g_r, lse, first, dq, dk, dv)
        for a, new in enumerate((dq, dk, dv)):
            every[2 * long : 2 * long + mid, a * width : (a + 1) * width] = new[0:mid, :]
        count = 2 * long + mid
        for c in range(3 * width // D):
            dw[:, D * c : D * (c + 1)] = dot(xt[:, 0:count], every[:, D * c : D * (c + 1)])
        bg[...] = jnp.zeros_like(bg)
        bg[0:1, :] = column_sum(every[:, 0:width])
        bg[1:2, :] = column_sum(every[:, 2 * width : 3 * width])
        if final:
            sums = jnp.concatenate([bg_before[...], bg[...]], axis=1)
        for half, out in ((0, keep), (1, send)):
            for r in range(16):
                d = block_number(half, r) ^ me[0]
                for c in range(3 * width // D):
                    emit_24(dw, D * c, d, out, r, 1152 * c)
                if final:
                    small = pltpu.roll(sums, lax.rem(D - 24 * d, D), 1)[:, 0:128]
                    small = jnp.concatenate([small, small], axis=0)
                    out[r, :, 1152 * (3 * width // D) :] = small.astype(bf16)


def group_backward(me, place, q, k, v, dctx, lse, before, xt, lengths, pairs, first, bg_before):
    final = bg_before is not None
    width = 128 * pairs
    column = first // pairs
    long, mid = lengths
    count = 2 * long + mid
    tok = pl.BlockSpec((long, width), lambda i, *_: (1 + i, column))
    old = pl.BlockSpec((long, width), lambda i, *_: (0, column))
    new = pl.BlockSpec((long, width), lambda i, *_: (i, 0))
    size = 3 * width * 24 // 16 + (128 if final else 0)
    out = pl.BlockSpec((16, 16, size), lambda i, *_: (0, 0, 0))
    extra = [bg_before] if final else []
    specs = [pl.BlockSpec(a.shape, lambda i, *_: (0, 0)) for a in extra]
    return pl.pallas_call(
        functools.partial(group_kernel, lengths=lengths, pairs=pairs, first=first, final=final),
        grid_spec=pltpu.PrefetchScalarGridSpec(
            num_scalar_prefetch=5,
            grid=(2,),
            in_specs=[tok] * 4
            + [pl.BlockSpec((16, 512), lambda i, *_: (1 + i, 0))]
            + [old] * 3
            + [pl.BlockSpec(xt.shape, lambda i, *_: (0, 0))]
            + specs,
            out_specs=[new] * 3 + [out, out, pl.BlockSpec((8, width), lambda i, *_: (0, 0))],
            scratch_shapes=[pltpu.VMEM((count, 3 * width), bf16), pltpu.VMEM((D, 3 * width), f32)],
        ),
        out_shape=[SDS((2 * long, width), bf16)] * 3
        + [SDS((16, 16, size), bf16)] * 2
        + [SDS((8, width), f32)],
        compiler_params=pltpu.CompilerParams(vmem_limit_bytes=45 * 2**20),
        cost_estimate=LONG,
        name=f"back_group_{first}",
    )(me, *place, q, k, v, dctx, lse, *before, xt, *extra)


def input_grad_kernel(seq, dr1, *rest, lengths, lanes):
    groups = len(lanes)
    first, blocks = rest[:3], rest[3 : 3 * groups + 3]
    weights = rest[3 * groups + 3 : 3 * groups + 6]
    own, own_mid, other = rest[-3:]
    long, mid = lengths
    half = long // 2
    top = slice(0, long)
    total = dr1[top, :]
    for a, w in enumerate(weights):
        total = total + dot_nt(first[a][...], w[...])
    total = total.astype(bf16)
    own[0] = total[:half]
    other[0:half, :] = total[half:]
    total = dr1[long : 2 * long + mid, :]
    n = slice(0, long + mid)
    for a, w in enumerate(weights):
        for g, (low, high) in enumerate(lanes):
            total = total + dot_nt(blocks[3 * g + a][n, :], w[:, low:high])
    total = total.astype(bf16)
    own[1] = total[0:half]
    other[half:long, :] = total[half:long]
    own_mid[...] = total[long : long + mid // 2]
    other[long:, :] = total[long + mid // 2 :]


def input_grad(seq, dr1, first, groups, lanes, weights, lengths):
    long, mid = lengths
    whole = lambda a: pl.BlockSpec(a.shape, lambda i, s: (0, 0))
    ins = list(first) + [a for g in groups for a in g] + list(weights)
    return pl.pallas_call(
        functools.partial(input_grad_kernel, lengths=lengths, lanes=lanes),
        grid_spec=pltpu.PrefetchScalarGridSpec(
            num_scalar_prefetch=1,
            grid=(1,),
            in_specs=[whole(dr1)] + [whole(a) for a in ins],
            out_specs=[
                pl.BlockSpec((2, long // 2, D), lambda i, s: (s[0], 0, 0)),
                pl.BlockSpec((mid // 2, D), lambda i, s: (0, 0)),
                pl.BlockSpec((long + mid // 2, D), lambda i, s: (0, 0)),
            ],
        ),
        out_shape=[SDS((4, long // 2, D), bf16), SDS((mid // 2, D), bf16), SDS((long + mid // 2, D), bf16)],
        compiler_params=pltpu.CompilerParams(vmem_limit_bytes=32 * 2**20),
        cost_estimate=LONG,
        name="input_grad",
    )(seq, dr1, *ins)


def swap_seq(v):
    return lax.ppermute(v, "seq", [(0, 1), (1, 0)])


def later(value, *others):
    return lax.optimization_barrier((value, *others))[0]


AXES = {"w": (0, 16), "z": (1, 8), "y": (2, 4), "x": (3, 1)}
CORE = 2


def swap(v, mask):
    return lax.ppermute(v, ("dp", "seq"), [(i, i ^ mask) for i in range(BLOCKS)])


class Payload:
    def __init__(self, groups, order, whole=False):
        self.groups = groups
        self.order = order
        self.whole = whole

    def specs(self, bits):
        todo = {AXES[a][0] for a in "".join(self.order)}
        found = []
        for width, arrays in self.groups:
            for array, lane in arrays:
                shape = tuple(2 if d in todo and d not in bits else 1 for d in range(4))
                index = tuple(bits.get(d, 0) if array.shape[d] == 2 else 0 for d in range(4))
                found.append((array, pl.BlockSpec(shape + (16, width), functools.partial(fixed, index + (0, lane)))))
        return found

    def receive(self, after=None):
        for outgoing, mask in zip(self.outgoing, self.masks):
            received = swap(outgoing, mask)
            if after is not None:
                received = later(received, after)
            low = 0
            for width, arrays in self.groups:
                arrays.append((received, low // width))
                low += width
        return self


def fixed(index, *_):
    return index


def join(*sums):
    return Payload([g for h in sums for g in h.groups], sums[0].order)


def load_sum(refs):
    total = refs[0][...].astype(f32)
    for r in refs[1:]:
        total = total + r[...].astype(f32)
    return total


def add_kernel(*refs, plan):
    outs = refs[len(refs) - len(plan) :]
    at = 0
    for out, groups in zip(outs, plan):
        low = 0
        for count, width in groups:
            out[:, :, :, :, :, low : low + width] = load_sum(refs[at : at + count]).astype(bf16)
            at += count
            low += width


def send(*sums):
    arrays, specs, plan, shapes = [], [], [], []
    for h in sums:
        step, rest = h.order[0], h.order[1:]
        h.masks, h.count = [], 0
        left = {AXES[a][0] for a in "".join(rest)}
        shape = tuple(2 if d in left else 1 for d in range(4)) + (16, sum(g[0] for g in h.groups))
        for which in range(0 if h.whole else 1, 2 ** len(step)):
            bits = {AXES[a][0]: which >> i & 1 for i, a in enumerate(step)}
            h.masks.append(sum(AXES[a][1] for i, a in enumerate(step) if which >> i & 1))
            found = h.specs(bits)
            arrays += [f[0] for f in found]
            specs += [f[1] for f in found]
            plan.append([(len(g[1]), g[0]) for g in h.groups])
            shapes.append(shape)
            h.count += 1
        h.order = rest
    outs = pl.pallas_call(
        functools.partial(add_kernel, plan=plan),
        grid=(1,),
        in_specs=specs,
        out_specs=[pl.BlockSpec(n, functools.partial(fixed, (0,) * 6)) for n in shapes],
        out_shape=[SDS(n, bf16) for n in shapes],
        compiler_params=pltpu.CompilerParams(vmem_limit_bytes=SMALL_LIMIT),
        cost_estimate=LONG,
        name="add_parts",
    )(*arrays)
    at = 0
    for h in sums:
        h.outgoing = outs[at : at + h.count]
        at += h.count
        if h.whole:
            h.whole = False
            stays, h.outgoing, h.masks = h.outgoing[0], h.outgoing[1:], h.masks[1:]
            low = 0
            for n, (width, _) in enumerate(h.groups):
                h.groups[n] = (width, [(stays, low // width)])
                low += width


def across_cores(pair, after, ranges, order):
    leaving, keep = pair
    received = later(swap(leaving, CORE), after)
    both = [v.reshape(2, 2, 2, 2, 16, -1) for v in (keep, received)]
    return [
        Payload([(width, [(v, lane) for v in both]) for width, lane in groups], axes, len(axes[0]) == 1)
        for axes, groups in zip(order, ranges)
    ]


def store_24(block, out, column, lanes=D):
    for g in range(3):
        for t in range(2):
            piece = block[8 * t : 8 * t + 8, 384 * g : 384 * (g + 1)]
            out[8 * g : 8 * g + 8, column + lanes // 2 * t : column + lanes // 2 * t + 384] = piece


def last_dense_kernel(seq, *refs, plan):
    (*ins, w_up, w_down, w_out, small) = refs
    blocks = []
    at = 0
    for count in plan:
        blocks.append(load_sum(ins[at : at + count])[0, 0, 0, 0])
        at += count
    up = jnp.concatenate(blocks[:2], axis=1)
    down = jnp.concatenate(blocks[2:], axis=1)
    for j in range(4):
        store_24(up[:, 1152 * j : 1152 * (j + 1)], w_up, 384 * j, FF)
    for g in range(6):
        w_down[16 * g : 16 * (g + 1), :] = down[:, D * g : D * (g + 1)]
    store_24(down[:, 4608:5760], w_out, 0)
    small[...] = down[:, 5760:5888]


def last_qkv_kernel(seq, *refs, plan):
    (*ins, w_query, w_key, w_value, small, scr) = refs
    blocks = []
    at = 0
    for count in plan:
        blocks.append(load_sum(ins[at : at + count])[0, 0, 0, 0])
        at += count
    left, right, tail = blocks
    for c in range(2):
        store_24(left[:, 1152 * c : 1152 * (c + 1)], scr, D * c)
    store_24(right, scr, 2 * D)
    for a, out in enumerate((w_query, w_key, w_value)):
        out[:, 0:512] = scr[:, 512 * a : 512 * (a + 1)]
        out[:, 512:768] = scr[:, 2 * D + 256 * a : 2 * D + 256 * (a + 1)]
    small[...] = tail


def last_sums(kernel, seq, sums, shapes, scratch):
    found = [f for h in sums for f in h.specs({})]
    plan = [len(g[1]) for h in sums for g in h.groups]
    return pl.pallas_call(
        functools.partial(kernel, plan=plan),
        grid=(1,),
        in_specs=[pl.BlockSpec(memory_space=pltpu.SMEM)] + [f[1] for f in found],
        out_specs=[pl.BlockSpec(n, functools.partial(fixed, (0, 0))) for n in shapes],
        out_shape=[SDS(n, f32) for n in shapes],
        scratch_shapes=[pltpu.VMEM(n, f32) for n in scratch],
        compiler_params=pltpu.CompilerParams(vmem_limit_bytes=SMALL_LIMIT),
        cost_estimate=LONG,
        name="last_sums",
    )(seq, *[f[0] for f in found])


def rows_24(block):
    return block.reshape(2, 8, 3, 384).transpose(2, 1, 0, 3).reshape(24, D)


def unpack_up(block):
    return block.reshape(2, 8, 4, 3, 384).transpose(3, 1, 0, 2, 4).reshape(24, FF)


def unpack_down(block):
    return block[:, :4608].reshape(16, 6, D).transpose(1, 0, 2).reshape(96, D), rows_24(block[:, 4608:5760])


def unpack_qkv(blocks):
    wide, narrow = blocks
    left = jnp.concatenate([rows_24(wide[:, :1152]), rows_24(wide[:, 1152:])], axis=1)
    right = rows_24(narrow[:, :1152])
    return [
        jnp.concatenate([left[:, 512 * a : 512 * (a + 1)], right[:, 256 * a : 256 * (a + 1)]], axis=1) for a in range(3)
    ]


def reduce_plain(up_pair, down_pair, qkv_pairs, vec, bg):
    def ordered(pair):
        send, keep = pair
        both = jnp.stack([keep.reshape(8, 2, 16, -1), send.reshape(8, 2, 16, -1)], axis=1)
        return both.reshape(BLOCKS, 16, -1).astype(f32)

    scatter = lambda v: lax.psum_scatter(v, ("dp", "seq"), scatter_dimension=0, tiled=True)
    w_up = jax.vmap(unpack_up)(ordered(up_pair)).reshape(D, FF)
    w_down, w_out = (a.reshape(-1, D) for a in jax.vmap(unpack_down)(ordered(down_pair)))
    qkv = [a.reshape(D, D) for a in jax.vmap(unpack_qkv)([ordered(p) for p in qkv_pairs])]
    small = [scatter(vec[i]) for i in range(6)]
    return (
        scatter(qkv[0]), scatter(bg[0]), scatter(qkv[1]), scatter(qkv[2]), scatter(bg[1]), scatter(w_out),
        small, scatter(w_up), scatter(vec[8:12].reshape(FF)), scatter(w_down),
    )


def give_back_kernel(seq, here, got_first, got, got_end, long_in, long, middle, short):
    long[0] = jnp.where(pl.program_id(0) == 0, got_first[...], got[...])

    @pl.when(seq[0] == 0)
    def _():
        middle[0] = here[...]
        short[0] = got_end[: short.shape[1], :]

    @pl.when(seq[0] != 0)
    def _():
        middle[0] = got_end[...]
        short[0] = here[: short.shape[1], :]


def give_back(seq, long, here, got, short):
    count, half, _ = long.shape
    mid = here.shape[0]
    mine = count // 2
    skip = 2 - len(got)
    return pl.pallas_call(
        give_back_kernel,
        grid_spec=pltpu.PrefetchScalarGridSpec(
            num_scalar_prefetch=1,
            grid=(mine,),
            in_specs=[
                pl.BlockSpec((mid, D), lambda i, s: (0, 0)),
                pl.BlockSpec((half, D), lambda i, s: (0, 0)),
                pl.BlockSpec((half, D), lambda i, s: (jnp.maximum(i - 1, 0) + skip, 0)),
                pl.BlockSpec((mid, D), lambda i, s: ((mine - 1 + skip) * half // mid, 0)),
                ANY,
            ],
            out_specs=[
                pl.BlockSpec((1, half, D), lambda i, s: (mine * (1 - s[0]) + i, 0, 0)),
                pl.BlockSpec((1, mid, D), lambda i, s: (0, 0, 0)),
                pl.BlockSpec((1, short, D), lambda i, s: (0, 0, 0)),
            ],
        ),
        out_shape=[SDS(long.shape, bf16), SDS((1, mid, D), bf16), SDS((1, short, D), bf16)],
        input_output_aliases={5: 0},
        compiler_params=pltpu.CompilerParams(vmem_limit_bytes=SMALL_LIMIT),
        cost_estimate=LONG,
        name="add_halves",
    )(seq, here, got[0], got[-1], got[-1], long)


def per_device(
    tokens_short, tokens_middle, tokens_long, length_short, length_middle, length_long,
    query_weight, query_bias, key_weight, value_weight, value_bias, output_weight, output_bias,
    attention_gain, attention_shift, up_weight, up_bias, down_weight, down_bias, output_gain, output_shift,
    upstream_short, upstream_middle, upstream_long,
):
    seq = lax.axis_index("seq")
    first = seq == 0
    device = (lax.axis_index("dp") * 2 + seq).astype(jnp.int32)
    fast = lax.axis_size("dp") * lax.axis_size("seq") == BLOCKS
    me = device if fast else jnp.int32(0)
    me_ref = me.reshape(1)
    count, half, _ = tokens_long.shape
    mine = count // 2
    mid = tokens_middle.shape[1]
    short = tokens_short.shape[1]
    lengths = (2 * half,) * mine + (2 * mid,)
    tokens = sum(lengths)
    rows = 2 * half * (mine + 1)

    def own_rows(v):
        return lax.dynamic_slice_in_dim(v, mine * seq, mine, 0)

    def other_rows(v):
        return lax.dynamic_slice_in_dim(v, mine * (1 - seq), mine, 0)

    def middle_rows(middle, low):
        low = jnp.pad(low[0], ((0, mid - short), (0, 0)))
        return jnp.where(first, middle[0], low), jnp.where(first, low, middle[0])

    x_mid, x_mid_out = middle_rows(tokens_middle, tokens_short)
    x_mid_in = swap_seq(x_mid_out)
    x_own, x_out = own_rows(tokens_long), other_rows(tokens_long)
    x_in = [swap_seq(x_out[0])]
    u_mid, u_mid_out = middle_rows(upstream_middle, upstream_short)
    u_out = jnp.concatenate([other_rows(upstream_long).reshape(mine * half, D), u_mid_out], axis=0)

    place = (seq.astype(jnp.int32).reshape(1), length_short, length_middle, length_long)
    qkv = [query_weight, key_weight, value_weight]
    projections = qkv + [query_bias, value_bias]
    chain = attention_forward(place, x_mid, x_mid_in, projections, mine, 2 * mid, mine * half // mid, None, rows)
    x_in += [swap_seq(later(x_out[i], chain[5])) for i in range(1, mine)]
    for i in range(mine):
        chain = attention_forward(place, x_own[i], x_in[i], projections, i, 2 * half, i, chain, rows)
    x, q, k, v, ctx, lse, xt = chain
    u_in = swap_seq(later(u_out, lse))

    mats = [output_weight, up_weight, down_weight]
    dense = functools.partial(
        dense_steps, place[0], ctx, x, tokens=tokens, rows=rows, mats=mats,
        vecs=[up_bias, output_bias, attention_gain, attention_shift, down_bias, output_gain, output_shift],
    )
    res_long, *before = dense(ups=[upstream_long], before=None)
    res_first, res_rest, res_mid, act, dinn, nlow, dbr, datt, dr1, dctx, vec = dense(ups=[u_in, u_in, u_mid], before=before)

    up_pair = up_grad(me_ref, nlow, dinn, tokens)
    res_got = [swap_seq(later(res_first, up_pair[0]))]
    down_pair = down_grad(later(me_ref, up_pair[0]), act, dbr, ctx, datt, vec, tokens)
    res_got[0] = later(res_got[0], down_pair[0])
    res_got.append(swap_seq(later(res_rest, res_got[0])))

    def at(before, *sums, done=()):
        going = [v for h in sums for v in h.outgoing] if fast else []
        return (later(place[0], before, *going, *done), *place[1:])

    up = down = all_sum = ()
    if fast:
        up = across_cores(
            up_pair, down_pair[0], [[(2304, 0)], [(2304, 1)]], [["z", "x", "y", "w"], ["y", "x", "z", "w"]]
        )
        send(*up)
    before = first_row_backward(at(down_pair[0], *up), q, k, v, dctx, lse, 2 * half)
    first_done = before[0]
    if fast:
        for h in up:
            h.receive(first_done)
        down = across_cores(
            down_pair, first_done, [[(2944, 0)], [(2944, 1)]], [["z", "y", "x", "w"], ["y", "z", "x", "w"]]
        )
        send(*up, *down)
    res_got[1] = later(res_got[1], first_done)
    later_rows = (2 * half, 2 * mid)
    *wide, leaving, keep, bg = group_backward(
        me_ref, at(first_done, *up, *down, done=res_got), q, k, v, dctx, lse, before, xt, later_rows, 4, 0, None
    )
    wide_pair = (leaving, keep)
    if fast:
        for h in (*up, *down):
            h.receive(bg)
        send(*up, *down)
    *narrow, leaving, keep, bg_last = group_backward(
        me_ref, at(bg, *up, *down), q, k, v, dctx, lse, before, xt, later_rows, 2, 4, bg
    )
    narrow_pair = (leaving, keep)
    if fast:
        for h in (*up, *down):
            h.receive(bg_last)
        up = (join(*up),)
        down = (join(*down),)
        send(*up, *down)
        wide_sum = across_cores(wide_pair, bg_last, [[(2304, 0)]], [["yz", "xw"]])
        narrow_sum = across_cores(narrow_pair, up[0].outgoing[0], [[(1152, 0), (128, 9)]], [["yz", "xw"]])
        all_sum = (join(*wide_sum, *narrow_sum),)
        send(*all_sum)
    ig_long, ig_mid, ig_rest = input_grad(
        at(bg_last, *up, *down, *all_sum)[0], dr1, before, [wide, narrow], [(0, 512), (512, 768)], qkv, later_rows
    )
    ig_got = [swap_seq(ig_rest)]
    if fast:
        up[0].receive(ig_rest)
        down[0].receive(ig_rest)
        send(*down)
        all_sum[0].receive(down[0].outgoing[0])
        send(*all_sum)
        spare = all_sum[0].outgoing[0]
    else:
        spare = ig_rest
    res_long, res_middle, res_short = give_back(
        later(place[0], spare), res_long, res_mid, res_got, short
    )
    ig_long, ig_middle, ig_short = give_back(place[0], ig_long, ig_mid, ig_got, short)
    if fast:
        down[0].receive()
        w_up, w_down, w_out, small = last_sums(
            last_dense_kernel, later(place[0], spare), [*up, *down], [(24, FF), (96, D), (24, D), (16, 128)], []
        )
        all_sum[0].receive(ig_middle)
        w_query, w_key, w_value, ends = last_sums(
            last_qkv_kernel, place[0], all_sum, [(24, D)] * 3 + [(16, 128)], [(24, 3 * D)]
        )
        b_up = lax.dynamic_slice(small, (8 + (me >> 3), 0), (1, 96))[0]
        done = w_query, ends[0, :24], w_key, w_value, ends[1, :24], w_out, small[:8, :24], w_up, b_up, w_down
    else:
        done = reduce_plain(up_pair, down_pair, [wide_pair, narrow_pair], vec, jnp.concatenate([bg, bg_last], axis=1))
    results = (res_short, res_middle, res_long)
    input_grads = (ig_short, ig_middle, ig_long)
    w_query, bq, w_key, w_value, bv, w_out, small, w_up, b_up, w_down = done
    return (
        *results, *input_grads,
        w_query, bq, w_key, w_value, bv, w_out, small[5], small[3], small[4],
        w_up, b_up, w_down, small[2], small[0], small[1],
    )


def solution(mesh):
    tokens = P("dp", "seq", None)
    wide = P(("dp", "seq"), None)
    flat = P(("dp", "seq"))
    in_specs = (tokens,) * 3 + (P("dp"),) * 3 + (P(),) * 15 + (tokens,) * 3
    out_specs = (tokens,) * 6 + (
        wide, flat, wide, wide, flat, wide, flat, flat, flat, wide, flat, wide, flat, flat, flat,
    )
    return jax.shard_map(per_device, mesh=mesh, in_specs=in_specs, out_specs=out_specs, check_vma=False)
```

```python
import functools

import jax
import jax.numpy as jnp
from jax import lax
from jax.experimental import pallas as pl
from jax.experimental.pallas import tpu as pltpu
from jax.sharding import PartitionSpec as P

D = 768
FF = 3072
HEADS = 12
PAIRS = HEADS // 2
EPS = 1e-12
NEG = -1e30
SHORT_HALF = 64
BLOCKS = 32
VMEM_LIMIT = 60 * 2**20
SMALL_LIMIT = 12 * 2**20

bf16 = jnp.bfloat16
f32 = jnp.float32
SDS = jax.ShapeDtypeStruct
ANY = pl.BlockSpec(memory_space=pl.ANY)
LONG = pl.CostEstimate(flops=4 * 10**10, bytes_accessed=10**8, transcendentals=0)


def dot(a, b):
    return lax.dot_general(a, b, (((1,), (0,)), ((), ())), preferred_element_type=f32)


def dot_nt(a, b):
    return lax.dot_general(a, b, (((1,), (1,)), ((), ())), preferred_element_type=f32)


def dot_tn(a, b):
    return lax.dot_general(a, b, (((0,), (0,)), ((), ())), preferred_element_type=f32)


def wide(vector):
    return vector[...].reshape(1, -1)


def mean(v):
    return jnp.mean(v, axis=-1, keepdims=True)


def column_sum(v):
    return jnp.sum(v.astype(f32), axis=0, keepdims=True)


A1, A2, A3, A4, A5 = 0.254829592, -0.284496736, 1.421413741, -1.453152027, 1.061405429
P_SCALED = 0.3275911 * 0.7071067811865476
INV_SQRT_2PI = 0.3989422804014327


def gelu_and_slope(v):
    t = 1.0 / (1.0 + P_SCALED * jnp.abs(v))
    e = jnp.exp(v * v * -0.5)
    tail = t * (A1 + t * (A2 + t * (A3 + t * (A4 + t * A5)))) * (0.5 * e)
    cdf = jnp.where(v < 0, tail, 1.0 - tail)
    return v * cdf, cdf + v * (e * INV_SQRT_2PI)


def mask_column(place, row, length):
    seq, short, middle, long = place
    half = length // 2
    mine = long.shape[0] // 2
    s = seq[0]
    if row < mine:
        count, valid, own, other = long[mine * s + row], half, half * s, half * (1 - s)
    else:
        is_first = s == 0
        count = jnp.where(is_first, middle[0], short[0])
        valid = jnp.where(is_first, half, SHORT_HALF)
        own, other = jnp.where(is_first, 0, SHORT_HALF), jnp.where(is_first, half, 0)
    i = lax.broadcasted_iota(jnp.int32, (length, 1), 0)
    inner = jnp.where(i < half, i, i - half)
    live = (inner + jnp.where(i < half, own, other) < count) & (inner < valid)
    return jnp.where(live, 0.0, NEG).astype(f32)


def low_lanes():
    return lax.broadcasted_iota(jnp.int32, (1, 128), 1) < 64


def stack_heads(pair, low):
    zero = jnp.zeros_like(pair)
    return jnp.concatenate([jnp.where(low, pair, zero), jnp.where(low, zero, pair)], axis=0)


def split_rows(pair_t):
    row = lax.broadcasted_iota(jnp.int32, (128, 1), 0) < 64
    zero = jnp.zeros_like(pair_t)
    return jnp.where(row, pair_t, zero), jnp.where(row, zero, pair_t)


def scaled(q):
    return (q.astype(f32) * 0.125).astype(bf16)


def emit_24(scr, lane, d, out, r, base):
    for g in range(3):
        rows = pl.ds(pl.multiple_of(24 * d + 8 * g, 8), 8)
        both = jnp.concatenate(
            [scr[rows, lane : lane + 384], scr[rows, lane + 384 : lane + 768]], axis=0
        )
        out[r, :, base + 384 * g : base + 384 * (g + 1)] = both.astype(bf16)


def block_number(half, r):
    return ((r >> 1) << 2) | (half << 1) | (r & 1)


def forward_kernel(s0, s1, s2, s3, xl, xr, wq, wk, wv, bq, bv, *rest, length, row, chained):
    x_o, q_o, k_o, v_o, c_o, lse_o, xt_o = rest[7:] if chained else rest
    x = jnp.concatenate([xl[...], xr[...]], axis=0)
    x_o[...] = x
    xt_o[...] = x.T
    q_o[...] = (dot(x, wq[...]) + wide(bq)).astype(bf16)
    k_o[...] = dot(x, wk[...]).astype(bf16)
    v_o[...] = (dot(x, wv[...]) + wide(bv)).astype(bf16)
    bias = mask_column((s0, s1, s2, s3), row, length)
    low = low_lanes()
    row_low = lax.broadcasted_iota(jnp.int32, (128, 1), 0) < 64
    for p in range(PAIRS):
        sl = slice(128 * p, 128 * p + 128)
        scores = dot_nt(stack_heads(k_o[:, sl], low), scaled(q_o[:, sl]))
        parts = []
        inverse = []
        for h in range(2):
            s = scores[h * length : (h + 1) * length, :] + bias
            top = jnp.max(s, axis=0, keepdims=True)
            raised = jnp.exp(s - top)
            total = jnp.sum(raised, axis=0, keepdims=True)
            lse_o[2 * p + h : 2 * p + h + 1, 0:length] = top + jnp.log(total)
            parts.append(raised.astype(bf16))
            inverse.append(1.0 / total)
        upper, lower = split_rows(v_o[:, sl].T)
        context = dot(upper, parts[0]) + dot(lower, parts[1])
        context = context * jnp.where(row_low, inverse[0], inverse[1])
        c_o[:, sl] = context.T.astype(bf16)


def attention_forward(place, own, other, weights, row, length, block, chain, rows):
    half = pl.BlockSpec((length // 2, D), lambda i: (0, 0))
    full = lambda a: pl.BlockSpec(a.shape, lambda i: (0,) * a.ndim)
    tok = pl.BlockSpec((length, D), lambda i: (block, 0))
    lse = pl.BlockSpec((16, 512), lambda i: (row, 0))
    turned = pl.BlockSpec((D, length), lambda i: (0, block))
    chained = chain is not None
    extra = list(chain) if chained else []
    return pl.pallas_call(
        functools.partial(forward_kernel, length=length, row=row, chained=chained),
        grid=(1,),
        in_specs=[pl.BlockSpec(memory_space=pltpu.SMEM)] * 4
        + [half, half]
        + [full(w) for w in weights]
        + [ANY] * len(extra),
        out_specs=[tok] * 5 + [lse, turned],
        out_shape=[SDS((rows, D), bf16)] * 5 + [SDS((48, 512), f32), SDS((D, rows), bf16)],
        input_output_aliases={11 + i: i for i in range(7)} if chained else {},
        compiler_params=pltpu.CompilerParams(vmem_limit_bytes=57 * 2**20),
        cost_estimate=LONG,
        name=f"attend_{row}",
    )(*place, own, other, *weights, *extra)


def drop_first(kernel):
    return lambda _, *refs, **options: kernel(*refs, **options)


def dense_kernel(*refs, chunks, own):
    ctx, x = refs[0], refs[1]
    step = pl.program_id(0)
    last = step == pl.num_programs(0) - 1
    if own:
        up_refs, refs = refs[2:3], refs[3:]
        up = up_refs[0][0]
    else:
        up_refs, refs = refs[2:5], refs[5:]
        up = jnp.concatenate([jnp.where(last, up_refs[2][...], up_refs[0][...]), up_refs[1][...]], axis=0)
    wo, wup, wdn, bup, bo, g1, s1, bdn, g2, s2 = refs[:10]
    bup, bo, g1, s1, bdn, g2, s2 = (wide(v) for v in (bup, bo, g1, s1, bdn, g2, s2))
    if own:
        res_own, act, dinn, nlow_o, dbr, datt, dr1_o, dctx, vec, slope_s = refs[10:]
    else:
        vec_in = refs[10]
        res_first, res_rest, res_mid, act, dinn, nlow_o, dbr, datt, dr1_o, dctx, vec, slope_s = refs[18:]

    @pl.when(step == 0)
    def _():
        vec[...] = jnp.zeros_like(vec) if own else vec_in[...]

    r1 = x[...].astype(f32) + dot(ctx[...], wo[...]) + bo
    c1 = r1 - mean(r1)
    rs1 = lax.rsqrt(mean(c1 * c1) + EPS)
    n1 = c1 * rs1
    normed = n1 * g1 + s1
    nlow = normed.astype(bf16)
    nlow_o[...] = nlow
    acc = normed + bdn
    width = FF // chunks
    for j in range(chunks):
        sl = slice(j * width, (j + 1) * width)
        value, slope = gelu_and_slope(dot(nlow, wup[:, sl]) + bup[:, sl])
        value = value.astype(bf16)
        act[:, sl] = value
        slope_s[:, sl] = slope
        acc = acc + dot(value, wdn[sl, :])
    c2 = acc - mean(acc)
    rs2 = lax.rsqrt(mean(c2 * c2) + EPS)
    n2 = c2 * rs2
    result = (n2 * g2 + s2).astype(bf16)
    if own:
        res_own[0] = result
    else:
        size = result.shape[0]

        @pl.when(step == 0)
        def _():
            res_first[...] = result

        @pl.when((step > 0) & jnp.logical_not(last))
        def _():
            res_rest[pl.ds(pl.multiple_of((step - 1) * size, size), size), :] = result

        @pl.when(last)
        def _():
            res_mid[...] = result[: size // 2]
            res_rest[res_rest.shape[0] - size // 2 :, :] = result[size // 2 :]

    upstream = up.astype(f32)
    u = upstream * g2
    dr2 = (u - mean(u) - n2 * mean(u * n2)) * rs2
    branch = dr2.astype(bf16)
    dbr[...] = branch
    vec[0:1, :] += column_sum(upstream * n2)
    vec[1:2, :] += column_sum(upstream)
    vec[2:3, :] += column_sum(branch)
    acc = dr2
    for j in range(chunks):
        sl = slice(j * width, (j + 1) * width)
        d_inner = (dot_nt(branch, wdn[sl, :]) * slope_s[:, sl]).astype(bf16)
        dinn[:, sl] = d_inner
        vec[8 + j : 9 + j, :] += column_sum(d_inner)
        acc = acc + dot_nt(d_inner, wup[:, sl])
    vec[3:4, :] += column_sum(acc * n1)
    vec[4:5, :] += column_sum(acc)
    u1 = acc * g1
    d1 = (u1 - mean(u1) - n1 * mean(u1 * n1)) * rs1
    d_attn = d1.astype(bf16)
    datt[...] = d_attn
    dr1_o[...] = d1
    vec[5:6, :] += column_sum(d_attn)
    dctx[...] = dot_nt(d_attn, wo[...]).astype(bf16)


def dense_steps(seq, ctx, x, ups, mats, vecs, tokens, rows, before):
    tile = 256
    half = tile // 2
    mine = tokens // tile // 2
    own = before is None
    full = lambda a: pl.BlockSpec(a.shape, lambda i, s: (0,) * a.ndim, pipeline_mode=pl.Buffered(1))
    whole = lambda n: pl.BlockSpec((n, D), lambda i, s: (0, 0))
    if own:
        place = lambda i: 2 * i
        steps = mine
        up_specs = [pl.BlockSpec((1, tile, D), lambda i, s: (s[0] * mine + i, 0, 0))]
        res_specs = [pl.BlockSpec((1, tile, D), lambda i, s: (s[0] * mine + i, 0, 0))]
        res_shapes = [SDS((2 * mine, tile, D), bf16)]
        extra, extra_specs, aliases = [], [], {}
    else:
        place = lambda i: jnp.minimum(2 * i + 1, 2 * mine)
        steps = mine + 1
        up_specs = [
            pl.BlockSpec((half, D), lambda i, s: (jnp.minimum(2 * i, 2 * mine - 2), 0)),
            pl.BlockSpec((half, D), lambda i, s: (jnp.minimum(2 * i + 1, 2 * mine), 0)),
            whole(half),
        ]
        sizes = (tile, tokens // 2 - tile, half)
        res_specs = [whole(n) for n in sizes]
        res_shapes = [SDS((n, D), bf16) for n in sizes]
        *arrays, vec = before
        extra = [vec] + arrays
        extra_specs = [whole(16)] + [ANY] * len(arrays)
        first = 1 + 2 + len(ups) + len(mats) + len(vecs) + 1
        aliases = {first + i: 3 + i for i in range(len(arrays))}
    tok = pl.BlockSpec((tile, D), lambda i, s: (place(i), 0))
    ffs = pl.BlockSpec((tile, FF), lambda i, s: (place(i), 0))
    return pl.pallas_call(
        functools.partial(drop_first(dense_kernel), chunks=4, own=own),
        grid_spec=pltpu.PrefetchScalarGridSpec(
            num_scalar_prefetch=1,
            grid=(steps,),
            in_specs=[tok, tok] + up_specs + [full(a) for a in mats + vecs] + extra_specs,
            out_specs=res_specs + [ffs, ffs] + [tok] * 5 + [whole(16)],
            scratch_shapes=[pltpu.VMEM((tile, FF), f32)],
        ),
        out_shape=res_shapes
        + [SDS((tokens, FF), bf16)] * 2
        + [SDS((tokens, D), bf16)] * 3
        + [SDS((rows, D), f32), SDS((rows, D), bf16), SDS((16, D), f32)],
        input_output_aliases=aliases,
        compiler_params=pltpu.CompilerParams(vmem_limit_bytes=VMEM_LIMIT),
        cost_estimate=LONG,
        name="dense_own" if own else "dense_rest",
    )(seq, ctx, x, *ups, *mats, *vecs, *extra)


def up_grad_kernel(me, nlow, left, right, send, keep, turned, scr):

    @pl.when(pl.program_id(0) == 0)
    def _():
        turned[...] = nlow[...].T

    scr[:, 0:384] = dot(turned[...], left[...])
    scr[:, 384:768] = dot(turned[...], right[...])
    for half, out in ((0, keep), (1, send)):
        for r in range(16):
            emit_24(scr, 0, block_number(half, r) ^ me[0], out, r, 0)


def up_grad(me, nlow, dinn, tokens):
    out = pl.BlockSpec((16, 16, 1152), lambda j, m: (0, 0, j))
    return pl.pallas_call(
        up_grad_kernel,
        grid_spec=pltpu.PrefetchScalarGridSpec(
            num_scalar_prefetch=1,
            grid=(4,),
            in_specs=[
                pl.BlockSpec((tokens, D), lambda j, m: (0, 0)),
                pl.BlockSpec((tokens, 384), lambda j, m: (0, j)),
                pl.BlockSpec((tokens, 384), lambda j, m: (0, j + 4)),
            ],
            out_specs=[out, out],
            scratch_shapes=[pltpu.VMEM((D, tokens), bf16), pltpu.VMEM((D, D), f32)],
        ),
        out_shape=[SDS((16, 16, 4608), bf16)] * 2,
        compiler_params=pltpu.CompilerParams(vmem_limit_bytes=VMEM_LIMIT),
        cost_estimate=LONG,
        name="up_grad",
    )(me, nlow, dinn, dinn)


DOWN_WIDTH = 4608 + 1152 + 128


def down_grad_kernel(me, act, dbr, ctx, datt, vec, send, keep, scr, wo_s):
    j = pl.program_id(0)

    @pl.when(j == 0)
    def _():
        wo_s[...] = dot_tn(ctx[...], datt[...])

    scr[...] = dot_tn(act[...], dbr[...])
    z = j ^ (me[0] >> 3)
    for half, out in ((0, keep), (1, send)):
        for r in range(4):
            near = block_number(half, r) ^ (me[0] & 7)
            d = z * 8 + near
            for g in range(6):
                rows = pl.ds(pl.multiple_of(96 * near + 16 * g, 16), 16)
                out[r, :, D * g : D * (g + 1)] = scr[rows, :].astype(bf16)
            emit_24(wo_s, 0, d, out, r, 4608)
            small = pltpu.roll(vec[0:8, :], lax.rem(D - 24 * d, D), 1)[:, 0:128]
            wide = pltpu.roll(vec[8:16, :], lax.rem(D - 96 * near, D), 1)[:, 0:128]
            out[r, :, 5760:5888] = jnp.concatenate([small, wide], axis=0).astype(bf16)


def down_grad(me, act, dbr, ctx, datt, vec, tokens):
    out = pl.BlockSpec((4, 16, DOWN_WIDTH), lambda j, m: (j, 0, 0))
    tok = pl.BlockSpec((tokens, D), lambda j, m: (0, 0))
    return pl.pallas_call(
        down_grad_kernel,
        grid_spec=pltpu.PrefetchScalarGridSpec(
            num_scalar_prefetch=1,
            grid=(4,),
            in_specs=[
                pl.BlockSpec((tokens, D), lambda j, m: (0, j ^ (m[0] >> 3))),
                tok,
                tok,
                tok,
                pl.BlockSpec((16, D), lambda j, m: (0, 0)),
            ],
            out_specs=[out, out],
            scratch_shapes=[pltpu.VMEM((D, D), f32), pltpu.VMEM((D, D), f32)],
        ),
        out_shape=[SDS((16, 16, DOWN_WIDTH), bf16)] * 2,
        compiler_params=pltpu.CompilerParams(vmem_limit_bytes=VMEM_LIMIT),
        cost_estimate=LONG,
        name="down_grad",
    )(me, act, dbr, ctx, datt, vec)


def backward_pairs(pairs, place, row, length, q_r, k_r, v_r, g_r, lse, first, dq_o, dk_o, dv_o):
    n = slice(0, length)
    bias = mask_column(place, row, length)
    low = low_lanes()
    for p in range(pairs):
        sl = slice(128 * p, 128 * p + 128)
        q2 = scaled(q_r[n, sl])
        k2 = k_r[n, sl]
        g2 = g_r[n, sl]
        scores = dot_nt(stack_heads(k2, low), q2)
        d_probs = dot_nt(stack_heads(v_r[n, sl], low), g2)
        probs_low = []
        d_scores = []
        for h in range(2):
            part = slice(h * length, (h + 1) * length)
            head = 2 * (first + p) + h
            probs = jnp.exp(scores[part, :] + bias - lse[head : head + 1, n])
            d_part = d_probs[part, :]
            centre = jnp.sum(probs * d_part, axis=0, keepdims=True)
            probs_low.append(probs.astype(bf16))
            d_scores.append((probs * (d_part - centre)).astype(bf16))
        dv_o[n, sl] = jnp.where(low, dot(probs_low[0], g2), dot(probs_low[1], g2)).astype(bf16)
        dk_o[n, sl] = jnp.where(low, dot(d_scores[0], q2), dot(d_scores[1], q2)).astype(bf16)
        upper, lower = split_rows(k2.T)
        turned = dot(upper, d_scores[0]) + dot(lower, d_scores[1])
        dq_o[n, sl] = (turned * 0.125).T.astype(bf16)


def first_row_kernel(s0, s1, s2, s3, q_r, k_r, v_r, g_r, lse, dr1, wq, wk, wv, dq, dk, dv, ig_own, ig_other, *, length):
    backward_pairs(PAIRS, (s0, s1, s2, s3), 0, length, q_r, k_r, v_r, g_r, lse, 0, dq, dk, dv)
    ig = dr1[...] + dot_nt(dq[...], wq[...]) + dot_nt(dk[...], wk[...]) + dot_nt(dv[...], wv[...])
    ig = ig.astype(bf16)
    ig_own[0] = ig[: length // 2]
    ig_other[...] = ig[length // 2 :]


def first_row_backward(place, q, k, v, dctx, lse, dr1, weights, length):
    tok = pl.BlockSpec((length, D), lambda i, *_: (0, 0))
    half = length // 2
    mine = place[3].shape[0] // 2
    full = pl.BlockSpec((D, D), lambda i, *_: (0, 0))
    return pl.pallas_call(
        functools.partial(first_row_kernel, length=length),
        grid_spec=pltpu.PrefetchScalarGridSpec(
            num_scalar_prefetch=4,
            grid=(1,),
            in_specs=[tok] * 4 + [pl.BlockSpec((16, 512), lambda i, *_: (0, 0)), tok] + [full] * 3,
            out_specs=[tok] * 3
            + [
                pl.BlockSpec((1, half, D), lambda i, s, *_: (mine * s[0], 0, 0)),
                pl.BlockSpec((half, D), lambda i, *_: (0, 0)),
            ],
        ),
        out_shape=[SDS((length, D), bf16)] * 3 + [SDS((2 * mine, half, D), bf16), SDS((half, D), bf16)],
        compiler_params=pltpu.CompilerParams(vmem_limit_bytes=VMEM_LIMIT),
        cost_estimate=LONG,
        name="back_first",
    )(*place, q, k, v, dctx, lse, dr1, *weights)


def group_kernel(me, s0, s1, s2, s3, q_r, k_r, v_r, g_r, lse, dq0, dk0, dv0, xt, *rest, lengths, pairs, first, final):
    if final:
        bg_before, rest = rest[0], rest[1:]
    dq, dk, dv, send, keep, bg, every, dw = rest
    width = 128 * pairs
    long, mid = lengths
    step = pl.program_id(0)

    @pl.when(step == 0)
    def _():
        backward_pairs(pairs, (s0, s1, s2, s3), 1, long, q_r, k_r, v_r, g_r, lse, first, dq, dk, dv)
        for a, (old, new) in enumerate(((dq0, dq), (dk0, dk), (dv0, dv))):
            lanes = slice(a * width, (a + 1) * width)
            every[0:long, lanes] = old[...]
            every[long : 2 * long, lanes] = new[...]

    @pl.when(step == 1)
    def _():
        backward_pairs(pairs, (s0, s1, s2, s3), 2, mid, q_r, k_r, v_r, g_r, lse, first, dq, dk, dv)
        for a, new in enumerate((dq, dk, dv)):
            every[2 * long : 2 * long + mid, a * width : (a + 1) * width] = new[0:mid, :]
        count = 2 * long + mid
        for c in range(3 * width // D):
            dw[:, D * c : D * (c + 1)] = dot(xt[:, 0:count], every[:, D * c : D * (c + 1)])
        bg[...] = jnp.zeros_like(bg)
        bg[0:1, :] = column_sum(every[:, 0:width])
        bg[1:2, :] = column_sum(every[:, 2 * width : 3 * width])
        if final:
            sums = jnp.concatenate([bg_before[...], bg[...]], axis=1)
        for half, out in ((0, keep), (1, send)):
            for r in range(16):
                d = block_number(half, r) ^ me[0]
                for c in range(3 * width // D):
                    emit_24(dw, D * c, d, out, r, 1152 * c)
                if final:
                    small = pltpu.roll(sums, lax.rem(D - 24 * d, D), 1)[:, 0:128]
                    small = jnp.concatenate([small, small], axis=0)
                    out[r, :, 1152 * (3 * width // D) :] = small.astype(bf16)


def group_backward(me, place, q, k, v, dctx, lse, before, xt, lengths, pairs, first, bg_before):
    final = bg_before is not None
    width = 128 * pairs
    column = first // pairs
    long, mid = lengths
    count = 2 * long + mid
    tok = pl.BlockSpec((long, width), lambda i, *_: (1 + i, column))
    old = pl.BlockSpec((long, width), lambda i, *_: (0, column))
    new = pl.BlockSpec((long, width), lambda i, *_: (i, 0))
    size = 3 * width * 24 // 16 + (128 if final else 0)
    out = pl.BlockSpec((16, 16, size), lambda i, *_: (0, 0, 0))
    extra = [bg_before] if final else []
    specs = [pl.BlockSpec(a.shape, lambda i, *_: (0, 0)) for a in extra]
    return pl.pallas_call(
        functools.partial(group_kernel, lengths=lengths, pairs=pairs, first=first, final=final),
        grid_spec=pltpu.PrefetchScalarGridSpec(
            num_scalar_prefetch=5,
            grid=(2,),
            in_specs=[tok] * 4
            + [pl.BlockSpec((16, 512), lambda i, *_: (1 + i, 0))]
            + [old] * 3
            + [pl.BlockSpec(xt.shape, lambda i, *_: (0, 0))]
            + specs,
            out_specs=[new] * 3 + [out, out, pl.BlockSpec((8, width), lambda i, *_: (0, 0))],
            scratch_shapes=[pltpu.VMEM((count, 3 * width), bf16), pltpu.VMEM((D, 3 * width), f32)],
        ),
        out_shape=[SDS((2 * long, width), bf16)] * 3
        + [SDS((16, 16, size), bf16)] * 2
        + [SDS((8, width), f32)],
        compiler_params=pltpu.CompilerParams(vmem_limit_bytes=45 * 2**20),
        cost_estimate=LONG,
        name=f"back_group_{first}",
    )(me, *place, q, k, v, dctx, lse, *before, xt, *extra)


def input_grad_kernel(seq, dr1, *rest, lengths, lanes):
    groups = len(lanes)
    blocks, (wq, wk, wv), (_, own, own_mid, other) = rest[: 3 * groups], rest[3 * groups : 3 * groups + 3], rest[-4:]
    long, mid = lengths
    n = slice(0, long + mid)
    total = dr1[...]
    for a, w in enumerate((wq, wk, wv)):
        for g, (low, high) in enumerate(lanes):
            total = total + dot_nt(blocks[3 * g + a][n, :], w[:, low:high])
    total = total.astype(bf16)
    own[0] = total[0 : long // 2]
    other[0 : long // 2, :] = total[long // 2 : long]
    own_mid[...] = total[long : long + mid // 2]
    other[long // 2 :, :] = total[long + mid // 2 :]


def input_grad(seq, dr1, groups, lanes, weights, lengths, before):
    long, mid = lengths
    flat = [a for g in groups for a in g]
    mine = before.shape[0] // 2
    whole = lambda a: pl.BlockSpec(a.shape, lambda i, s: (0, 0))
    ins = flat + list(weights)
    return pl.pallas_call(
        functools.partial(input_grad_kernel, lengths=lengths, lanes=lanes),
        grid_spec=pltpu.PrefetchScalarGridSpec(
            num_scalar_prefetch=1,
            grid=(1,),
            in_specs=[pl.BlockSpec((pl.Element(long + mid), pl.Element(D)), lambda i, s: (long, 0))]
            + [whole(a) for a in ins]
            + [ANY],
            out_specs=[
                pl.BlockSpec((1, long // 2, D), lambda i, s: (mine * s[0] + 1, 0, 0)),
                pl.BlockSpec((mid // 2, D), lambda i, s: (0, 0)),
                pl.BlockSpec(((long + mid) // 2, D), lambda i, s: (0, 0)),
            ],
        ),
        out_shape=[SDS(before.shape, bf16), SDS((mid // 2, D), bf16), SDS(((long + mid) // 2, D), bf16)],
        input_output_aliases={2 + len(ins): 0},
        compiler_params=pltpu.CompilerParams(vmem_limit_bytes=24 * 2**20),
        cost_estimate=LONG,
        name="input_grad",
    )(seq, dr1, *ins, before)


def swap_seq(v):
    return lax.ppermute(v, "seq", [(0, 1), (1, 0)])


def later(value, *others):
    return lax.optimization_barrier((value, *others))[0]


AXES = {"w": (0, 16), "z": (1, 8), "y": (2, 4), "x": (3, 1)}
CORE = 2


def swap(v, mask):
    return lax.ppermute(v, ("dp", "seq"), [(i, i ^ mask) for i in range(BLOCKS)])


class Payload:
    def __init__(self, groups, order, whole=False):
        self.groups = groups
        self.order = order
        self.whole = whole

    def specs(self, bits):
        todo = {AXES[a][0] for a in "".join(self.order)}
        found = []
        for width, arrays in self.groups:
            for array, lane in arrays:
                shape = tuple(2 if d in todo and d not in bits else 1 for d in range(4))
                index = tuple(bits.get(d, 0) if array.shape[d] == 2 else 0 for d in range(4))
                found.append((array, pl.BlockSpec(shape + (16, width), functools.partial(fixed, index + (0, lane)))))
        return found

    def receive(self, after=None):
        for outgoing, mask in zip(self.outgoing, self.masks):
            received = swap(outgoing, mask)
            if after is not None:
                received = later(received, after)
            low = 0
            for width, arrays in self.groups:
                arrays.append((received, low // width))
                low += width
        return self


def fixed(index, *_):
    return index


def join(*sums):
    return Payload([g for h in sums for g in h.groups], sums[0].order)


def load_sum(refs):
    total = refs[0][...].astype(f32)
    for r in refs[1:]:
        total = total + r[...].astype(f32)
    return total


def add_kernel(*refs, plan):
    outs = refs[len(refs) - len(plan) :]
    at = 0
    for out, groups in zip(outs, plan):
        low = 0
        for count, width in groups:
            out[:, :, :, :, :, low : low + width] = load_sum(refs[at : at + count]).astype(bf16)
            at += count
            low += width


def send(*sums):
    arrays, specs, plan, shapes = [], [], [], []
    for h in sums:
        step, rest = h.order[0], h.order[1:]
        h.masks, h.count = [], 0
        left = {AXES[a][0] for a in "".join(rest)}
        shape = tuple(2 if d in left else 1 for d in range(4)) + (16, sum(g[0] for g in h.groups))
        for which in range(0 if h.whole else 1, 2 ** len(step)):
            bits = {AXES[a][0]: which >> i & 1 for i, a in enumerate(step)}
            h.masks.append(sum(AXES[a][1] for i, a in enumerate(step) if which >> i & 1))
            found = h.specs(bits)
            arrays += [f[0] for f in found]
            specs += [f[1] for f in found]
            plan.append([(len(g[1]), g[0]) for g in h.groups])
            shapes.append(shape)
            h.count += 1
        h.order = rest
    outs = pl.pallas_call(
        functools.partial(add_kernel, plan=plan),
        grid=(1,),
        in_specs=specs,
        out_specs=[pl.BlockSpec(n, functools.partial(fixed, (0,) * 6)) for n in shapes],
        out_shape=[SDS(n, bf16) for n in shapes],
        compiler_params=pltpu.CompilerParams(vmem_limit_bytes=SMALL_LIMIT),
        cost_estimate=LONG,
        name="add_parts",
    )(*arrays)
    at = 0
    for h in sums:
        h.outgoing = outs[at : at + h.count]
        at += h.count
        if h.whole:
            h.whole = False
            stays, h.outgoing, h.masks = h.outgoing[0], h.outgoing[1:], h.masks[1:]
            low = 0
            for n, (width, _) in enumerate(h.groups):
                h.groups[n] = (width, [(stays, low // width)])
                low += width


def across_cores(pair, after, ranges, order):
    leaving, keep = pair
    received = later(swap(leaving, CORE), after)
    both = [v.reshape(2, 2, 2, 2, 16, -1) for v in (keep, received)]
    return [
        Payload([(width, [(v, lane) for v in both]) for width, lane in groups], axes, len(axes[0]) == 1)
        for axes, groups in zip(order, ranges)
    ]


def store_24(block, out, column, lanes=D):
    for g in range(3):
        for t in range(2):
            piece = block[8 * t : 8 * t + 8, 384 * g : 384 * (g + 1)]
            out[8 * g : 8 * g + 8, column + lanes // 2 * t : column + lanes // 2 * t + 384] = piece


def last_dense_kernel(seq, *refs, plan):
    (*ins, w_up, w_down, w_out, small) = refs
    blocks = []
    at = 0
    for count in plan:
        blocks.append(load_sum(ins[at : at + count])[0, 0, 0, 0])
        at += count
    up = jnp.concatenate(blocks[:2], axis=1)
    down = jnp.concatenate(blocks[2:], axis=1)
    for j in range(4):
        store_24(up[:, 1152 * j : 1152 * (j + 1)], w_up, 384 * j, FF)
    for g in range(6):
        w_down[16 * g : 16 * (g + 1), :] = down[:, D * g : D * (g + 1)]
    store_24(down[:, 4608:5760], w_out, 0)
    small[...] = down[:, 5760:5888]


def last_qkv_kernel(seq, *refs, plan):
    (*ins, w_query, w_key, w_value, small, scr) = refs
    blocks = []
    at = 0
    for count in plan:
        blocks.append(load_sum(ins[at : at + count])[0, 0, 0, 0])
        at += count
    left, right, tail = blocks
    for c in range(2):
        store_24(left[:, 1152 * c : 1152 * (c + 1)], scr, D * c)
    store_24(right, scr, 2 * D)
    for a, out in enumerate((w_query, w_key, w_value)):
        out[:, 0:512] = scr[:, 512 * a : 512 * (a + 1)]
        out[:, 512:768] = scr[:, 2 * D + 256 * a : 2 * D + 256 * (a + 1)]
    small[...] = tail


def last_sums(kernel, seq, sums, shapes, scratch):
    found = [f for h in sums for f in h.specs({})]
    plan = [len(g[1]) for h in sums for g in h.groups]
    return pl.pallas_call(
        functools.partial(kernel, plan=plan),
        grid=(1,),
        in_specs=[pl.BlockSpec(memory_space=pltpu.SMEM)] + [f[1] for f in found],
        out_specs=[pl.BlockSpec(n, functools.partial(fixed, (0, 0))) for n in shapes],
        out_shape=[SDS(n, f32) for n in shapes],
        scratch_shapes=[pltpu.VMEM(n, f32) for n in scratch],
        compiler_params=pltpu.CompilerParams(vmem_limit_bytes=SMALL_LIMIT),
        cost_estimate=LONG,
        name="last_sums",
    )(seq, *[f[0] for f in found])


def rows_24(block):
    return block.reshape(2, 8, 3, 384).transpose(2, 1, 0, 3).reshape(24, D)


def unpack_up(block):
    return block.reshape(2, 8, 4, 3, 384).transpose(3, 1, 0, 2, 4).reshape(24, FF)


def unpack_down(block):
    return block[:, :4608].reshape(16, 6, D).transpose(1, 0, 2).reshape(96, D), rows_24(block[:, 4608:5760])


def unpack_qkv(blocks):
    wide, narrow = blocks
    left = jnp.concatenate([rows_24(wide[:, :1152]), rows_24(wide[:, 1152:])], axis=1)
    right = rows_24(narrow[:, :1152])
    return [
        jnp.concatenate([left[:, 512 * a : 512 * (a + 1)], right[:, 256 * a : 256 * (a + 1)]], axis=1) for a in range(3)
    ]


def reduce_plain(up_pair, down_pair, qkv_pairs, vec, bg):
    def ordered(pair):
        send, keep = pair
        both = jnp.stack([keep.reshape(8, 2, 16, -1), send.reshape(8, 2, 16, -1)], axis=1)
        return both.reshape(BLOCKS, 16, -1).astype(f32)

    scatter = lambda v: lax.psum_scatter(v, ("dp", "seq"), scatter_dimension=0, tiled=True)
    w_up = jax.vmap(unpack_up)(ordered(up_pair)).reshape(D, FF)
    w_down, w_out = (a.reshape(-1, D) for a in jax.vmap(unpack_down)(ordered(down_pair)))
    qkv = [a.reshape(D, D) for a in jax.vmap(unpack_qkv)([ordered(p) for p in qkv_pairs])]
    small = [scatter(vec[i]) for i in range(6)]
    return (
        scatter(qkv[0]), scatter(bg[0]), scatter(qkv[1]), scatter(qkv[2]), scatter(bg[1]), scatter(w_out),
        small, scatter(w_up), scatter(vec[8:12].reshape(FF)), scatter(w_down),
    )


def give_back_kernel(seq, here, got_first, got, got_end, long_in, long, middle, short):
    long[0] = jnp.where(pl.program_id(0) == 0, got_first[...], got[...])

    @pl.when(seq[0] == 0)
    def _():
        middle[0] = here[...]
        short[0] = got_end[: short.shape[1], :]

    @pl.when(seq[0] != 0)
    def _():
        middle[0] = got_end[...]
        short[0] = here[: short.shape[1], :]


def give_back(seq, long, here, got, short):
    count, half, _ = long.shape
    mid = here.shape[0]
    mine = count // 2
    return pl.pallas_call(
        give_back_kernel,
        grid_spec=pltpu.PrefetchScalarGridSpec(
            num_scalar_prefetch=1,
            grid=(mine,),
            in_specs=[
                pl.BlockSpec((mid, D), lambda i, s: (0, 0)),
                pl.BlockSpec((half, D), lambda i, s: (0, 0)),
                pl.BlockSpec((half, D), lambda i, s: (jnp.maximum(i - 1, 0), 0)),
                pl.BlockSpec((mid, D), lambda i, s: ((mine - 1) * half // mid, 0)),
                ANY,
            ],
            out_specs=[
                pl.BlockSpec((1, half, D), lambda i, s: (mine * (1 - s[0]) + i, 0, 0)),
                pl.BlockSpec((1, mid, D), lambda i, s: (0, 0, 0)),
                pl.BlockSpec((1, short, D), lambda i, s: (0, 0, 0)),
            ],
        ),
        out_shape=[SDS(long.shape, bf16), SDS((1, mid, D), bf16), SDS((1, short, D), bf16)],
        input_output_aliases={5: 0},
        compiler_params=pltpu.CompilerParams(vmem_limit_bytes=SMALL_LIMIT),
        cost_estimate=LONG,
        name="add_halves",
    )(seq, here, got[0], got[1], got[1], long)


def per_device(
    tokens_short, tokens_middle, tokens_long, length_short, length_middle, length_long,
    query_weight, query_bias, key_weight, value_weight, value_bias, output_weight, output_bias,
    attention_gain, attention_shift, up_weight, up_bias, down_weight, down_bias, output_gain, output_shift,
    upstream_short, upstream_middle, upstream_long,
):
    seq = lax.axis_index("seq")
    first = seq == 0
    device = (lax.axis_index("dp") * 2 + seq).astype(jnp.int32)
    fast = lax.axis_size("dp") * lax.axis_size("seq") == BLOCKS
    me = device if fast else jnp.int32(0)
    me_ref = me.reshape(1)
    count, half, _ = tokens_long.shape
    mine = count // 2
    mid = tokens_middle.shape[1]
    short = tokens_short.shape[1]
    lengths = (2 * half,) * mine + (2 * mid,)
    tokens = sum(lengths)
    rows = 2 * half * (mine + 1)

    def own_rows(v):
        return lax.dynamic_slice_in_dim(v, mine * seq, mine, 0)

    def other_rows(v):
        return lax.dynamic_slice_in_dim(v, mine * (1 - seq), mine, 0)

    def middle_rows(middle, low):
        low = jnp.pad(low[0], ((0, mid - short), (0, 0)))
        return jnp.where(first, middle[0], low), jnp.where(first, low, middle[0])

    x_mid, x_mid_out = middle_rows(tokens_middle, tokens_short)
    x_mid_in = swap_seq(x_mid_out)
    x_own, x_out = own_rows(tokens_long), other_rows(tokens_long)
    x_in = [swap_seq(x_out[0])]
    u_mid, u_mid_out = middle_rows(upstream_middle, upstream_short)
    u_out = jnp.concatenate([other_rows(upstream_long).reshape(mine * half, D), u_mid_out], axis=0)

    place = (seq.astype(jnp.int32).reshape(1), length_short, length_middle, length_long)
    qkv = [query_weight, key_weight, value_weight]
    projections = qkv + [query_bias, value_bias]
    chain = attention_forward(place, x_mid, x_mid_in, projections, mine, 2 * mid, mine * half // mid, None, rows)
    x_in += [swap_seq(later(x_out[i], chain[5])) for i in range(1, mine)]
    for i in range(mine):
        chain = attention_forward(place, x_own[i], x_in[i], projections, i, 2 * half, i, chain, rows)
    x, q, k, v, ctx, lse, xt = chain
    u_in = swap_seq(later(u_out, lse))

    mats = [output_weight, up_weight, down_weight]
    dense = functools.partial(
        dense_steps, place[0], ctx, x, tokens=tokens, rows=rows, mats=mats,
        vecs=[up_bias, output_bias, attention_gain, attention_shift, down_bias, output_gain, output_shift],
    )
    res_long, *before = dense(ups=[upstream_long], before=None)
    res_first, res_rest, res_mid, act, dinn, nlow, dbr, datt, dr1, dctx, vec = dense(ups=[u_in, u_in, u_mid], before=before)

    up_pair = up_grad(me_ref, nlow, dinn, tokens)
    res_got = [swap_seq(later(res_first, up_pair[0]))]
    down_pair = down_grad(later(me_ref, up_pair[0]), act, dbr, ctx, datt, vec, tokens)
    res_got[0] = later(res_got[0], down_pair[0])
    res_got.append(swap_seq(later(res_rest, res_got[0])))

    def at(before, *sums, done=()):
        going = [v for h in sums for v in h.outgoing] if fast else []
        return (later(place[0], before, *going, *done), *place[1:])

    up = down = all_sum = ()
    if fast:
        up = across_cores(
            up_pair, down_pair[0], [[(2304, 0)], [(2304, 1)]], [["z", "x", "y", "w"], ["y", "x", "z", "w"]]
        )
        send(*up)
    *before, ig_long, ig_other = first_row_backward(
        at(down_pair[0], *up), q, k, v, dctx, lse, dr1, qkv, 2 * half
    )
    if fast:
        for h in up:
            h.receive(ig_other)
        down = across_cores(
            down_pair, ig_other, [[(2944, 0)], [(2944, 1)]], [["z", "y", "x", "w"], ["y", "z", "x", "w"]]
        )
        send(*up, *down)
    res_got[1] = later(res_got[1], ig_other)
    later_rows = (2 * half, 2 * mid)
    *wide, leaving, keep, bg = group_backward(
        me_ref, at(ig_other, *up, *down, done=res_got), q, k, v, dctx, lse, before, xt, later_rows, 4, 0, None
    )
    wide_pair = (leaving, keep)
    if fast:
        for h in (*up, *down):
            h.receive(bg)
        send(*up, *down)
    ig_got = [swap_seq(later(ig_other, bg))]
    *narrow, leaving, keep, bg_last = group_backward(
        me_ref, at(bg, *up, *down), q, k, v, dctx, lse, before, xt, later_rows, 2, 4, bg
    )
    narrow_pair = (leaving, keep)
    ig_got[0] = later(ig_got[0], bg_last)
    if fast:
        for h in (*up, *down):
            h.receive(bg_last)
        up = (join(*up),)
        down = (join(*down),)
        send(*up, *down)
        wide_sum = across_cores(wide_pair, bg_last, [[(2304, 0)]], [["yz", "xw"]])
        narrow_sum = across_cores(narrow_pair, up[0].outgoing[0], [[(1152, 0), (128, 9)]], [["yz", "xw"]])
        all_sum = (join(*wide_sum, *narrow_sum),)
        send(*all_sum)
    ig_long, ig_mid, ig_rest = input_grad(
        at(bg_last, *up, *down, *all_sum)[0], later(dr1, ig_got[0]), [wide, narrow], [(0, 512), (512, 768)], qkv, later_rows, ig_long
    )
    ig_got.append(swap_seq(ig_rest))
    if fast:
        up[0].outgoing = [later(up[0].outgoing[0], ig_rest)]
    if fast:
        down[0].receive(ig_rest)
        send(*down)
        all_sum[0].receive(down[0].outgoing[0])
        send(*all_sum)
        spare = all_sum[0].outgoing[0]
        up[0].receive(spare)
    else:
        spare = ig_rest
    res_long, res_middle, res_short = give_back(
        later(place[0], spare), res_long, res_mid, res_got, short
    )
    ig_long, ig_middle, ig_short = give_back(place[0], ig_long, ig_mid, ig_got, short)
    if fast:
        down[0].receive()
        w_up, w_down, w_out, small = last_sums(
            last_dense_kernel, later(place[0], spare), [*up, *down], [(24, FF), (96, D), (24, D), (16, 128)], []
        )
        all_sum[0].receive(ig_middle)
        w_query, w_key, w_value, ends = last_sums(
            last_qkv_kernel, place[0], all_sum, [(24, D)] * 3 + [(16, 128)], [(24, 3 * D)]
        )
        b_up = lax.dynamic_slice(small, (8 + (me >> 3), 0), (1, 96))[0]
        done = w_query, ends[0, :24], w_key, w_value, ends[1, :24], w_out, small[:8, :24], w_up, b_up, w_down
    else:
        done = reduce_plain(up_pair, down_pair, [wide_pair, narrow_pair], vec, jnp.concatenate([bg, bg_last], axis=1))
    results = (res_short, res_middle, res_long)
    input_grads = (ig_short, ig_middle, ig_long)
    w_query, bq, w_key, w_value, bv, w_out, small, w_up, b_up, w_down = done
    return (
        *results, *input_grads,
        w_query, bq, w_key, w_value, bv, w_out, small[5], small[3], small[4],
        w_up, b_up, w_down, small[2], small[0], small[1],
    )


def solution(mesh):
    tokens = P("dp", "seq", None)
    wide = P(("dp", "seq"), None)
    flat = P(("dp", "seq"))
    in_specs = (tokens,) * 3 + (P("dp"),) * 3 + (P(),) * 15 + (tokens,) * 3
    out_specs = (tokens,) * 6 + (
        wide, flat, wide, wide, flat, wide, flat, flat, flat, wide, flat, wide, flat, flat, flat,
    )
    return jax.shard_map(per_device, mesh=mesh, in_specs=in_specs, out_specs=out_specs, check_vma=False)
```
